32 devices in a mesh: groups: 2 (over x), frame: 16 (over z, y, core).
Axes of the slice: x: 2, y: 2, z: 4, core: 2. Of those that a mesh axis runs over, the one named last changes fastest.
Arguments:
- latent: bfloat16 [128, 32, 1152], P(('groups', 'frame')), parts along dimension 0, may hold values from -6 to 6
- ln_gain: float32 [1152], replicated, may hold values from 0.1 to 1.9
- q_gain: float32 [72], replicated, may hold values from 0.1 to 1.9
- k_gain: float32 [72], replicated, may hold values from 0.1 to 1.9
- w_qkv: bfloat16 [1152, 3456], replicated, may hold values from -0.1875 to 0.1875
- w_out: bfloat16 [1152, 1152], replicated, may hold values from -0.5 to 0.5
Outputs:
- result: bfloat16 [128, 32, 1152], P(('groups', 'frame')), parts along dimension 0
The draws below stay inside these ranges and needn't reach their ends.
There are 2 independent parts, one for each index of `groups`. The reference program is written for one: setup_inputs(seed, part) draws one part's arguments, and reference() takes and returns one part's arrays. A program takes and returns all parts, laid end to end along the dimension named above; an argument that names none is the same for every part. Nothing has to cross between parts.
All inputs are finite; a program needn't handle non-finite values.
Results may differ from the reference program's by a relative error of at most 0.006.
Values may be sent and summed in bfloat16 or wider, within the bound.
No kernel may reach another device: no remote copies, remote signals or barrier semaphores. Data moves between devices by JAX's collectives and lax.ppermute only.
A program may use at most 64 MiB of HBM per device.

```python
import jax
import jax.numpy as jnp
from jax import lax

D = 1152
HEADS = 16
HEAD_DIM = 72
LAT_W = 32
WIN_ROWS = 4
FRAMES = 16


def block_levels(own_key, extent, shards, smallest, top_value):
    def one(axis_at, parts):
        steps = jax.random.uniform(jax.random.fold_in(jax.random.fold_in(own_key, 6), axis_at), (parts,), jnp.float32, smallest / len(shards), top_value / len(shards))
        return jnp.repeat(jnp.exp(steps), extent[axis_at] // parts).reshape((-1,) + (1,) * (len(extent) - axis_at - 1))

    level = one(*shards[0])
    for cut in shards[1:]:
        level = level * one(*cut)
    return level


def gaussian(own_key, shape, scale, limit, split=(), held_as=jnp.bfloat16):
    values = scale * jax.random.normal(own_key, shape, jnp.float32)
    if split:
        values = values * block_levels(own_key, shape, split, -0.22, 0.18)
    return jnp.clip(values, -limit, limit).astype(held_as)


def setup_inputs(seed: int = 0, part: int = 0) -> dict:
    arg_keys = jax.random.split(jax.random.key(seed), 7)
    part_splits = jax.random.split(jax.random.fold_in(arg_keys[6], part), 7)
    return {
        "latent": gaussian(part_splits[0], (FRAMES * WIN_ROWS, LAT_W, D), 1.0, 6.0, ((0, 16),)),
        "ln_gain": jnp.clip(1.0 + 0.18 * jax.random.normal(arg_keys[1], (D,), jnp.float32), 0.1, 1.9),
        "q_gain": jnp.clip(1.0 + 0.18 * jax.random.normal(arg_keys[2], (HEAD_DIM,), jnp.float32), 0.1, 1.9),
        "k_gain": jnp.clip(1.0 + 0.18 * jax.random.normal(arg_keys[3], (HEAD_DIM,), jnp.float32), 0.1, 1.9),
        "w_qkv": gaussian(arg_keys[4], (D, 3 * D), D ** -0.5, 0.1875),
        "w_out": gaussian(arg_keys[5], (D, D), (D // 8) ** -0.5, 0.5),
    }


def layer_norm(rows, ln_gain):
    values = rows.astype(jnp.float32)
    center = values - lax.optimization_barrier(jnp.mean(values, axis=-1, keepdims=True))
    spread = lax.optimization_barrier(jnp.mean(center * center, axis=-1, keepdims=True))
    return (center * lax.rsqrt(spread + 1e-06) * ln_gain).astype(jnp.bfloat16)

def head_norm(values, gain):
    shaped = values.reshape(values.shape[:-1] + (HEADS, HEAD_DIM))
    mean_sq = lax.optimization_barrier(jnp.mean(shaped * shaped, axis=-1, keepdims=True))
    return (shaped * lax.rsqrt(mean_sq + 1e-06) * gain).astype(jnp.bfloat16).reshape(values.shape)

def project(normed, w_qkv, q_gain, k_gain):
    width = normed.shape[-1]
    mixed = jnp.dot(normed.reshape(-1, width), w_qkv, preferred_element_type=jnp.float32)
    mixed = mixed.reshape(normed.shape[:-1] + (3 * width,))
    query = head_norm(mixed[..., :width], q_gain)
    keys = head_norm(mixed[..., width:2 * width], k_gain)
    values = mixed[..., 2 * width:].astype(jnp.bfloat16)
    return (query, keys, values)

def attend(query, keys, values):
    lead = query.shape[0]
    others = query.shape[1]
    q_four = query.reshape(lead, others, HEADS, HEAD_DIM).astype(jnp.float32)
    k_four = keys.reshape(lead, others, HEADS, HEAD_DIM).astype(jnp.float32)
    v_four = values.reshape(lead, others, HEADS, HEAD_DIM).astype(jnp.float32)
    scores = jnp.einsum('tshe,ushe->shtu', q_four, k_four) * HEAD_DIM ** (-0.5)
    weights = jnp.exp(scores)
    weights = (weights / lax.optimization_barrier(jnp.sum(weights, axis=-1, keepdims=True))).astype(jnp.bfloat16)
    mixed = jnp.einsum('shtu,ushe->tshe', weights.astype(jnp.float32), v_four)
    return mixed.astype(jnp.bfloat16).reshape(query.shape)

def reference(latent, ln_gain, q_gain, k_gain, w_qkv, w_out):
    frame_count = latent.shape[0] // WIN_ROWS
    grid = latent.reshape(frame_count, WIN_ROWS, LAT_W, D)

    def one_row(slab):
        normed = layer_norm(slab, ln_gain)
        query, keys, values = project(normed, w_qkv, q_gain, k_gain)
        mixed = attend(query, keys, values)
        branch = jnp.dot(mixed.reshape(-1, D), w_out, preferred_element_type=jnp.float32)
        return (slab.astype(jnp.float32) + branch.reshape(slab.shape)).astype(jnp.bfloat16)
    result = lax.map(one_row, jnp.swapaxes(grid, 0, 1))
    return jnp.swapaxes(result, 0, 1).reshape(latent.shape)
```

```python
import functools

import jax
import jax.numpy as jnp
from jax import lax
from jax.experimental import pallas as pl
from jax.experimental.pallas import tpu as pltpu
from jax.sharding import PartitionSpec as P

HEADS = 16
HEAD_DIM = 72
LANES = 128
EPS = 1e-06


def tokens_kernel(
    positions, x_ref, ln_ref, qg_ref, kg_ref, wqkv_ref, wout_ref, o_ref, normed, queries, keys, values, attended
):
    tokens, width = x_ref.shape
    bf16 = jnp.bfloat16

    gain = ln_ref[...]
    for row in range(0, tokens, 16):
        rows = pl.ds(row, 16)
        x = x_ref[rows, :].astype(jnp.float32)
        center = x - jnp.mean(x, axis=-1, keepdims=True)
        spread = jnp.mean(center * center, axis=-1, keepdims=True)
        normed[rows, :] = (center * lax.rsqrt(spread + EPS) * gain).astype(bf16)

    feature = lax.broadcasted_iota(jnp.int32, (width, LANES), 0)
    first = lax.broadcasted_iota(jnp.int32, (width, LANES), 1) * HEAD_DIM
    member = ((feature >= first) & (feature < first + HEAD_DIM)).astype(bf16)
    feature = lax.broadcasted_iota(jnp.int32, (LANES, width), 1)
    first = lax.broadcasted_iota(jnp.int32, (LANES, width), 0) * HEAD_DIM
    spread_out = ((feature >= first) & (feature < first + HEAD_DIM)).astype(bf16)

    def dot(a, b):
        return jnp.dot(a, b, preferred_element_type=jnp.float32)

    def head_norm(part, head_gain, out):
        mixed = dot(normed[...], wqkv_ref[:, part * width : (part + 1) * width])
        squares = mixed * mixed
        high = squares.astype(bf16)
        low = (squares - high.astype(jnp.float32)).astype(bf16)
        total = dot(high, member) + dot(low, member)
        inverse = lax.rsqrt(total * (1.0 / HEAD_DIM) + EPS)
        high = inverse.astype(bf16)
        low = (inverse - high.astype(jnp.float32)).astype(bf16)
        scale = dot(high, spread_out) + dot(low, spread_out)
        full_gain = jnp.concatenate([head_gain] * HEADS, axis=1)
        out[...] = (mixed * scale * full_gain).astype(bf16)

    head_norm(0, qg_ref[...], queries)
    head_norm(1, kg_ref[...], keys)
    values[...] = dot(normed[...], wqkv_ref[:, 2 * width :]).astype(bf16)

    place = lax.broadcasted_iota(jnp.int32, (tokens, tokens), 0) % positions
    other = lax.broadcasted_iota(jnp.int32, (tokens, tokens), 1) % positions
    same = place == other
    held = {}
    for head in range(HEADS):
        begin, end = head * HEAD_DIM, (head + 1) * HEAD_DIM
        low, high = begin // LANES, -(-end // LANES)
        window = slice(low * LANES, high * LANES)
        lane = lax.broadcasted_iota(jnp.int32, (1, (high - low) * LANES), 1) + low * LANES
        mine = (lane >= begin) & (lane < end)
        query = jnp.where(mine, queries[:, window], jnp.zeros((), bf16))
        scores = lax.dot_general(
            query, keys[:, window], (((1,), (1,)), ((), ())), preferred_element_type=jnp.float32
        ) * HEAD_DIM ** (-0.5)
        weights = jnp.where(same, jnp.exp(scores), 0.0)
        weights = (weights / jnp.sum(weights, axis=-1, keepdims=True)).astype(bf16)
        value = jnp.where(mine, values[:, window], jnp.zeros((), bf16))
        mixed = dot(weights, value)
        for tile in range(low, high):
            piece = mixed[:, (tile - low) * LANES : (tile - low + 1) * LANES]
            held[tile] = held[tile] + piece if tile in held else piece
            if end >= (tile + 1) * LANES:
                attended[:, tile * LANES : (tile + 1) * LANES] = held.pop(tile).astype(bf16)

    branch = dot(attended[...], wout_ref[...])
    o_ref[...] = (x_ref[...].astype(jnp.float32) + branch).astype(bf16)


def body(latent, ln_gain, q_gain, k_gain, w_qkv, w_out):
    device_count = lax.axis_size("frame")
    rows, columns, model = latent.shape
    tokens = rows * columns
    per_peer = tokens // device_count
    exchange = functools.partial(
        lax.all_to_all, axis_name="frame", split_axis=0, concat_axis=0, tiled=True
    )
    gathered = exchange(latent.reshape(device_count, per_peer, model))
    block = functools.partial(pltpu.VMEM, dtype=jnp.bfloat16)
    result = pl.pallas_call(
        functools.partial(tokens_kernel, per_peer),
        out_shape=jax.ShapeDtypeStruct((tokens, model), jnp.bfloat16),
        in_specs=[pl.BlockSpec(memory_space=pltpu.VMEM)] * 6,
        out_specs=pl.BlockSpec(memory_space=pltpu.VMEM),
        scratch_shapes=[block((tokens, model)) for _ in range(5)],
        compiler_params=pltpu.CompilerParams(vmem_limit_bytes=32 * 1024 * 1024),
        name="tokens",
    )(
        gathered.reshape(tokens, model),
        ln_gain.reshape(1, model),
        q_gain.reshape(1, HEAD_DIM),
        k_gain.reshape(1, HEAD_DIM),
        w_qkv,
        w_out,
    )
    return exchange(result.reshape(device_count, per_peer, model)).reshape(latent.shape)


def solution(mesh):
    placed = (P(("groups", "frame"), None, None), P(), P(), P(), P(), P())
    return jax.shard_map(
        body,
        mesh=mesh,
        in_specs=placed,
        out_specs=P(("groups", "frame"), None, None),
        check_vma=False,
    )
```

```python
import functools

import jax
import jax.numpy as jnp
from jax import lax
from jax.experimental import pallas as pl
from jax.experimental.pallas import tpu as pltpu
from jax.sharding import PartitionSpec as P

HEADS = 16
HEAD_DIM = 72
LANES = 128
EPS = 1e-06


def weights_kernel(
    ln_ref, qg_ref, kg_ref, wqkv_ref, wout_ref, gains_out, wqkv_out, wout_out, ln_held, qg_held, kg_held, sems
):
    pairs = [
        (wqkv_ref, wqkv_out),
        (wout_ref, wout_out),
        (ln_ref, ln_held),
        (qg_ref, qg_held),
        (kg_ref, kg_held),
    ]
    copies = [pltpu.make_async_copy(src, dst, sems.at[i]) for i, (src, dst) in enumerate(pairs)]
    for copy in copies:
        copy.start()
    for copy in copies[2:]:
        copy.wait()
    gains_out[0:1, :] = ln_held[...].reshape(1, -1)
    gains_out[1:2, :] = jnp.concatenate([qg_held[...].reshape(1, -1)] * HEADS, axis=1)
    gains_out[2:3, :] = jnp.concatenate([kg_held[...].reshape(1, -1)] * HEADS, axis=1)
    for copy in copies[:2]:
        copy.wait()


def tokens_kernel(
    positions, x_ref, gains_ref, wqkv_ref, wout_ref, o_ref, normed, queries, keys, values, attended
):
    tokens, width = x_ref.shape
    bf16 = jnp.bfloat16

    gain = gains_ref[0:1, :]
    for row in range(0, tokens, 16):
        rows = pl.ds(row, 16)
        x = x_ref[rows, :].astype(jnp.float32)
        center = x - jnp.mean(x, axis=-1, keepdims=True)
        spread = jnp.mean(center * center, axis=-1, keepdims=True)
        normed[rows, :] = (center * lax.rsqrt(spread + EPS) * gain).astype(bf16)

    feature = lax.broadcasted_iota(jnp.int32, (width, LANES), 0)
    first = lax.broadcasted_iota(jnp.int32, (width, LANES), 1) * HEAD_DIM
    member = ((feature >= first) & (feature < first + HEAD_DIM)).astype(bf16)
    feature = lax.broadcasted_iota(jnp.int32, (LANES, width), 1)
    first = lax.broadcasted_iota(jnp.int32, (LANES, width), 0) * HEAD_DIM
    spread_out = ((feature >= first) & (feature < first + HEAD_DIM)).astype(bf16)

    def dot(a, b):
        return jnp.dot(a, b, preferred_element_type=jnp.float32)

    def head_norm(part, out):
        mixed = dot(normed[...], wqkv_ref[:, part * width : (part + 1) * width])
        squares = mixed * mixed
        high = squares.astype(bf16)
        low = (squares - high.astype(jnp.float32)).astype(bf16)
        total = dot(high, member) + dot(low, member)
        inverse = lax.rsqrt(total * (1.0 / HEAD_DIM) + EPS)
        high = inverse.astype(bf16)
        low = (inverse - high.astype(jnp.float32)).astype(bf16)
        scale = dot(high, spread_out) + dot(low, spread_out)
        out[...] = (mixed * scale * gains_ref[part + 1 : part + 2, :]).astype(bf16)

    head_norm(0, queries)
    head_norm(1, keys)
    values[...] = dot(normed[...], wqkv_ref[:, 2 * width :]).astype(bf16)

    place = lax.broadcasted_iota(jnp.int32, (tokens, tokens), 0) % positions
    other = lax.broadcasted_iota(jnp.int32, (tokens, tokens), 1) % positions
    same = place == other
    held = {}
    for head in range(HEADS):
        begin, end = head * HEAD_DIM, (head + 1) * HEAD_DIM
        low, high = begin // LANES, -(-end // LANES)
        window = slice(low * LANES, high * LANES)
        lane = lax.broadcasted_iota(jnp.int32, (1, (high - low) * LANES), 1) + low * LANES
        mine = (lane >= begin) & (lane < end)
        query = jnp.where(mine, queries[:, window], jnp.zeros((), bf16))
        scores = lax.dot_general(
            query, keys[:, window], (((1,), (1,)), ((), ())), preferred_element_type=jnp.float32
        ) * HEAD_DIM ** (-0.5)
        weights = jnp.where(same, jnp.exp(scores), 0.0)
        weights = (weights / jnp.sum(weights, axis=-1, keepdims=True)).astype(bf16)
        value = jnp.where(mine, values[:, window], jnp.zeros((), bf16))
        mixed = dot(weights, value)
        for tile in range(low, high):
            piece = mixed[:, (tile - low) * LANES : (tile - low + 1) * LANES]
            held[tile] = held[tile] + piece if tile in held else piece
            if end >= (tile + 1) * LANES:
                attended[:, tile * LANES : (tile + 1) * LANES] = held.pop(tile).astype(bf16)

    branch = dot(attended[...], wout_ref[...])
    o_ref[...] = (x_ref[...].astype(jnp.float32) + branch).astype(bf16)


def body(latent, ln_gain, q_gain, k_gain, w_qkv, w_out):
    device_count = lax.axis_size("frame")
    rows, columns, model = latent.shape
    tokens = rows * columns
    per_peer = tokens // device_count
    exchange = functools.partial(
        lax.all_to_all, axis_name="frame", split_axis=0, concat_axis=0, tiled=True
    )
    in_vmem = pl.BlockSpec(memory_space=pltpu.VMEM)
    in_hbm = pl.BlockSpec(memory_space=pltpu.HBM)
    gains, wqkv_held, wout_held = pl.pallas_call(
        weights_kernel,
        out_shape=(
            pltpu.VMEM((8, model), jnp.float32),
            pltpu.VMEM(w_qkv.shape, w_qkv.dtype),
            pltpu.VMEM(w_out.shape, w_out.dtype),
        ),
        in_specs=[in_hbm] * 5,
        out_specs=[in_vmem] * 3,
        scratch_shapes=[
            pltpu.VMEM((model,), jnp.float32),
            pltpu.VMEM((HEAD_DIM,), jnp.float32),
            pltpu.VMEM((HEAD_DIM,), jnp.float32),
            pltpu.SemaphoreType.DMA((5,)),
        ],
        compiler_params=pltpu.CompilerParams(vmem_limit_bytes=16 * 1024 * 1024),
        cost_estimate=pl.CostEstimate(
            flops=0, bytes_accessed=2 * (w_qkv.size + w_out.size) * 2, transcendentals=0
        ),
        name="weights",
    )(*(pltpu.with_memory_space_constraint(a, pltpu.HBM) for a in (ln_gain, q_gain, k_gain, w_qkv, w_out)))
    gathered = exchange(latent.reshape(device_count, per_peer, model))
    block = functools.partial(pltpu.VMEM, dtype=jnp.bfloat16)
    result = pl.pallas_call(
        functools.partial(tokens_kernel, per_peer),
        out_shape=jax.ShapeDtypeStruct((tokens, model), jnp.bfloat16),
        in_specs=[in_vmem] * 4,
        out_specs=in_vmem,
        scratch_shapes=[block((tokens, model)) for _ in range(5)],
        compiler_params=pltpu.CompilerParams(vmem_limit_bytes=32 * 1024 * 1024),
        name="tokens",
    )(gathered.reshape(tokens, model), gains, wqkv_held, wout_held)
    return exchange(result.reshape(device_count, per_peer, model)).reshape(latent.shape)


def solution(mesh):
    placed = (P(("groups", "frame"), None, None), P(), P(), P(), P(), P())
    return jax.shard_map(
        body,
        mesh=mesh,
        in_specs=placed,
        out_specs=P(("groups", "frame"), None, None),
        check_vma=False,
    )
```

```python
import functools

import jax
import jax.numpy as jnp
from jax import lax
from jax.experimental import pallas as pl
from jax.experimental.pallas import tpu as pltpu
from jax.sharding import PartitionSpec as P

HEADS = 16
HEAD_DIM = 72
LANES = 128
EPS = 1e-06


def dot(a, b):
    return jnp.dot(a, b, preferred_element_type=jnp.float32)


def tokens_kernel(
    x_ref,
    ln_hbm,
    qg_hbm,
    kg_hbm,
    wqkv_hbm,
    wout_hbm,
    o_ref,
    wqkv,
    wout,
    ln_ref,
    qg_ref,
    kg_ref,
    normed,
    mixed,
    queries,
    keys,
    values,
    attended,
    sems,
):
    frames, positions, width = x_ref.shape
    tokens = frames * positions
    bf16, f32 = jnp.bfloat16, jnp.float32

    cut = width // 2 // LANES * LANES
    bounds = [(0, cut), (cut, width), (width, 2 * width), (2 * width, 3 * width)]
    pairs = [(ln_hbm, ln_ref), (qg_hbm, qg_ref), (kg_hbm, kg_ref)]
    pairs += [(wqkv_hbm.at[:, pl.ds(a, b - a)], wqkv.at[:, pl.ds(a, b - a)]) for a, b in bounds]
    pairs += [(wout_hbm, wout)]
    copies = [pltpu.make_async_copy(src, dst, sems.at[i]) for i, (src, dst) in enumerate(pairs)]
    for copy in copies:
        copy.start()

    def member_of(feature, lane):
        head = jnp.where(lane >= HEADS, lane - HEADS, lane)
        first = head * HEAD_DIM
        held = (feature >= first) & (feature < first + HEAD_DIM) & (lane < 2 * HEADS)
        return held.astype(f32).astype(bf16)

    shape = (width, LANES)
    member = member_of(lax.broadcasted_iota(jnp.int32, shape, 0), lax.broadcasted_iota(jnp.int32, shape, 1))
    shape = (LANES, width)
    spread_out = member_of(lax.broadcasted_iota(jnp.int32, shape, 1), lax.broadcasted_iota(jnp.int32, shape, 0))

    for copy in copies[:3]:
        copy.wait()
    gain = ln_ref[...].reshape(1, width)
    step = max(1, 16 // positions)
    for frame in range(0, frames, step):
        x = x_ref[frame : frame + step].astype(f32).reshape(step * positions, width)
        center = x - jnp.mean(x, axis=-1, keepdims=True)
        spread = jnp.mean(center * center, axis=-1, keepdims=True)
        rows = slice(frame * positions, (frame + step) * positions)
        normed[rows, :] = (center * lax.rsqrt(spread + EPS) * gain).astype(bf16)

    for copy, (a, b) in zip(copies[3:6], bounds):
        copy.wait()
        part = a // width
        mixed[part * tokens : (part + 1) * tokens, a - part * width : b - part * width] = dot(
            normed[...], wqkv[:, a:b]
        )
    total = dot((mixed[...] * mixed[...]).astype(bf16), member)
    inverse = lax.rsqrt(total * (1.0 / HEAD_DIM) + EPS)
    high = inverse.astype(bf16)
    low = (inverse - high.astype(f32)).astype(bf16)
    lane = lax.broadcasted_iota(jnp.int32, inverse.shape, 1)
    scale = dot(jnp.where(lane < HEADS, high, low), spread_out)
    for part, (head_gain, out) in enumerate(((qg_ref, queries), (kg_ref, keys))):
        rows = slice(part * tokens, (part + 1) * tokens)
        full_gain = jnp.concatenate([head_gain[...].reshape(1, HEAD_DIM)] * HEADS, axis=1)
        out[...] = (mixed[rows, :] * scale[rows, :] * full_gain).astype(bf16)
    copies[6].wait()
    values[...] = dot(normed[...], wqkv[:, 2 * width :]).astype(bf16)

    place = lax.broadcasted_iota(jnp.int32, (tokens, tokens), 0) % positions
    other = lax.broadcasted_iota(jnp.int32, (tokens, tokens), 1) % positions
    same = place == other
    held = {}
    for head in range(HEADS):
        begin, end = head * HEAD_DIM, (head + 1) * HEAD_DIM
        low, high = begin // LANES, -(-end // LANES)
        window = slice(low * LANES, high * LANES)
        lane = lax.broadcasted_iota(jnp.int32, (1, (high - low) * LANES), 1) + low * LANES
        mine = (lane >= begin) & (lane < end)
        query = jnp.where(mine, queries[:, window], jnp.zeros((), bf16))
        scores = lax.dot_general(
            query, keys[:, window], (((1,), (1,)), ((), ())), preferred_element_type=f32
        ) * HEAD_DIM ** (-0.5)
        weights = jnp.where(same, jnp.exp(scores), 0.0)
        weights = (weights / jnp.sum(weights, axis=-1, keepdims=True)).astype(bf16)
        value = jnp.where(mine, values[:, window], jnp.zeros((), bf16))
        heads_out = dot(weights, value)
        for tile in range(low, high):
            piece = heads_out[:, (tile - low) * LANES : (tile - low + 1) * LANES]
            held[tile] = held[tile] + piece if tile in held else piece
            if end >= (tile + 1) * LANES:
                attended[:, tile * LANES : (tile + 1) * LANES] = held.pop(tile).astype(bf16)

    copies[7].wait()
    branch = dot(attended[...], wout[...])
    o_ref[...] = (x_ref[...].astype(f32) + branch.reshape(x_ref.shape)).astype(bf16)


def body(latent, ln_gain, q_gain, k_gain, w_qkv, w_out):
    device_count = lax.axis_size("frame")
    rows, columns, model = latent.shape
    tokens = rows * columns
    per_peer = tokens // device_count
    exchange = functools.partial(
        lax.all_to_all, axis_name="frame", split_axis=0, concat_axis=0, tiled=True
    )
    gathered = exchange(latent.reshape(device_count, per_peer, model))
    in_vmem = pl.BlockSpec(memory_space=pltpu.VMEM)
    in_hbm = pl.BlockSpec(memory_space=pltpu.HBM)
    bf16, f32 = jnp.bfloat16, jnp.float32
    result = pl.pallas_call(
        tokens_kernel,
        out_shape=jax.ShapeDtypeStruct(gathered.shape, bf16),
        in_specs=[in_vmem] + [in_hbm] * 5,
        out_specs=in_vmem,
        scratch_shapes=[
            pltpu.VMEM(w_qkv.shape, bf16),
            pltpu.VMEM(w_out.shape, bf16),
            pltpu.VMEM((model,), f32),
            pltpu.VMEM((HEAD_DIM,), f32),
            pltpu.VMEM((HEAD_DIM,), f32),
            pltpu.VMEM((tokens, model), bf16),
            pltpu.VMEM((2 * tokens, model), f32),
            pltpu.VMEM((tokens, model), bf16),
            pltpu.VMEM((tokens, model), bf16),
            pltpu.VMEM((tokens, model), bf16),
            pltpu.VMEM((tokens, model), bf16),
            pltpu.SemaphoreType.DMA((8,)),
        ],
        compiler_params=pltpu.CompilerParams(vmem_limit_bytes=40 * 1024 * 1024),
        name="tokens",
    )(gathered, *(pltpu.with_memory_space_constraint(a, pltpu.HBM) for a in (ln_gain, q_gain, k_gain, w_qkv, w_out)))
    return exchange(result).reshape(latent.shape)


def solution(mesh):
    placed = (P(("groups", "frame"), None, None), P(), P(), P(), P(), P())
    return jax.shard_map(
        body,
        mesh=mesh,
        in_specs=placed,
        out_specs=P(("groups", "frame"), None, None),
        check_vma=False,
    )
```

```python
import functools

import jax
import jax.numpy as jnp
from jax import lax
from jax.experimental import pallas as pl
from jax.experimental.pallas import tpu as pltpu
from jax.sharding import PartitionSpec as P

HEADS = 16
HEAD_DIM = 72
LANES = 128
EPS = 1e-06


def dot(a, b):
    return jnp.dot(a, b, preferred_element_type=jnp.float32)


def tokens_kernel(x_ref, ln_hbm, qg_hbm, kg_hbm, wqkv_hbm, wout_hbm, *refs):
    frames, positions, width = x_ref.shape
    tokens = frames * positions
    slabs = refs[:frames]
    wqkv, wout, ln_ref, qg_ref, kg_ref, normed, mixed, queries, keys, values, attended, result, sems = refs[frames:]
    bf16, f32 = jnp.bfloat16, jnp.float32

    cut = width // 2 // LANES * LANES
    bounds = [(0, cut), (cut, width), (width, 2 * width), (2 * width, 3 * width)]
    pairs = [(ln_hbm, ln_ref), (qg_hbm, qg_ref), (kg_hbm, kg_ref)]
    pairs += [(wqkv_hbm.at[:, pl.ds(a, b - a)], wqkv.at[:, pl.ds(a, b - a)]) for a, b in bounds]
    pairs += [(wout_hbm, wout)]
    copies = [pltpu.make_async_copy(src, dst, sems.at[i]) for i, (src, dst) in enumerate(pairs)]
    for copy in copies:
        copy.start()

    def member_of(feature, lane):
        head = jnp.where(lane >= HEADS, lane - HEADS, lane)
        first = head * HEAD_DIM
        held = (feature >= first) & (feature < first + HEAD_DIM) & (lane < 2 * HEADS)
        return held.astype(f32).astype(bf16)

    shape = (width, LANES)
    member = member_of(lax.broadcasted_iota(jnp.int32, shape, 0), lax.broadcasted_iota(jnp.int32, shape, 1))
    shape = (LANES, width)
    spread_out = member_of(lax.broadcasted_iota(jnp.int32, shape, 1), lax.broadcasted_iota(jnp.int32, shape, 0))

    for copy in copies[:3]:
        copy.wait()
    gain = ln_ref[...].reshape(1, width)
    step = max(1, 16 // positions)
    for frame in range(0, frames, step):
        x = x_ref[frame : frame + step].astype(f32).reshape(step * positions, width)
        center = x - jnp.mean(x, axis=-1, keepdims=True)
        spread = jnp.mean(center * center, axis=-1, keepdims=True)
        rows = slice(frame * positions, (frame + step) * positions)
        normed[rows, :] = (center * lax.rsqrt(spread + EPS) * gain).astype(bf16)

    for copy, (a, b) in zip(copies[3:6], bounds):
        copy.wait()
        part = a // width
        mixed[part * tokens : (part + 1) * tokens, a - part * width : b - part * width] = dot(
            normed[...], wqkv[:, a:b]
        )
    squares = mixed[...] * mixed[...]
    high = squares.astype(bf16)
    low = (squares - high.astype(f32)).astype(bf16)
    total = dot(high, member) + dot(low, member)
    inverse = lax.rsqrt(total * (1.0 / HEAD_DIM) + EPS)
    high = inverse.astype(bf16)
    low = (inverse - high.astype(f32)).astype(bf16)
    lane = lax.broadcasted_iota(jnp.int32, inverse.shape, 1)
    scale = dot(jnp.where(lane < HEADS, high, low), spread_out)
    for part, (head_gain, out) in enumerate(((qg_ref, queries), (kg_ref, keys))):
        rows = slice(part * tokens, (part + 1) * tokens)
        full_gain = jnp.concatenate([head_gain[...].reshape(1, HEAD_DIM)] * HEADS, axis=1)
        out[...] = (mixed[rows, :] * scale[rows, :] * full_gain).astype(bf16)
    copies[6].wait()
    values[...] = dot(normed[...], wqkv[:, 2 * width :]).astype(bf16)

    place = lax.broadcasted_iota(jnp.int32, (tokens, tokens), 0) % positions
    other = lax.broadcasted_iota(jnp.int32, (tokens, tokens), 1) % positions
    same = place == other
    held = {}
    for head in range(HEADS):
        begin, end = head * HEAD_DIM, (head + 1) * HEAD_DIM
        low, high = begin // LANES, -(-end // LANES)
        window = slice(low * LANES, high * LANES)
        lane = lax.broadcasted_iota(jnp.int32, (1, (high - low) * LANES), 1) + low * LANES
        mine = (lane >= begin) & (lane < end)
        query = jnp.where(mine, queries[:, window], jnp.zeros((), bf16))
        scores = lax.dot_general(
            query, keys[:, window], (((1,), (1,)), ((), ())), preferred_element_type=f32
        ) * HEAD_DIM ** (-0.5)
        weights = jnp.where(same, jnp.exp(scores), 0.0)
        weights = (weights / jnp.sum(weights, axis=-1, keepdims=True)).astype(bf16)
        value = jnp.where(mine, values[:, window], jnp.zeros((), bf16))
        heads_out = dot(weights, value)
        for tile in range(low, high):
            piece = heads_out[:, (tile - low) * LANES : (tile - low + 1) * LANES]
            held[tile] = held[tile] + piece if tile in held else piece
            if end >= (tile + 1) * LANES:
                attended[:, tile * LANES : (tile + 1) * LANES] = held.pop(tile).astype(bf16)

    copies[7].wait()
    branch = dot(attended[...], wout[...])
    result[...] = (x_ref[...].astype(f32) + branch.reshape(x_ref.shape)).astype(bf16)
    me = lax.axis_index("frame")
    for k, slab in enumerate(slabs):
        slab[...] = result[lax.rem(me + k, frames)]


def ordered_kernel(*refs):
    slabs, out, sems = refs[:-2], refs[-2], refs[-1]
    count = len(slabs)
    me = lax.axis_index("frame")
    copies = [
        pltpu.make_async_copy(slab, out.at[lax.rem(me + count - k, count)], sems.at[k])
        for k, slab in enumerate(slabs)
    ]
    for copy in copies:
        copy.start()
    for copy in copies:
        copy.wait()


def body(latent, ln_gain, q_gain, k_gain, w_qkv, w_out):
    device_count = lax.axis_size("frame")
    rows, columns, model = latent.shape
    tokens = rows * columns
    per_peer = tokens // device_count
    exchange = functools.partial(
        lax.all_to_all, axis_name="frame", split_axis=0, concat_axis=0, tiled=True
    )
    gathered = exchange(latent.reshape(device_count, per_peer, model))
    in_vmem = pl.BlockSpec(memory_space=pltpu.VMEM)
    in_hbm = pl.BlockSpec(memory_space=pltpu.HBM)
    bf16, f32 = jnp.bfloat16, jnp.float32
    slabs = pl.pallas_call(
        tokens_kernel,
        out_shape=[jax.ShapeDtypeStruct((per_peer, model), bf16)] * device_count,
        in_specs=[in_vmem] + [in_hbm] * 5,
        out_specs=[in_vmem] * device_count,
        scratch_shapes=[
            pltpu.VMEM(w_qkv.shape, bf16),
            pltpu.VMEM(w_out.shape, bf16),
            pltpu.VMEM((model,), f32),
            pltpu.VMEM((HEAD_DIM,), f32),
            pltpu.VMEM((HEAD_DIM,), f32),
            pltpu.VMEM((tokens, model), bf16),
            pltpu.VMEM((2 * tokens, model), f32),
            pltpu.VMEM((tokens, model), bf16),
            pltpu.VMEM((tokens, model), bf16),
            pltpu.VMEM((tokens, model), bf16),
            pltpu.VMEM((tokens, model), bf16),
            pltpu.VMEM(gathered.shape, bf16),
            pltpu.SemaphoreType.DMA((8,)),
        ],
        compiler_params=pltpu.CompilerParams(vmem_limit_bytes=40 * 1024 * 1024),
        name="tokens",
    )(gathered, *(pltpu.with_memory_space_constraint(a, pltpu.HBM) for a in (ln_gain, q_gain, k_gain, w_qkv, w_out)))
    arrived = [slabs[0]]
    for k in range(1, device_count):
        ahead = [(i, (i + k) % device_count) for i in range(device_count)]
        arrived.append(lax.ppermute(slabs[k], "frame", ahead))
    result = pl.pallas_call(
        ordered_kernel,
        out_shape=pltpu.HBM(gathered.shape, bf16),
        in_specs=[pl.BlockSpec(memory_space=pl.ANY)] * device_count,
        out_specs=in_hbm,
        scratch_shapes=[pltpu.SemaphoreType.DMA((device_count,))],
        name="ordered",
    )(*arrived)
    return result.reshape(latent.shape)


def solution(mesh):
    placed = (P(("groups", "frame"), None, None), P(), P(), P(), P(), P())
    return jax.shard_map(
        body,
        mesh=mesh,
        in_specs=placed,
        out_specs=P(("groups", "frame"), None, None),
        check_vma=False,
    )
```

```python
import jax
import jax.numpy as jnp
from jax import lax
from jax.experimental import pallas as pl
from jax.experimental.pallas import tpu as pltpu
from jax.sharding import PartitionSpec as P

HEADS = 16
HEAD_DIM = 72
LANES = 128
EPS = 1e-06


def dot(a, b):
    return jnp.dot(a, b, preferred_element_type=jnp.float32)


def tokens_kernel(
    x_ref,
    ln_hbm,
    qg_hbm,
    kg_hbm,
    wqkv_hbm,
    wout_hbm,
    o_ref,
    wqkv,
    wout,
    ln_ref,
    qg_ref,
    kg_ref,
    normed,
    mixed,
    queries,
    keys,
    values,
    attended,
    sems,
):
    frames, positions, width = x_ref.shape
    tokens = frames * positions
    bf16, f32 = jnp.bfloat16, jnp.float32

    cut = width // 2 // LANES * LANES
    bounds = [(0, cut), (cut, width), (width, 2 * width), (2 * width, 3 * width)]
    pairs = [(ln_hbm, ln_ref), (qg_hbm, qg_ref), (kg_hbm, kg_ref)]
    pairs += [(wqkv_hbm.at[:, pl.ds(a, b - a)], wqkv.at[:, pl.ds(a, b - a)]) for a, b in bounds]
    pairs += [(wout_hbm, wout)]
    copies = [pltpu.make_async_copy(src, dst, sems.at[i]) for i, (src, dst) in enumerate(pairs)]
    for copy in copies:
        copy.start()

    def member_of(feature, lane):
        head = jnp.where(lane >= HEADS, lane - HEADS, lane)
        first = head * HEAD_DIM
        held = (feature >= first) & (feature < first + HEAD_DIM) & (lane < 2 * HEADS)
        return held.astype(f32).astype(bf16)

    shape = (width, LANES)
    member = member_of(lax.broadcasted_iota(jnp.int32, shape, 0), lax.broadcasted_iota(jnp.int32, shape, 1))
    shape = (LANES, width)
    spread_out = member_of(lax.broadcasted_iota(jnp.int32, shape, 1), lax.broadcasted_iota(jnp.int32, shape, 0))

    for copy in copies[:3]:
        copy.wait()
    gain = ln_ref[...].reshape(1, width)
    step = max(1, 16 // positions)
    for frame in range(0, frames, step):
        x = x_ref[frame : frame + step].astype(f32).reshape(step * positions, width)
        center = x - jnp.mean(x, axis=-1, keepdims=True)
        spread = jnp.mean(center * center, axis=-1, keepdims=True)
        rows = slice(frame * positions, (frame + step) * positions)
        normed[rows, :] = (center * lax.rsqrt(spread + EPS) * gain).astype(bf16)

    for copy, (a, b) in zip(copies[3:6], bounds):
        copy.wait()
        part = a // width
        mixed[part * tokens : (part + 1) * tokens, a - part * width : b - part * width] = dot(
            normed[...], wqkv[:, a:b]
        )
    squares = mixed[...] * mixed[...]
    high = squares.astype(bf16)
    low = (squares - high.astype(f32)).astype(bf16)
    total = dot(high, member) + dot(low, member)
    inverse = lax.rsqrt(total * (1.0 / HEAD_DIM) + EPS)
    high = inverse.astype(bf16)
    low = (inverse - high.astype(f32)).astype(bf16)
    lane = lax.broadcasted_iota(jnp.int32, inverse.shape, 1)
    scale = dot(jnp.where(lane < HEADS, high, low), spread_out)
    for part, (head_gain, out) in enumerate(((qg_ref, queries), (kg_ref, keys))):
        rows = slice(part * tokens, (part + 1) * tokens)
        full_gain = jnp.concatenate([head_gain[...].reshape(1, HEAD_DIM)] * HEADS, axis=1)
        out[...] = (mixed[rows, :] * scale[rows, :] * full_gain).astype(bf16)
    copies[6].wait()
    values[...] = dot(normed[...], wqkv[:, 2 * width :]).astype(bf16)

    place = lax.broadcasted_iota(jnp.int32, (tokens, tokens), 0) % positions
    other = lax.broadcasted_iota(jnp.int32, (tokens, tokens), 1) % positions
    same = place == other
    held = {}
    for head in range(HEADS):
        begin, end = head * HEAD_DIM, (head + 1) * HEAD_DIM
        low, high = begin // LANES, -(-end // LANES)
        window = slice(low * LANES, high * LANES)
        lane = lax.broadcasted_iota(jnp.int32, (1, (high - low) * LANES), 1) + low * LANES
        mine = (lane >= begin) & (lane < end)
        query = jnp.where(mine, queries[:, window], jnp.zeros((), bf16))
        scores = lax.dot_general(
            query, keys[:, window], (((1,), (1,)), ((), ())), preferred_element_type=f32
        ) * HEAD_DIM ** (-0.5)
        weights = jnp.where(same, jnp.exp(scores), 0.0)
        weights = (weights / jnp.sum(weights, axis=-1, keepdims=True)).astype(bf16)
        value = jnp.where(mine, values[:, window], jnp.zeros((), bf16))
        heads_out = dot(weights, value)
        for tile in range(low, high):
            piece = heads_out[:, (tile - low) * LANES : (tile - low + 1) * LANES]
            held[tile] = held[tile] + piece if tile in held else piece
            if end >= (tile + 1) * LANES:
                attended[:, tile * LANES : (tile + 1) * LANES] = held.pop(tile).astype(bf16)

    copies[7].wait()
    branch = dot(attended[...], wout[...])
    o_ref[...] = (x_ref[...].astype(f32) + branch.reshape(x_ref.shape)).astype(bf16)


def body(latent, ln_gain, q_gain, k_gain, w_qkv, w_out):
    device_count = lax.axis_size("frame")
    rows, columns, model = latent.shape
    tokens = rows * columns
    per_peer = tokens // device_count
    chips = device_count // 2
    pairs = [[2 * c, 2 * c + 1] for c in range(chips)]
    alike = [[2 * c + core for c in range(chips)] for core in range(2)]

    def exchange(slabs):
        paired = slabs.reshape(chips, 2, per_peer, model)
        paired = lax.all_to_all(paired, "frame", 1, 1, axis_index_groups=pairs, tiled=True)
        paired = lax.all_to_all(paired, "frame", 0, 0, axis_index_groups=alike, tiled=True)
        return paired.reshape(slabs.shape)

    gathered = exchange(latent.reshape(device_count, per_peer, model))
    in_vmem = pl.BlockSpec(memory_space=pltpu.VMEM)
    in_hbm = pl.BlockSpec(memory_space=pltpu.HBM)
    bf16, f32 = jnp.bfloat16, jnp.float32
    result = pl.pallas_call(
        tokens_kernel,
        out_shape=jax.ShapeDtypeStruct(gathered.shape, bf16),
        in_specs=[in_vmem] + [in_hbm] * 5,
        out_specs=in_vmem,
        scratch_shapes=[
            pltpu.VMEM(w_qkv.shape, bf16),
            pltpu.VMEM(w_out.shape, bf16),
            pltpu.VMEM((model,), f32),
            pltpu.VMEM((HEAD_DIM,), f32),
            pltpu.VMEM((HEAD_DIM,), f32),
            pltpu.VMEM((tokens, model), bf16),
            pltpu.VMEM((2 * tokens, model), f32),
            pltpu.VMEM((tokens, model), bf16),
            pltpu.VMEM((tokens, model), bf16),
            pltpu.VMEM((tokens, model), bf16),
            pltpu.VMEM((tokens, model), bf16),
            pltpu.SemaphoreType.DMA((8,)),
        ],
        compiler_params=pltpu.CompilerParams(vmem_limit_bytes=40 * 1024 * 1024),
        name="tokens",
    )(gathered, *(pltpu.with_memory_space_constraint(a, pltpu.HBM) for a in (ln_gain, q_gain, k_gain, w_qkv, w_out)))
    return exchange(result).reshape(latent.shape)


def solution(mesh):
    placed = (P(("groups", "frame"), None, None), P(), P(), P(), P(), P())
    return jax.shard_map(
        body,
        mesh=mesh,
        in_specs=placed,
        out_specs=P(("groups", "frame"), None, None),
        check_vma=False,
    )
```

```python
import functools

import jax
import jax.numpy as jnp
from jax import lax
from jax.experimental import pallas as pl
from jax.experimental.pallas import tpu as pltpu
from jax.sharding import PartitionSpec as P

HEADS = 16
HEAD_DIM = 72
LANES = 128
EPS = 1e-06


def dot(a, b):
    return jnp.dot(a, b, preferred_element_type=jnp.float32)


def held_kernel(ln_ref, qg_ref, kg_ref, wqkv_ref, gains_out, wq_out, ln, qg, kg, sems):
    width = wq_out.shape[1]
    pairs = [(ln_ref, ln), (qg_ref, qg), (kg_ref, kg), (wqkv_ref.at[:, pl.ds(0, width)], wq_out)]
    copies = [pltpu.make_async_copy(src, dst, sems.at[i]) for i, (src, dst) in enumerate(pairs)]
    for copy in copies:
        copy.start()
    for copy in copies[:3]:
        copy.wait()
    gains_out[0:1, :] = ln[...].reshape(1, width)
    gains_out[1:2, :] = jnp.concatenate([qg[...].reshape(1, HEAD_DIM)] * HEADS, axis=1)
    gains_out[2:3, :] = jnp.concatenate([kg[...].reshape(1, HEAD_DIM)] * HEADS, axis=1)
    copies[3].wait()


def tokens_kernel(
    x_ref,
    gains_ref,
    wq,
    wqkv_hbm,
    wout_hbm,
    o_ref,
    wkv,
    wout,
    normed,
    mixed,
    queries,
    keys,
    values,
    attended,
    sems,
):
    frames, positions, width = x_ref.shape
    tokens = frames * positions
    bf16, f32 = jnp.bfloat16, jnp.float32

    pairs = [
        (wqkv_hbm.at[:, pl.ds(width, width)], wkv.at[:, pl.ds(0, width)]),
        (wqkv_hbm.at[:, pl.ds(2 * width, width)], wkv.at[:, pl.ds(width, width)]),
        (wout_hbm, wout),
    ]
    copies = [pltpu.make_async_copy(src, dst, sems.at[i]) for i, (src, dst) in enumerate(pairs)]
    for copy in copies:
        copy.start()

    def member_of(feature, lane):
        head = jnp.where(lane >= HEADS, lane - HEADS, lane)
        first = head * HEAD_DIM
        held = (feature >= first) & (feature < first + HEAD_DIM) & (lane < 2 * HEADS)
        return held.astype(f32).astype(bf16)

    shape = (width, LANES)
    member = member_of(lax.broadcasted_iota(jnp.int32, shape, 0), lax.broadcasted_iota(jnp.int32, shape, 1))
    shape = (LANES, width)
    spread_out = member_of(lax.broadcasted_iota(jnp.int32, shape, 1), lax.broadcasted_iota(jnp.int32, shape, 0))

    gain = gains_ref[0:1, :]
    step = max(1, 16 // positions)
    for frame in range(0, frames, step):
        x = x_ref[frame : frame + step].astype(f32).reshape(step * positions, width)
        center = x - jnp.mean(x, axis=-1, keepdims=True)
        spread = jnp.mean(center * center, axis=-1, keepdims=True)
        rows = slice(frame * positions, (frame + step) * positions)
        normed[rows, :] = (center * lax.rsqrt(spread + EPS) * gain).astype(bf16)

    mixed[:tokens, :] = dot(normed[...], wq[...])
    copies[0].wait()
    mixed[tokens:, :] = dot(normed[...], wkv[:, :width])
    squares = mixed[...] * mixed[...]
    high = squares.astype(bf16)
    low = (squares - high.astype(f32)).astype(bf16)
    total = dot(high, member) + dot(low, member)
    inverse = lax.rsqrt(total * (1.0 / HEAD_DIM) + EPS)
    high = inverse.astype(bf16)
    low = (inverse - high.astype(f32)).astype(bf16)
    lane = lax.broadcasted_iota(jnp.int32, inverse.shape, 1)
    scale = dot(jnp.where(lane < HEADS, high, low), spread_out)
    for part, out in enumerate((queries, keys)):
        rows = slice(part * tokens, (part + 1) * tokens)
        out[...] = (mixed[rows, :] * scale[rows, :] * gains_ref[part + 1 : part + 2, :]).astype(bf16)
    copies[1].wait()
    values[...] = dot(normed[...], wkv[:, width:]).astype(bf16)

    place = lax.broadcasted_iota(jnp.int32, (tokens, tokens), 0) % positions
    other = lax.broadcasted_iota(jnp.int32, (tokens, tokens), 1) % positions
    same = place == other
    held = {}
    for head in range(HEADS):
        begin, end = head * HEAD_DIM, (head + 1) * HEAD_DIM
        low, high = begin // LANES, -(-end // LANES)
        window = slice(low * LANES, high * LANES)
        lane = lax.broadcasted_iota(jnp.int32, (1, (high - low) * LANES), 1) + low * LANES
        mine = (lane >= begin) & (lane < end)
        query = jnp.where(mine, queries[:, window], jnp.zeros((), bf16))
        scores = lax.dot_general(
            query, keys[:, window], (((1,), (1,)), ((), ())), preferred_element_type=f32
        ) * HEAD_DIM ** (-0.5)
        weights = jnp.where(same, jnp.exp(scores), 0.0)
        weights = (weights / jnp.sum(weights, axis=-1, keepdims=True)).astype(bf16)
        value = jnp.where(mine, values[:, window], jnp.zeros((), bf16))
        heads_out = dot(weights, value)
        for tile in range(low, high):
            piece = heads_out[:, (tile - low) * LANES : (tile - low + 1) * LANES]
            held[tile] = held[tile] + piece if tile in held else piece
            if end >= (tile + 1) * LANES:
                attended[:, tile * LANES : (tile + 1) * LANES] = held.pop(tile).astype(bf16)

    copies[2].wait()
    branch = dot(attended[...], wout[...])
    o_ref[...] = (x_ref[...].astype(f32) + branch.reshape(x_ref.shape)).astype(bf16)


def body(latent, ln_gain, q_gain, k_gain, w_qkv, w_out):
    device_count = lax.axis_size("frame")
    rows, columns, model = latent.shape
    tokens = rows * columns
    per_peer = tokens // device_count
    exchange = functools.partial(
        lax.all_to_all, axis_name="frame", split_axis=0, concat_axis=0, tiled=True
    )
    gathered = exchange(latent.reshape(device_count, per_peer, model))
    in_vmem = pl.BlockSpec(memory_space=pltpu.VMEM)
    in_hbm = pl.BlockSpec(memory_space=pltpu.HBM)
    bf16, f32 = jnp.bfloat16, jnp.float32
    held = [pltpu.with_memory_space_constraint(a, pltpu.HBM) for a in (ln_gain, q_gain, k_gain, w_qkv, w_out)]
    gains, wq = pl.pallas_call(
        held_kernel,
        out_shape=(pltpu.VMEM((8, model), f32), pltpu.VMEM((model, model), bf16)),
        in_specs=[in_hbm] * 4,
        out_specs=[in_vmem] * 2,
        scratch_shapes=[
            pltpu.VMEM((model,), f32),
            pltpu.VMEM((HEAD_DIM,), f32),
            pltpu.VMEM((HEAD_DIM,), f32),
            pltpu.SemaphoreType.DMA((4,)),
        ],
        compiler_params=pltpu.CompilerParams(vmem_limit_bytes=8 * 1024 * 1024),
        cost_estimate=pl.CostEstimate(flops=0, bytes_accessed=4 * model * model, transcendentals=0),
        name="held",
    )(*held[:4])
    result = pl.pallas_call(
        tokens_kernel,
        out_shape=jax.ShapeDtypeStruct(gathered.shape, bf16),
        in_specs=[in_vmem] * 3 + [in_hbm] * 2,
        out_specs=in_vmem,
        scratch_shapes=[
            pltpu.VMEM((model, 2 * model), bf16),
            pltpu.VMEM(w_out.shape, bf16),
            pltpu.VMEM((tokens, model), bf16),
            pltpu.VMEM((2 * tokens, model), f32),
            pltpu.VMEM((tokens, model), bf16),
            pltpu.VMEM((tokens, model), bf16),
            pltpu.VMEM((tokens, model), bf16),
            pltpu.VMEM((tokens, model), bf16),
            pltpu.SemaphoreType.DMA((3,)),
        ],
        compiler_params=pltpu.CompilerParams(vmem_limit_bytes=40 * 1024 * 1024),
        name="tokens",
    )(gathered, gains, wq, *held[3:])
    return exchange(result).reshape(latent.shape)


def solution(mesh):
    placed = (P(("groups", "frame"), None, None), P(), P(), P(), P(), P())
    return jax.shard_map(
        body,
        mesh=mesh,
        in_specs=placed,
        out_specs=P(("groups", "frame"), None, None),
        check_vma=False,
    )
```

```python
import functools
import math

import jax
import jax.numpy as jnp
from jax import lax
from jax.experimental import pallas as pl
from jax.experimental.pallas import tpu as pltpu
from jax.sharding import PartitionSpec as P

HEADS = 16
HEAD_DIM = 72
LANES = 128
EPS = 1e-06
EXP2_SCALE = HEAD_DIM**-0.5 * math.log2(math.e)


def dot(a, b):
    return jnp.dot(a, b, preferred_element_type=jnp.float32)


def held_kernel(
    ln_ref, qg_ref, kg_ref, wqkv_ref, gains_out, member_out, spread_out, wq_out, ln, qg, kg, sems
):
    width = wq_out.shape[1]
    pairs = [(ln_ref, ln), (qg_ref, qg), (kg_ref, kg), (wqkv_ref.at[:, pl.ds(0, width)], wq_out)]
    copies = [pltpu.make_async_copy(src, dst, sems.at[i]) for i, (src, dst) in enumerate(pairs)]
    for copy in copies:
        copy.start()

    def belongs(feature, lane):
        head = jnp.where(lane >= HEADS, lane - HEADS, lane)
        first = head * HEAD_DIM
        held = (feature >= first) & (feature < first + HEAD_DIM) & (lane < 2 * HEADS)
        return held.astype(jnp.float32).astype(jnp.bfloat16)

    for out, axis in ((member_out, 0), (spread_out, 1)):
        feature = lax.broadcasted_iota(jnp.int32, out.shape, axis)
        out[...] = belongs(feature, lax.broadcasted_iota(jnp.int32, out.shape, 1 - axis))
    for copy in copies[:3]:
        copy.wait()
    gains_out[0:1, :] = ln[...].reshape(1, width)
    gains_out[1:2, :] = jnp.concatenate([qg[...].reshape(1, HEAD_DIM)] * HEADS, axis=1)
    gains_out[2:3, :] = jnp.concatenate([kg[...].reshape(1, HEAD_DIM)] * HEADS, axis=1)
    copies[3].wait()


def tokens_kernel(
    x_ref,
    gains_ref,
    member_ref,
    spread_ref,
    wq,
    wqkv_hbm,
    wout_hbm,
    o_ref,
    wkv,
    wout,
    normed,
    mixed_q,
    mixed_k,
    queries,
    keys,
    values,
    attended,
    same,
    sems,
):
    frames, positions, width = x_ref.shape
    tokens = frames * positions
    bf16, f32 = jnp.bfloat16, jnp.float32

    pairs = [
        (wqkv_hbm.at[:, pl.ds(width, width)], wkv.at[:, pl.ds(0, width)]),
        (wqkv_hbm.at[:, pl.ds(2 * width, width)], wkv.at[:, pl.ds(width, width)]),
        (wout_hbm, wout),
    ]
    copies = [pltpu.make_async_copy(src, dst, sems.at[i]) for i, (src, dst) in enumerate(pairs)]
    for copy in copies:
        copy.start()

    gain = gains_ref[0:1, :]
    step = max(1, 16 // positions)
    for frame in range(0, frames, step):
        x = x_ref[frame : frame + step].astype(f32).reshape(step * positions, width)
        center = x - jnp.mean(x, axis=-1, keepdims=True)
        spread = jnp.mean(center * center, axis=-1, keepdims=True)
        rows = slice(frame * positions, (frame + step) * positions)
        normed[rows, :] = (center * lax.rsqrt(spread + EPS) * gain).astype(bf16)

    def head_norm(mixed, row, out):
        squares = mixed[...] * mixed[...]
        high = squares.astype(bf16)
        low = (squares - high.astype(f32)).astype(bf16)
        total = dot(jnp.concatenate([high, low], axis=0), member_ref[...])
        total = total[:tokens] + total[tokens:]
        inverse = lax.rsqrt(total * (1.0 / HEAD_DIM) + EPS)
        high = inverse.astype(bf16)
        low = (inverse - high.astype(f32)).astype(bf16)
        lane = lax.broadcasted_iota(jnp.int32, inverse.shape, 1)
        parts = jnp.where(lane < HEADS, high, low)[:, : 2 * HEADS]
        out[...] = (mixed[...] * dot(parts, spread_ref[...]) * gains_ref[row : row + 1, :]).astype(bf16)

    mixed_q[...] = dot(normed[...], wq[...])
    copies[0].wait()
    mixed_k[...] = dot(normed[...], wkv[:, :width])
    head_norm(mixed_q, 1, queries)
    copies[1].wait()
    values[...] = dot(normed[...], wkv[:, width:]).astype(bf16)
    head_norm(mixed_k, 2, keys)

    place = lax.broadcasted_iota(jnp.int32, (tokens, tokens), 0) % positions
    other = lax.broadcasted_iota(jnp.int32, (tokens, tokens), 1) % positions
    same[...] = (place == other).astype(f32)

    held = None
    for pair in range(HEADS // 2):
        window = slice(pair * LANES, (pair + 2) * LANES)
        lane = lax.broadcasted_iota(jnp.int32, (1, 2 * LANES), 1)
        begin = pair * (2 * HEAD_DIM - LANES)
        mine = [(lane >= begin + h * HEAD_DIM) & (lane < begin + (h + 1) * HEAD_DIM) for h in range(2)]
        zero = jnp.zeros((), bf16)
        key, value = (
            jnp.concatenate([jnp.where(own, ref[:, window], zero) for own in mine], axis=0)
            for ref in (keys, values)
        )
        scores = lax.dot_general(
            queries[:, window], key, (((1,), (1,)), ((), ())), preferred_element_type=f32
        )
        weights = []
        for h in range(2):
            part = jnp.exp2(scores[:, h * tokens : (h + 1) * tokens] * EXP2_SCALE) * same[...]
            weights.append((part / jnp.sum(part, axis=-1, keepdims=True)).astype(bf16))
        both = dot(jnp.concatenate(weights, axis=1), value)
        first = both[:, :LANES]
        if held is not None:
            first = first + held
        held = both[:, LANES:]
        attended[:, pair * LANES : (pair + 1) * LANES] = first.astype(bf16)
    attended[:, HEADS // 2 * LANES :] = held.astype(bf16)

    copies[2].wait()
    branch = dot(attended[...], wout[...])
    o_ref[...] = (x_ref[...].astype(f32) + branch.reshape(x_ref.shape)).astype(bf16)


def body(latent, ln_gain, q_gain, k_gain, w_qkv, w_out):
    device_count = lax.axis_size("frame")
    rows, columns, model = latent.shape
    tokens = rows * columns
    per_peer = tokens // device_count
    exchange = functools.partial(
        lax.all_to_all, axis_name="frame", split_axis=0, concat_axis=0, tiled=True
    )
    gathered = exchange(latent.reshape(device_count, per_peer, model))
    in_vmem = pl.BlockSpec(memory_space=pltpu.VMEM)
    in_hbm = pl.BlockSpec(memory_space=pltpu.HBM)
    bf16, f32 = jnp.bfloat16, jnp.float32
    held = [pltpu.with_memory_space_constraint(a, pltpu.HBM) for a in (ln_gain, q_gain, k_gain, w_qkv, w_out)]
    gains, member, spread, wq = pl.pallas_call(
        held_kernel,
        out_shape=(
            pltpu.VMEM((8, model), f32),
            pltpu.VMEM((model, LANES), bf16),
            pltpu.VMEM((2 * HEADS, model), bf16),
            pltpu.VMEM((model, model), bf16),
        ),
        in_specs=[in_hbm] * 4,
        out_specs=[in_vmem] * 4,
        scratch_shapes=[
            pltpu.VMEM((model,), f32),
            pltpu.VMEM((HEAD_DIM,), f32),
            pltpu.VMEM((HEAD_DIM,), f32),
            pltpu.SemaphoreType.DMA((4,)),
        ],
        compiler_params=pltpu.CompilerParams(vmem_limit_bytes=8 * 1024 * 1024),
        cost_estimate=pl.CostEstimate(flops=0, bytes_accessed=4 * model * model, transcendentals=0),
        name="held",
    )(*held[:4])
    result = pl.pallas_call(
        tokens_kernel,
        out_shape=jax.ShapeDtypeStruct(gathered.shape, bf16),
        in_specs=[in_vmem] * 5 + [in_hbm] * 2,
        out_specs=in_vmem,
        scratch_shapes=[
            pltpu.VMEM((model, 2 * model), bf16),
            pltpu.VMEM(w_out.shape, bf16),
            pltpu.VMEM((tokens, model), bf16),
            pltpu.VMEM((tokens, model), f32),
            pltpu.VMEM((tokens, model), f32),
            pltpu.VMEM((tokens, model), bf16),
            pltpu.VMEM((tokens, model), bf16),
            pltpu.VMEM((tokens, model), bf16),
            pltpu.VMEM((tokens, model), bf16),
            pltpu.VMEM((tokens, tokens), f32),
            pltpu.SemaphoreType.DMA((3,)),
        ],
        compiler_params=pltpu.CompilerParams(vmem_limit_bytes=40 * 1024 * 1024),
        name="tokens",
    )(gathered, gains, member, spread, wq, *held[3:])
    return exchange(result).reshape(latent.shape)


def solution(mesh):
    placed = (P(("groups", "frame"), None, None), P(), P(), P(), P(), P())
    return jax.shard_map(
        body,
        mesh=mesh,
        in_specs=placed,
        out_specs=P(("groups", "frame"), None, None),
        check_vma=False,
    )
```

```python
import functools
import math

import jax
import jax.numpy as jnp
from jax import lax
from jax.experimental import pallas as pl
from jax.experimental.pallas import tpu as pltpu
from jax.sharding import PartitionSpec as P

HEADS = 16
HEAD_DIM = 72
LANES = 128
EPS = 1e-06
EXP2_SCALE = HEAD_DIM**-0.5 * math.log2(math.e)


def dot(a, b):
    return jnp.dot(a, b, preferred_element_type=jnp.float32)


def held_kernel(
    ln_ref, qg_ref, kg_ref, wqkv_ref, gains_out, member_out, spread_out, wq_out, ln, qg, kg, sems
):
    width = wq_out.shape[1]
    pairs = [(ln_ref, ln), (qg_ref, qg), (kg_ref, kg), (wqkv_ref.at[:, pl.ds(0, width)], wq_out)]
    copies = [pltpu.make_async_copy(src, dst, sems.at[i]) for i, (src, dst) in enumerate(pairs)]
    for copy in copies:
        copy.start()

    def belongs(feature, lane):
        head = jnp.where(lane >= HEADS, lane - HEADS, lane)
        first = head * HEAD_DIM
        held = (feature >= first) & (feature < first + HEAD_DIM) & (lane < 2 * HEADS)
        return held.astype(jnp.float32).astype(jnp.bfloat16)

    for out, axis in ((member_out, 0), (spread_out, 1)):
        feature = lax.broadcasted_iota(jnp.int32, out.shape, axis)
        out[...] = belongs(feature, lax.broadcasted_iota(jnp.int32, out.shape, 1 - axis))
    for copy in copies[:3]:
        copy.wait()
    gains_out[0:1, :] = ln[...].reshape(1, width)
    gains_out[1:2, :] = jnp.concatenate([qg[...].reshape(1, HEAD_DIM)] * HEADS, axis=1)
    gains_out[2:3, :] = jnp.concatenate([kg[...].reshape(1, HEAD_DIM)] * HEADS, axis=1)
    copies[3].wait()


def tokens_kernel(
    x_ref,
    gains_ref,
    member_ref,
    spread_ref,
    wq,
    wqkv_hbm,
    wout_hbm,
    o_ref,
    wkv,
    wout,
    normed,
    mixed_q,
    mixed_k,
    queries,
    keys,
    values,
    attended,
    same,
    sems,
):
    frames, positions, width = x_ref.shape
    tokens = frames * positions
    bf16, f32 = jnp.bfloat16, jnp.float32

    pairs = [
        (wqkv_hbm.at[:, pl.ds(width, width)], wkv.at[:, pl.ds(0, width)]),
        (wqkv_hbm.at[:, pl.ds(2 * width, width)], wkv.at[:, pl.ds(width, width)]),
        (wout_hbm, wout),
    ]
    copies = [pltpu.make_async_copy(src, dst, sems.at[i]) for i, (src, dst) in enumerate(pairs)]
    for copy in copies:
        copy.start()

    gain = gains_ref[0:1, :]
    step = max(1, 16 // positions)

    def norm_rows(i, carry):
        x = x_ref[pl.ds(i * step, step)].astype(f32).reshape(step * positions, width)
        center = x - jnp.mean(x, axis=-1, keepdims=True)
        spread = jnp.mean(center * center, axis=-1, keepdims=True)
        rows = pl.ds(pl.multiple_of(i * step * positions, step * positions), step * positions)
        normed[rows, :] = (center * lax.rsqrt(spread + EPS) * gain).astype(bf16)
        return carry

    lax.fori_loop(0, frames // step, norm_rows, 0, unroll=2)

    def head_norm(mixed, row, out):
        squares = mixed[...] * mixed[...]
        high = squares.astype(bf16)
        low = (squares - high.astype(f32)).astype(bf16)
        total = dot(jnp.concatenate([high, low], axis=0), member_ref[...])
        total = total[:tokens] + total[tokens:]
        inverse = lax.rsqrt(total * (1.0 / HEAD_DIM) + EPS)
        high = inverse.astype(bf16)
        low = (inverse - high.astype(f32)).astype(bf16)
        lane = lax.broadcasted_iota(jnp.int32, inverse.shape, 1)
        parts = jnp.where(lane < HEADS, high, low)[:, : 2 * HEADS]
        out[...] = (mixed[...] * dot(parts, spread_ref[...]) * gains_ref[row : row + 1, :]).astype(bf16)

    mixed_q[...] = dot(normed[...], wq[...])
    copies[0].wait()
    mixed_k[...] = dot(normed[...], wkv[:, :width])
    head_norm(mixed_q, 1, queries)
    copies[1].wait()
    values[...] = dot(normed[...], wkv[:, width:]).astype(bf16)
    head_norm(mixed_k, 2, keys)

    place = lax.broadcasted_iota(jnp.int32, (tokens, tokens), 0) % positions
    other = lax.broadcasted_iota(jnp.int32, (tokens, tokens), 1) % positions
    same[...] = (place == other).astype(f32)

    lane = lax.broadcasted_iota(jnp.int32, (1, 2 * LANES), 1)
    zero = jnp.zeros((), bf16)

    def attend(pair, held):
        window = pl.ds(pl.multiple_of(pair * LANES, LANES), 2 * LANES)
        begin = pair * (2 * HEAD_DIM - LANES)
        mine = [(lane >= begin + h * HEAD_DIM) & (lane < begin + (h + 1) * HEAD_DIM) for h in range(2)]
        key, value = (
            jnp.concatenate([jnp.where(own, ref[:, window], zero) for own in mine], axis=0)
            for ref in (keys, values)
        )
        scores = lax.dot_general(
            queries[:, window], key, (((1,), (1,)), ((), ())), preferred_element_type=f32
        )
        weights = []
        for h in range(2):
            part = jnp.exp2(scores[:, h * tokens : (h + 1) * tokens] * EXP2_SCALE) * same[...]
            weights.append((part / jnp.sum(part, axis=-1, keepdims=True)).astype(bf16))
        both = dot(jnp.concatenate(weights, axis=1), value)
        tile = pl.ds(pl.multiple_of(pair * LANES, LANES), LANES)
        attended[:, tile] = (both[:, :LANES] + held).astype(bf16)
        return both[:, LANES:]

    last = lax.fori_loop(0, HEADS // 2, attend, jnp.zeros((tokens, LANES), f32), unroll=2)
    attended[:, HEADS // 2 * LANES :] = last.astype(bf16)

    copies[2].wait()
    branch = dot(attended[...], wout[...])
    o_ref[...] = (x_ref[...].astype(f32) + branch.reshape(x_ref.shape)).astype(bf16)


def body(latent, ln_gain, q_gain, k_gain, w_qkv, w_out):
    device_count = lax.axis_size("frame")
    rows, columns, model = latent.shape
    tokens = rows * columns
    per_peer = tokens // device_count
    exchange = functools.partial(
        lax.all_to_all, axis_name="frame", split_axis=0, concat_axis=0, tiled=True
    )
    gathered = exchange(latent.reshape(device_count, per_peer, model))
    in_vmem = pl.BlockSpec(memory_space=pltpu.VMEM)
    in_hbm = pl.BlockSpec(memory_space=pltpu.HBM)
    bf16, f32 = jnp.bfloat16, jnp.float32
    held = [pltpu.with_memory_space_constraint(a, pltpu.HBM) for a in (ln_gain, q_gain, k_gain, w_qkv, w_out)]
    gains, member, spread, wq = pl.pallas_call(
        held_kernel,
        out_shape=(
            pltpu.VMEM((8, model), f32),
            pltpu.VMEM((model, LANES), bf16),
            pltpu.VMEM((2 * HEADS, model), bf16),
            pltpu.VMEM((model, model), bf16),
        ),
        in_specs=[in_hbm] * 4,
        out_specs=[in_vmem] * 4,
        scratch_shapes=[
            pltpu.VMEM((model,), f32),
            pltpu.VMEM((HEAD_DIM,), f32),
            pltpu.VMEM((HEAD_DIM,), f32),
            pltpu.SemaphoreType.DMA((4,)),
        ],
        compiler_params=pltpu.CompilerParams(vmem_limit_bytes=8 * 1024 * 1024),
        cost_estimate=pl.CostEstimate(flops=0, bytes_accessed=4 * model * model, transcendentals=0),
        name="held",
    )(*held[:4])
    result = pl.pallas_call(
        tokens_kernel,
        out_shape=jax.ShapeDtypeStruct(gathered.shape, bf16),
        in_specs=[in_vmem] * 5 + [in_hbm] * 2,
        out_specs=in_vmem,
        scratch_shapes=[
            pltpu.VMEM((model, 2 * model), bf16),
            pltpu.VMEM(w_out.shape, bf16),
            pltpu.VMEM((tokens, model), bf16),
            pltpu.VMEM((tokens, model), f32),
            pltpu.VMEM((tokens, model), f32),
            pltpu.VMEM((tokens, model), bf16),
            pltpu.VMEM((tokens, model), bf16),
            pltpu.VMEM((tokens, model), bf16),
            pltpu.VMEM((tokens, model), bf16),
            pltpu.VMEM((tokens, tokens), f32),
            pltpu.SemaphoreType.DMA((3,)),
        ],
        compiler_params=pltpu.CompilerParams(vmem_limit_bytes=40 * 1024 * 1024),
        name="tokens",
    )(gathered, gains, member, spread, wq, *held[3:])
    return exchange(result).reshape(latent.shape)


def solution(mesh):
    placed = (P(("groups", "frame"), None, None), P(), P(), P(), P(), P())
    return jax.shard_map(
        body,
        mesh=mesh,
        in_specs=placed,
        out_specs=P(("groups", "frame"), None, None),
        check_vma=False,
    )
```

```python
import functools
import math

import jax
import jax.numpy as jnp
from jax import lax
from jax.experimental import pallas as pl
from jax.experimental.pallas import tpu as pltpu
from jax.sharding import PartitionSpec as P

HEADS = 16
HEAD_DIM = 72
LANES = 128
EPS = 1e-06
EXP2_SCALE = HEAD_DIM**-0.5 * math.log2(math.e)


def dot(a, b):
    return jnp.dot(a, b, preferred_element_type=jnp.float32)


def held_kernel(
    ln_ref, qg_ref, kg_ref, wqkv_ref, gains_out, member_out, spread_out, wq_out, ln, qg, kg, sems
):
    width = wq_out.shape[1]
    pairs = [(ln_ref, ln), (qg_ref, qg), (kg_ref, kg), (wqkv_ref.at[:, pl.ds(0, width)], wq_out)]
    copies = [pltpu.make_async_copy(src, dst, sems.at[i]) for i, (src, dst) in enumerate(pairs)]
    for copy in copies:
        copy.start()

    def belongs(feature, lane):
        head = jnp.where(lane >= HEADS, lane - HEADS, lane)
        first = head * HEAD_DIM
        held = (feature >= first) & (feature < first + HEAD_DIM) & (lane < 2 * HEADS)
        return held.astype(jnp.float32).astype(jnp.bfloat16)

    for out, axis in ((member_out, 0), (spread_out, 1)):
        feature = lax.broadcasted_iota(jnp.int32, out.shape, axis)
        out[...] = belongs(feature, lax.broadcasted_iota(jnp.int32, out.shape, 1 - axis))
    for copy in copies[:3]:
        copy.wait()
    gains_out[0:1, :] = ln[...].reshape(1, width)
    gains_out[1:2, :] = jnp.concatenate([qg[...].reshape(1, HEAD_DIM)] * HEADS, axis=1)
    gains_out[2:3, :] = jnp.concatenate([kg[...].reshape(1, HEAD_DIM)] * HEADS, axis=1)
    copies[3].wait()


def tokens_kernel(
    x_ref,
    gains_ref,
    member_ref,
    spread_ref,
    wq,
    wqkv_hbm,
    wout_hbm,
    o_ref,
    wkv,
    wout,
    normed,
    mixed_q,
    mixed_k,
    queries,
    keys,
    values,
    attended,
    same,
    sems,
):
    frames, positions, width = x_ref.shape
    tokens = frames * positions
    bf16, f32 = jnp.bfloat16, jnp.float32

    pairs = [
        (wqkv_hbm.at[:, pl.ds(width, width)], wkv.at[:, pl.ds(0, width)]),
        (wqkv_hbm.at[:, pl.ds(2 * width, width)], wkv.at[:, pl.ds(width, width)]),
        (wout_hbm, wout),
    ]
    copies = [pltpu.make_async_copy(src, dst, sems.at[i]) for i, (src, dst) in enumerate(pairs)]
    copies[0].start()

    gain = gains_ref[0:1, :]
    step = max(1, 16 // positions)
    for frame in range(0, frames, step):
        x = x_ref[frame : frame + step].astype(f32).reshape(step * positions, width)
        center = x - jnp.mean(x, axis=-1, keepdims=True)
        spread = jnp.mean(center * center, axis=-1, keepdims=True)
        rows = slice(frame * positions, (frame + step) * positions)
        normed[rows, :] = (center * lax.rsqrt(spread + EPS) * gain).astype(bf16)

    def head_norm(mixed, row, out):
        squares = mixed[...] * mixed[...]
        high = squares.astype(bf16)
        low = (squares - high.astype(f32)).astype(bf16)
        total = dot(jnp.concatenate([high, low], axis=0), member_ref[...])
        total = total[:tokens] + total[tokens:]
        inverse = lax.rsqrt(total * (1.0 / HEAD_DIM) + EPS)
        high = inverse.astype(bf16)
        low = (inverse - high.astype(f32)).astype(bf16)
        lane = lax.broadcasted_iota(jnp.int32, inverse.shape, 1)
        parts = jnp.where(lane < HEADS, high, low)[:, : 2 * HEADS]
        out[...] = (mixed[...] * dot(parts, spread_ref[...]) * gains_ref[row : row + 1, :]).astype(bf16)

    copies[1].start()
    mixed_q[...] = dot(normed[...], wq[...])
    head_norm(mixed_q, 1, queries)
    copies[0].wait()
    copies[2].start()
    mixed_k[...] = dot(normed[...], wkv[:, :width])
    head_norm(mixed_k, 2, keys)
    copies[1].wait()
    values[...] = dot(normed[...], wkv[:, width:]).astype(bf16)

    place = lax.broadcasted_iota(jnp.int32, (tokens, tokens), 0) % positions
    other = lax.broadcasted_iota(jnp.int32, (tokens, tokens), 1) % positions
    same[...] = (place == other).astype(f32)

    held = None
    for pair in range(HEADS // 2):
        window = slice(pair * LANES, (pair + 2) * LANES)
        lane = lax.broadcasted_iota(jnp.int32, (1, 2 * LANES), 1)
        begin = pair * (2 * HEAD_DIM - LANES)
        mine = [(lane >= begin + h * HEAD_DIM) & (lane < begin + (h + 1) * HEAD_DIM) for h in range(2)]
        zero = jnp.zeros((), bf16)
        key, value = (
            jnp.concatenate([jnp.where(own, ref[:, window], zero) for own in mine], axis=0)
            for ref in (keys, values)
        )
        scores = lax.dot_general(
            queries[:, window], key, (((1,), (1,)), ((), ())), preferred_element_type=f32
        )
        weights = []
        for h in range(2):
            part = jnp.exp2(scores[:, h * tokens : (h + 1) * tokens] * EXP2_SCALE) * same[...]
            weights.append((part / jnp.sum(part, axis=-1, keepdims=True)).astype(bf16))
        both = dot(jnp.concatenate(weights, axis=1), value)
        first = both[:, :LANES]
        if held is not None:
            first = first + held
        held = both[:, LANES:]
        attended[:, pair * LANES : (pair + 1) * LANES] = first.astype(bf16)
    attended[:, HEADS // 2 * LANES :] = held.astype(bf16)

    copies[2].wait()
    branch = dot(attended[...], wout[...])
    o_ref[...] = (x_ref[...].astype(f32) + branch.reshape(x_ref.shape)).astype(bf16)


def body(latent, ln_gain, q_gain, k_gain, w_qkv, w_out):
    device_count = lax.axis_size("frame")
    rows, columns, model = latent.shape
    tokens = rows * columns
    per_peer = tokens // device_count
    exchange = functools.partial(
        lax.all_to_all, axis_name="frame", split_axis=0, concat_axis=0, tiled=True
    )
    gathered = exchange(latent.reshape(device_count, per_peer, model))
    in_vmem = pl.BlockSpec(memory_space=pltpu.VMEM)
    in_hbm = pl.BlockSpec(memory_space=pltpu.HBM)
    bf16, f32 = jnp.bfloat16, jnp.float32
    held = [pltpu.with_memory_space_constraint(a, pltpu.HBM) for a in (ln_gain, q_gain, k_gain, w_qkv, w_out)]
    gains, member, spread, wq = pl.pallas_call(
        held_kernel,
        out_shape=(
            pltpu.VMEM((8, model), f32),
            pltpu.VMEM((model, LANES), bf16),
            pltpu.VMEM((2 * HEADS, model), bf16),
            pltpu.VMEM((model, model), bf16),
        ),
        in_specs=[in_hbm] * 4,
        out_specs=[in_vmem] * 4,
        scratch_shapes=[
            pltpu.VMEM((model,), f32),
            pltpu.VMEM((HEAD_DIM,), f32),
            pltpu.VMEM((HEAD_DIM,), f32),
            pltpu.SemaphoreType.DMA((4,)),
        ],
        compiler_params=pltpu.CompilerParams(vmem_limit_bytes=8 * 1024 * 1024),
        cost_estimate=pl.CostEstimate(flops=0, bytes_accessed=4 * model * model, transcendentals=0),
        name="held",
    )(*held[:4])
    result = pl.pallas_call(
        tokens_kernel,
        out_shape=jax.ShapeDtypeStruct(gathered.shape, bf16),
        in_specs=[in_vmem] * 5 + [in_hbm] * 2,
        out_specs=in_vmem,
        scratch_shapes=[
            pltpu.VMEM((model, 2 * model), bf16),
            pltpu.VMEM(w_out.shape, bf16),
            pltpu.VMEM((tokens, model), bf16),
            pltpu.VMEM((tokens, model), f32),
            pltpu.VMEM((tokens, model), f32),
            pltpu.VMEM((tokens, model), bf16),
            pltpu.VMEM((tokens, model), bf16),
            pltpu.VMEM((tokens, model), bf16),
            pltpu.VMEM((tokens, model), bf16),
            pltpu.VMEM((tokens, tokens), f32),
            pltpu.SemaphoreType.DMA((3,)),
        ],
        compiler_params=pltpu.CompilerParams(vmem_limit_bytes=40 * 1024 * 1024),
        name="tokens",
    )(gathered, gains, member, spread, wq, *held[3:])
    return exchange(result).reshape(latent.shape)


def solution(mesh):
    placed = (P(("groups", "frame"), None, None), P(), P(), P(), P(), P())
    return jax.shard_map(
        body,
        mesh=mesh,
        in_specs=placed,
        out_specs=P(("groups", "frame"), None, None),
        check_vma=False,
    )
```

```python
import math

import jax
import jax.numpy as jnp
from jax import lax
from jax.experimental import pallas as pl
from jax.experimental.pallas import tpu as pltpu
from jax.sharding import PartitionSpec as P

HEADS = 16
HEAD_DIM = 72
LANES = 128
EPS = 1e-06
EXP2_SCALE = HEAD_DIM**-0.5 * math.log2(math.e)


def dot(a, b):
    return jnp.dot(a, b, preferred_element_type=jnp.float32)


def layer_norm(x_ref, gain, out):
    frames, positions, width = x_ref.shape
    step = max(1, 16 // positions)
    for frame in range(0, frames, step):
        x = x_ref[frame : frame + step].astype(jnp.float32).reshape(step * positions, width)
        center = x - jnp.mean(x, axis=-1, keepdims=True)
        spread = jnp.mean(center * center, axis=-1, keepdims=True)
        rows = slice(frame * positions, (frame + step) * positions)
        out[rows, :] = (center * lax.rsqrt(spread + EPS) * gain).astype(jnp.bfloat16)


def head_norm(mixed, gain, member, spread, out):
    tokens = mixed.shape[0]
    bf16, f32 = jnp.bfloat16, jnp.float32
    squares = mixed[...] * mixed[...]
    high = squares.astype(bf16)
    low = (squares - high.astype(f32)).astype(bf16)
    total = dot(jnp.concatenate([high, low], axis=0), member[...])
    total = total[:tokens] + total[tokens:]
    inverse = lax.rsqrt(total * (1.0 / HEAD_DIM) + EPS)
    high = inverse.astype(bf16)
    low = (inverse - high.astype(f32)).astype(bf16)
    lane = lax.broadcasted_iota(jnp.int32, inverse.shape, 1)
    parts = jnp.where(lane < HEADS, high, low)[:, : 2 * HEADS]
    out[...] = (mixed[...] * dot(parts, spread[...]) * gain).astype(bf16)


def own_kernel(
    x_ref, ln_hbm, qg_hbm, kg_hbm, wqkv_hbm, wout_hbm,
    queries, keys, values, gains, member, spread, wkv, wout,
    ln, qg, kg, wq, normed, mixed_q, mixed_k, sems,
):
    width = x_ref.shape[-1]
    bf16 = jnp.bfloat16
    pairs = [(ln_hbm, ln), (qg_hbm, qg), (kg_hbm, kg), (wqkv_hbm.at[:, pl.ds(0, width)], wq)]
    pairs += [(wqkv_hbm.at[:, pl.ds(width, 2 * width)], wkv), (wout_hbm, wout)]
    copies = [pltpu.make_async_copy(src, dst, sems.at[i]) for i, (src, dst) in enumerate(pairs)]
    for copy in copies:
        copy.start()

    def belongs(feature, lane):
        head = jnp.where(lane >= HEADS, lane - HEADS, lane)
        first = head * HEAD_DIM
        held = (feature >= first) & (feature < first + HEAD_DIM) & (lane < 2 * HEADS)
        return held.astype(jnp.float32).astype(bf16)

    for out, axis in ((member, 0), (spread, 1)):
        feature = lax.broadcasted_iota(jnp.int32, out.shape, axis)
        out[...] = belongs(feature, lax.broadcasted_iota(jnp.int32, out.shape, 1 - axis))
    for copy in copies[:3]:
        copy.wait()
    gains[0:1, :] = ln[...].reshape(1, width)
    gains[1:2, :] = jnp.concatenate([qg[...].reshape(1, HEAD_DIM)] * HEADS, axis=1)
    gains[2:3, :] = jnp.concatenate([kg[...].reshape(1, HEAD_DIM)] * HEADS, axis=1)

    layer_norm(x_ref, gains[0:1, :], normed)
    copies[3].wait()
    mixed_q[...] = dot(normed[...], wq[...])
    head_norm(mixed_q, gains[1:2, :], member, spread, queries)
    copies[4].wait()
    mixed_k[...] = dot(normed[...], wkv[:, :width])
    head_norm(mixed_k, gains[2:3, :], member, spread, keys)
    values[...] = dot(normed[...], wkv[:, width:]).astype(bf16)
    copies[5].wait()


def tail_kernel(
    own_ref, other_ref, queries, own_keys, own_values, gains, member, spread, wkv, wout,
    o_ref, normed, mixed_k, other_keys, other_values, attended, same,
):
    frames, positions, width = own_ref.shape
    tokens = frames * positions
    bf16, f32 = jnp.bfloat16, jnp.float32

    layer_norm(other_ref, gains[0:1, :], normed)
    mixed_k[...] = dot(normed[...], wkv[:, :width])
    other_values[...] = dot(normed[...], wkv[:, width:]).astype(bf16)
    head_norm(mixed_k, gains[2:3, :], member, spread, other_keys)

    place = lax.broadcasted_iota(jnp.int32, (tokens, tokens), 0) % positions
    other = lax.broadcasted_iota(jnp.int32, (tokens, tokens), 1) % positions
    same[...] = (place == other).astype(f32)

    held = None
    zero = jnp.zeros((), bf16)
    for pair in range(HEADS // 2):
        window = slice(pair * LANES, (pair + 2) * LANES)
        lane = lax.broadcasted_iota(jnp.int32, (1, 2 * LANES), 1)
        begin = pair * (2 * HEAD_DIM - LANES)
        mine = [(lane >= begin + h * HEAD_DIM) & (lane < begin + (h + 1) * HEAD_DIM) for h in range(2)]
        both = None
        parts = []
        for key_ref in (own_keys, other_keys):
            key = jnp.concatenate([jnp.where(own, key_ref[:, window], zero) for own in mine], axis=0)
            scores = lax.dot_general(
                queries[:, window], key, (((1,), (1,)), ((), ())), preferred_element_type=f32
            )
            parts.append(
                [jnp.exp2(scores[:, h * tokens : (h + 1) * tokens] * EXP2_SCALE) * same[...] for h in range(2)]
            )
        sums = [jnp.sum(parts[0][h] + parts[1][h], axis=-1, keepdims=True) for h in range(2)]
        for half, value_ref in enumerate((own_values, other_values)):
            value = jnp.concatenate([jnp.where(own, value_ref[:, window], zero) for own in mine], axis=0)
            weights = jnp.concatenate([(parts[half][h] / sums[h]).astype(bf16) for h in range(2)], axis=1)
            product = dot(weights, value)
            both = product if both is None else both + product
        first = both[:, :LANES]
        if held is not None:
            first = first + held
        held = both[:, LANES:]
        attended[:, pair * LANES : (pair + 1) * LANES] = first.astype(bf16)
    attended[:, HEADS // 2 * LANES :] = held.astype(bf16)

    branch = dot(attended[...], wout[...])
    o_ref[...] = (own_ref[...].astype(f32) + branch.reshape(own_ref.shape)).astype(bf16)


def body(latent, ln_gain, q_gain, k_gain, w_qkv, w_out):
    device_count = lax.axis_size("frame")
    half = device_count // 2
    rows, columns, model = latent.shape
    tokens = rows * columns
    halves = [list(range(half)), list(range(half, device_count))]
    across = [(i, (i + half) % device_count) for i in range(device_count)]
    bf16, f32 = jnp.bfloat16, jnp.float32

    def exchange(slabs):
        return lax.all_to_all(slabs, "frame", 0, 0, axis_index_groups=halves, tiled=True)

    own = exchange(latent.reshape(half, tokens // half, model))
    other = lax.ppermute(own, "frame", across)

    in_vmem = pl.BlockSpec(memory_space=pltpu.VMEM)
    in_hbm = pl.BlockSpec(memory_space=pltpu.HBM)
    held = [pltpu.with_memory_space_constraint(a, pltpu.HBM) for a in (ln_gain, q_gain, k_gain, w_qkv, w_out)]
    rows16 = (tokens, model)
    kept = pl.pallas_call(
        own_kernel,
        out_shape=(
            pltpu.VMEM(rows16, bf16),
            pltpu.VMEM(rows16, bf16),
            pltpu.VMEM(rows16, bf16),
            pltpu.VMEM((8, model), f32),
            pltpu.VMEM((model, LANES), bf16),
            pltpu.VMEM((2 * HEADS, model), bf16),
            pltpu.VMEM((model, 2 * model), bf16),
            pltpu.VMEM(w_out.shape, bf16),
        ),
        in_specs=[in_vmem] + [in_hbm] * 5,
        out_specs=[in_vmem] * 8,
        scratch_shapes=[
            pltpu.VMEM((model,), f32),
            pltpu.VMEM((HEAD_DIM,), f32),
            pltpu.VMEM((HEAD_DIM,), f32),
            pltpu.VMEM((model, model), bf16),
            pltpu.VMEM(rows16, bf16),
            pltpu.VMEM(rows16, f32),
            pltpu.VMEM(rows16, f32),
            pltpu.SemaphoreType.DMA((6,)),
        ],
        compiler_params=pltpu.CompilerParams(vmem_limit_bytes=24 * 1024 * 1024),
        cost_estimate=pl.CostEstimate(
            flops=6 * tokens * model * model, bytes_accessed=8 * model * model, transcendentals=0
        ),
        name="own",
    )(own, *held)
    result = pl.pallas_call(
        tail_kernel,
        out_shape=jax.ShapeDtypeStruct(own.shape, bf16),
        in_specs=[in_vmem] * 10,
        out_specs=in_vmem,
        scratch_shapes=[
            pltpu.VMEM(rows16, bf16),
            pltpu.VMEM(rows16, f32),
            pltpu.VMEM(rows16, bf16),
            pltpu.VMEM(rows16, bf16),
            pltpu.VMEM(rows16, bf16),
            pltpu.VMEM((tokens, tokens), f32),
        ],
        compiler_params=pltpu.CompilerParams(vmem_limit_bytes=24 * 1024 * 1024),
        name="tail",
    )(own, other, *kept)
    return exchange(result).reshape(latent.shape)


def solution(mesh):
    placed = (P(("groups", "frame"), None, None), P(), P(), P(), P(), P())
    return jax.shard_map(
        body,
        mesh=mesh,
        in_specs=placed,
        out_specs=P(("groups", "frame"), None, None),
        check_vma=False,
    )
```

```python
import functools
import math

import jax
import jax.numpy as jnp
from jax import lax
from jax.experimental import pallas as pl
from jax.experimental.pallas import tpu as pltpu
from jax.sharding import PartitionSpec as P

HEADS = 16
HEAD_DIM = 72
LANES = 128
EPS = 1e-06
EXP2_SCALE = HEAD_DIM**-0.5 * math.log2(math.e)


def dot(a, b):
    return jnp.dot(a, b, preferred_element_type=jnp.float32)


def held_kernel(
    ln_ref, qg_ref, kg_ref, wqkv_ref, gains_out, member_out, spread_out, wq_out, ln, qg, kg, sems
):
    width = wq_out.shape[1]
    pairs = [(ln_ref, ln), (qg_ref, qg), (kg_ref, kg), (wqkv_ref.at[:, pl.ds(0, width)], wq_out)]
    copies = [pltpu.make_async_copy(src, dst, sems.at[i]) for i, (src, dst) in enumerate(pairs)]
    for copy in copies:
        copy.start()

    def belongs(feature, lane):
        head = jnp.where(lane >= HEADS, lane - HEADS, lane)
        first = head * HEAD_DIM
        held = (feature >= first) & (feature < first + HEAD_DIM) & (lane < 2 * HEADS)
        return held.astype(jnp.float32).astype(jnp.bfloat16)

    for out, axis in ((member_out, 0), (spread_out, 1)):
        feature = lax.broadcasted_iota(jnp.int32, out.shape, axis)
        out[...] = belongs(feature, lax.broadcasted_iota(jnp.int32, out.shape, 1 - axis))
    for copy in copies[:3]:
        copy.wait()
    gains_out[0:1, :] = ln[...].reshape(1, width)
    gains_out[1:2, :] = jnp.concatenate([qg[...].reshape(1, HEAD_DIM)] * HEADS, axis=1)
    gains_out[2:3, :] = jnp.concatenate([kg[...].reshape(1, HEAD_DIM)] * HEADS, axis=1)
    copies[3].wait()


def tokens_kernel(
    x_ref,
    gains_ref,
    member_ref,
    spread_ref,
    wq,
    wqkv_hbm,
    wout_hbm,
    o_ref,
    wkv,
    wout,
    normed,
    mixed_q,
    mixed_k,
    queries,
    queries_t,
    keys,
    values_t,
    attended_t,
    attended,
    same,
    sems,
):
    frames, positions, width = x_ref.shape
    tokens = frames * positions
    bf16, f32 = jnp.bfloat16, jnp.float32

    pairs = [(wqkv_hbm.at[:, pl.ds(width, 2 * width)], wkv), (wout_hbm, wout)]
    copies = [pltpu.make_async_copy(src, dst, sems.at[i]) for i, (src, dst) in enumerate(pairs)]
    copies[0].start()

    gain = gains_ref[0:1, :]
    step = max(1, 16 // positions)
    for frame in range(0, frames, step):
        x = x_ref[frame : frame + step].astype(f32).reshape(step * positions, width)
        center = x - jnp.mean(x, axis=-1, keepdims=True)
        spread = jnp.mean(center * center, axis=-1, keepdims=True)
        rows = slice(frame * positions, (frame + step) * positions)
        normed[rows, :] = (center * lax.rsqrt(spread + EPS) * gain).astype(bf16)

    def head_norm(mixed, row, out):
        squares = mixed[...] * mixed[...]
        high = squares.astype(bf16)
        low = (squares - high.astype(f32)).astype(bf16)
        total = dot(jnp.concatenate([high, low], axis=0), member_ref[...])
        total = total[:tokens] + total[tokens:]
        inverse = lax.rsqrt(total * (1.0 / HEAD_DIM) + EPS)
        high = inverse.astype(bf16)
        low = (inverse - high.astype(f32)).astype(bf16)
        lane = lax.broadcasted_iota(jnp.int32, inverse.shape, 1)
        parts = jnp.where(lane < HEADS, high, low)[:, : 2 * HEADS]
        out[...] = (mixed[...] * dot(parts, spread_ref[...]) * gains_ref[row : row + 1, :]).astype(bf16)

    copies[1].start()
    mixed_q[...] = dot(normed[...], wq[...])
    head_norm(mixed_q, 1, queries)
    copies[0].wait()
    mixed_k[...] = dot(normed[...], wkv[:, :width])
    queries_t[...] = queries[...].T
    values_t[...] = dot(normed[...], wkv[:, width:]).astype(bf16).T
    head_norm(mixed_k, 2, keys)

    place = lax.broadcasted_iota(jnp.int32, (tokens, tokens), 0) % positions
    other = lax.broadcasted_iota(jnp.int32, (tokens, tokens), 1) % positions
    same[...] = (place == other).astype(f32)

    row = lax.broadcasted_iota(jnp.int32, (2 * LANES, tokens), 0)
    for pair in range(HEADS // 2):
        window = slice(pair * LANES, (pair + 2) * LANES)
        begin = pair * (2 * HEAD_DIM - LANES)
        query = queries_t[window, :]
        both = [
            jnp.where((row >= begin + h * HEAD_DIM) & (row < begin + (h + 1) * HEAD_DIM), query, jnp.zeros((), bf16))
            for h in range(2)
        ]
        scores = dot(keys[:, window], jnp.concatenate(both, axis=1))
        weights = []
        for h in range(2):
            part = jnp.exp2(scores[:, h * tokens : (h + 1) * tokens] * EXP2_SCALE) * same[...]
            weights.append((part * (1.0 / jnp.sum(part, axis=0, keepdims=True))).astype(bf16))
        features = slice(pair * 2 * HEAD_DIM, (pair + 1) * 2 * HEAD_DIM)
        heads_out = dot(values_t[features, :], jnp.concatenate(weights, axis=1))
        for h in range(2):
            first = (2 * pair + h) * HEAD_DIM
            attended_t[first : first + HEAD_DIM, :] = heads_out[
                h * HEAD_DIM : (h + 1) * HEAD_DIM, h * tokens : (h + 1) * tokens
            ]
    attended[...] = attended_t[...].astype(bf16).T

    copies[1].wait()
    branch = dot(attended[...], wout[...])
    o_ref[...] = (x_ref[...].astype(f32) + branch.reshape(x_ref.shape)).astype(bf16)


def body(latent, ln_gain, q_gain, k_gain, w_qkv, w_out):
    device_count = lax.axis_size("frame")
    rows, columns, model = latent.shape
    tokens = rows * columns
    per_peer = tokens // device_count
    exchange = functools.partial(
        lax.all_to_all, axis_name="frame", split_axis=0, concat_axis=0, tiled=True
    )
    gathered = exchange(latent.reshape(device_count, per_peer, model))
    in_vmem = pl.BlockSpec(memory_space=pltpu.VMEM)
    in_hbm = pl.BlockSpec(memory_space=pltpu.HBM)
    bf16, f32 = jnp.bfloat16, jnp.float32
    held = [pltpu.with_memory_space_constraint(a, pltpu.HBM) for a in (ln_gain, q_gain, k_gain, w_qkv, w_out)]
    gains, member, spread, wq = pl.pallas_call(
        held_kernel,
        out_shape=(
            pltpu.VMEM((8, model), f32),
            pltpu.VMEM((model, LANES), bf16),
            pltpu.VMEM((2 * HEADS, model), bf16),
            pltpu.VMEM((model, model), bf16),
        ),
        in_specs=[in_hbm] * 4,
        out_specs=[in_vmem] * 4,
        scratch_shapes=[
            pltpu.VMEM((model,), f32),
            pltpu.VMEM((HEAD_DIM,), f32),
            pltpu.VMEM((HEAD_DIM,), f32),
            pltpu.SemaphoreType.DMA((4,)),
        ],
        compiler_params=pltpu.CompilerParams(vmem_limit_bytes=8 * 1024 * 1024),
        cost_estimate=pl.CostEstimate(flops=0, bytes_accessed=4 * model * model, transcendentals=0),
        name="held",
    )(*held[:4])
    result = pl.pallas_call(
        tokens_kernel,
        out_shape=jax.ShapeDtypeStruct(gathered.shape, bf16),
        in_specs=[in_vmem] * 5 + [in_hbm] * 2,
        out_specs=in_vmem,
        scratch_shapes=[
            pltpu.VMEM((model, 2 * model), bf16),
            pltpu.VMEM(w_out.shape, bf16),
            pltpu.VMEM((tokens, model), bf16),
            pltpu.VMEM((tokens, model), f32),
            pltpu.VMEM((tokens, model), f32),
            pltpu.VMEM((tokens, model), bf16),
            pltpu.VMEM((model, tokens), bf16),
            pltpu.VMEM((tokens, model), bf16),
            pltpu.VMEM((model, tokens), bf16),
            pltpu.VMEM((model, tokens), f32),
            pltpu.VMEM((tokens, model), bf16),
            pltpu.VMEM((tokens, tokens), f32),
            pltpu.SemaphoreType.DMA((2,)),
        ],
        compiler_params=pltpu.CompilerParams(vmem_limit_bytes=40 * 1024 * 1024),
        name="tokens",
    )(gathered, gains, member, spread, wq, *held[3:])
    return exchange(result).reshape(latent.shape)


def solution(mesh):
    placed = (P(("groups", "frame"), None, None), P(), P(), P(), P(), P())
    return jax.shard_map(
        body,
        mesh=mesh,
        in_specs=placed,
        out_specs=P(("groups", "frame"), None, None),
        check_vma=False,
    )
```

```python
import functools
import math

import jax
import jax.numpy as jnp
from jax import lax
from jax.experimental import pallas as pl
from jax.experimental.pallas import tpu as pltpu
from jax.sharding import PartitionSpec as P

HEADS = 16
HEAD_DIM = 72
LANES = 128
EPS = 1e-06
EXP2_SCALE = HEAD_DIM**-0.5 * math.log2(math.e)


def dot(a, b):
    return jnp.dot(a, b, preferred_element_type=jnp.float32)


def held_kernel(
    ln_ref, qg_ref, kg_ref, wqkv_ref, gains_out, member_out, spread_out, wq_out, ln, qg, kg, sems
):
    width = wq_out.shape[1]
    pairs = [(ln_ref, ln), (qg_ref, qg), (kg_ref, kg), (wqkv_ref.at[:, pl.ds(0, width)], wq_out)]
    copies = [pltpu.make_async_copy(src, dst, sems.at[i]) for i, (src, dst) in enumerate(pairs)]
    for copy in copies:
        copy.start()

    def belongs(feature, lane):
        head = jnp.where(lane >= HEADS, lane - HEADS, lane)
        first = head * HEAD_DIM
        held = (feature >= first) & (feature < first + HEAD_DIM) & (lane < 2 * HEADS)
        return held.astype(jnp.float32).astype(jnp.bfloat16)

    for out, axis in ((member_out, 0), (spread_out, 1)):
        feature = lax.broadcasted_iota(jnp.int32, out.shape, axis)
        out[...] = belongs(feature, lax.broadcasted_iota(jnp.int32, out.shape, 1 - axis))
    for copy in copies[:3]:
        copy.wait()
    gains_out[0:1, :] = ln[...].reshape(1, width)
    gains_out[1:2, :] = jnp.concatenate([qg[...].reshape(1, HEAD_DIM)] * HEADS, axis=1)
    gains_out[2:3, :] = jnp.concatenate([kg[...].reshape(1, HEAD_DIM)] * HEADS, axis=1)
    copies[3].wait()


def tokens_kernel(
    x_ref,
    gains_ref,
    member_ref,
    spread_ref,
    wq,
    wqkv_hbm,
    wout_hbm,
    o_ref,
    wkv,
    wout,
    normed,
    mixed_q,
    mixed_k,
    queries,
    queries_t,
    keys,
    values_t,
    attended_t,
    attended,
    same,
    sems,
):
    frames, positions, width = x_ref.shape
    tokens = frames * positions
    bf16, f32 = jnp.bfloat16, jnp.float32

    pairs = [
        (wqkv_hbm.at[:, pl.ds(width, width)], wkv.at[:, pl.ds(0, width)]),
        (wqkv_hbm.at[:, pl.ds(2 * width, width)], wkv.at[:, pl.ds(width, width)]),
        (wout_hbm, wout),
    ]
    copies = [pltpu.make_async_copy(src, dst, sems.at[i]) for i, (src, dst) in enumerate(pairs)]
    copies[0].start()

    gain = gains_ref[0:1, :]
    step = max(1, 16 // positions)
    for frame in range(0, frames, step):
        x = x_ref[frame : frame + step].astype(f32).reshape(step * positions, width)
        center = x - jnp.mean(x, axis=-1, keepdims=True)
        spread = jnp.mean(center * center, axis=-1, keepdims=True)
        rows = slice(frame * positions, (frame + step) * positions)
        normed[rows, :] = (center * lax.rsqrt(spread + EPS) * gain).astype(bf16)

    def head_norm(mixed, row, out):
        squares = mixed[...] * mixed[...]
        high = squares.astype(bf16)
        low = (squares - high.astype(f32)).astype(bf16)
        total = dot(jnp.concatenate([high, low], axis=0), member_ref[...])
        total = total[:tokens] + total[tokens:]
        inverse = lax.rsqrt(total * (1.0 / HEAD_DIM) + EPS)
        high = inverse.astype(bf16)
        low = (inverse - high.astype(f32)).astype(bf16)
        lane = lax.broadcasted_iota(jnp.int32, inverse.shape, 1)
        parts = jnp.where(lane < HEADS, high, low)[:, : 2 * HEADS]
        out[...] = (mixed[...] * dot(parts, spread_ref[...]) * gains_ref[row : row + 1, :]).astype(bf16)

    copies[1].start()
    mixed_q[...] = dot(normed[...], wq[...])
    head_norm(mixed_q, 1, queries)
    copies[0].wait()
    copies[2].start()
    mixed_k[...] = dot(normed[...], wkv[:, :width])
    queries_t[...] = queries[...].T
    head_norm(mixed_k, 2, keys)
    copies[1].wait()
    values_t[...] = dot(normed[...], wkv[:, width:]).astype(bf16).T

    place = lax.broadcasted_iota(jnp.int32, (tokens, tokens), 0) % positions
    other = lax.broadcasted_iota(jnp.int32, (tokens, tokens), 1) % positions
    same[...] = (place == other).astype(f32)

    row = lax.broadcasted_iota(jnp.int32, (2 * LANES, tokens), 0)
    for pair in range(HEADS // 2):
        window = slice(pair * LANES, (pair + 2) * LANES)
        begin = pair * (2 * HEAD_DIM - LANES)
        query = queries_t[window, :]
        both = [
            jnp.where((row >= begin + h * HEAD_DIM) & (row < begin + (h + 1) * HEAD_DIM), query, jnp.zeros((), bf16))
            for h in range(2)
        ]
        scores = dot(keys[:, window], jnp.concatenate(both, axis=1))
        weights = []
        for h in range(2):
            part = jnp.exp2(scores[:, h * tokens : (h + 1) * tokens] * EXP2_SCALE) * same[...]
            weights.append((part * (1.0 / jnp.sum(part, axis=0, keepdims=True))).astype(bf16))
        features = slice(pair * 2 * HEAD_DIM, (pair + 1) * 2 * HEAD_DIM)
        heads_out = dot(values_t[features, :], jnp.concatenate(weights, axis=1))
        for h in range(2):
            first = (2 * pair + h) * HEAD_DIM
            attended_t[first : first + HEAD_DIM, :] = heads_out[
                h * HEAD_DIM : (h + 1) * HEAD_DIM, h * tokens : (h + 1) * tokens
            ]
    attended[...] = attended_t[...].astype(bf16).T

    copies[2].wait()
    branch = dot(attended[...], wout[...])
    o_ref[...] = (x_ref[...].astype(f32) + branch.reshape(x_ref.shape)).astype(bf16)


def body(latent, ln_gain, q_gain, k_gain, w_qkv, w_out):
    device_count = lax.axis_size("frame")
    rows, columns, model = latent.shape
    tokens = rows * columns
    per_peer = tokens // device_count
    exchange = functools.partial(
        lax.all_to_all, axis_name="frame", split_axis=0, concat_axis=0, tiled=True
    )
    gathered = exchange(latent.reshape(device_count, per_peer, model))
    in_vmem = pl.BlockSpec(memory_space=pltpu.VMEM)
    in_hbm = pl.BlockSpec(memory_space=pltpu.HBM)
    bf16, f32 = jnp.bfloat16, jnp.float32
    held = [pltpu.with_memory_space_constraint(a, pltpu.HBM) for a in (ln_gain, q_gain, k_gain, w_qkv, w_out)]
    gains, member, spread, wq = pl.pallas_call(
        held_kernel,
        out_shape=(
            pltpu.VMEM((8, model), f32),
            pltpu.VMEM((model, LANES), bf16),
            pltpu.VMEM((2 * HEADS, model), bf16),
            pltpu.VMEM((model, model), bf16),
        ),
        in_specs=[in_hbm] * 4,
        out_specs=[in_vmem] * 4,
        scratch_shapes=[
            pltpu.VMEM((model,), f32),
            pltpu.VMEM((HEAD_DIM,), f32),
            pltpu.VMEM((HEAD_DIM,), f32),
            pltpu.SemaphoreType.DMA((4,)),
        ],
        compiler_params=pltpu.CompilerParams(vmem_limit_bytes=8 * 1024 * 1024),
        cost_estimate=pl.CostEstimate(flops=0, bytes_accessed=4 * model * model, transcendentals=0),
        name="held",
    )(*held[:4])
    result = pl.pallas_call(
        tokens_kernel,
        out_shape=jax.ShapeDtypeStruct(gathered.shape, bf16),
        in_specs=[in_vmem] * 5 + [in_hbm] * 2,
        out_specs=in_vmem,
        scratch_shapes=[
            pltpu.VMEM((model, 2 * model), bf16),
            pltpu.VMEM(w_out.shape, bf16),
            pltpu.VMEM((tokens, model), bf16),
            pltpu.VMEM((tokens, model), f32),
            pltpu.VMEM((tokens, model), f32),
            pltpu.VMEM((tokens, model), bf16),
            pltpu.VMEM((model, tokens), bf16),
            pltpu.VMEM((tokens, model), bf16),
            pltpu.VMEM((model, tokens), bf16),
            pltpu.VMEM((model, tokens), f32),
            pltpu.VMEM((tokens, model), bf16),
            pltpu.VMEM((tokens, tokens), f32),
            pltpu.SemaphoreType.DMA((3,)),
        ],
        compiler_params=pltpu.CompilerParams(vmem_limit_bytes=40 * 1024 * 1024),
        name="tokens",
    )(gathered, gains, member, spread, wq, *held[3:])
    return exchange(result).reshape(latent.shape)


def solution(mesh):
    placed = (P(("groups", "frame"), None, None), P(), P(), P(), P(), P())
    return jax.shard_map(
        body,
        mesh=mesh,
        in_specs=placed,
        out_specs=P(("groups", "frame"), None, None),
        check_vma=False,
    )
```

```python
import functools
import math

import jax
import jax.numpy as jnp
from jax import lax
from jax.experimental import pallas as pl
from jax.experimental.pallas import tpu as pltpu
from jax.sharding import PartitionSpec as P

HEADS = 16
HEAD_DIM = 72
LANES = 128
EPS = 1e-06
EXP2_SCALE = HEAD_DIM**-0.5 * math.log2(math.e)


def dot(a, b):
    return jnp.dot(a, b, preferred_element_type=jnp.float32)


def held_kernel(ln_ref, qg_ref, kg_ref, wqkv_ref, gain_out, head_gains_out, wq_out, ln, qg, kg, sems):
    width = wq_out.shape[1]
    pairs = [(ln_ref, ln), (qg_ref, qg), (kg_ref, kg), (wqkv_ref.at[:, pl.ds(0, width)], wq_out)]
    copies = [pltpu.make_async_copy(src, dst, sems.at[i]) for i, (src, dst) in enumerate(pairs)]
    for copy in copies:
        copy.start()
    for copy in copies[:3]:
        copy.wait()
    gain_out[...] = ln[...].reshape(1, width)
    for i, held in enumerate((qg, kg)):
        row = held[...].reshape(1, HEAD_DIM)
        row = jnp.concatenate([row, jnp.zeros((1, LANES - HEAD_DIM), jnp.float32)], axis=1)
        head_gains_out[i] = jnp.broadcast_to(row, (LANES, LANES)).T[:HEAD_DIM]
    copies[3].wait()


def tokens_kernel(
    x_ref,
    gain_ref,
    head_gains_ref,
    wq,
    wqkv_hbm,
    wout_hbm,
    o_ref,
    wkv,
    wout,
    normed,
    mixed,
    queries_t,
    keys_t,
    keys,
    values_t,
    attended_t,
    attended,
    same,
    sems,
):
    frames, positions, width = x_ref.shape
    tokens = frames * positions
    bf16, f32 = jnp.bfloat16, jnp.float32

    pairs = [
        (wqkv_hbm.at[:, pl.ds(width, width)], wkv.at[:, pl.ds(0, width)]),
        (wqkv_hbm.at[:, pl.ds(2 * width, width)], wkv.at[:, pl.ds(width, width)]),
        (wout_hbm, wout),
    ]
    copies = [pltpu.make_async_copy(src, dst, sems.at[i]) for i, (src, dst) in enumerate(pairs)]
    copies[0].start()

    gain = gain_ref[...]
    step = max(1, 16 // positions)
    for frame in range(0, frames, step):
        x = x_ref[frame : frame + step].astype(f32).reshape(step * positions, width)
        center = x - jnp.mean(x, axis=-1, keepdims=True)
        spread = jnp.mean(center * center, axis=-1, keepdims=True)
        rows = slice(frame * positions, (frame + step) * positions)
        normed[rows, :] = (center * lax.rsqrt(spread + EPS) * gain).astype(bf16)

    def head_norm(mixed, which):
        for pair in range(HEADS // 2):
            heads = []
            for first in (2 * pair * HEAD_DIM, (2 * pair + 1) * HEAD_DIM):
                head = mixed[first : first + HEAD_DIM, :]
                total = jnp.sum(head * head, axis=0, keepdims=True)
                heads.append(head * lax.rsqrt(total * (1.0 / HEAD_DIM) + EPS) * head_gains_ref[which])
            yield slice(2 * pair * HEAD_DIM, (2 * pair + 2) * HEAD_DIM), jnp.concatenate(heads, axis=0).astype(bf16)

    copies[1].start()
    mixed[...] = dot(normed[...], wq[...]).T
    for rows, heads in head_norm(mixed, 0):
        queries_t[rows, :] = heads
    copies[0].wait()
    copies[2].start()
    mixed[...] = dot(normed[...], wkv[:, :width]).T
    for rows, heads in head_norm(mixed, 1):
        keys_t[rows, :] = heads
    keys[...] = keys_t[...].T
    copies[1].wait()
    values_t[...] = dot(normed[...], wkv[:, width:]).astype(bf16).T

    place = lax.broadcasted_iota(jnp.int32, (tokens, tokens), 0) % positions
    other = lax.broadcasted_iota(jnp.int32, (tokens, tokens), 1) % positions
    same[...] = (place == other).astype(f32)

    row = lax.broadcasted_iota(jnp.int32, (2 * LANES, tokens), 0)
    for pair in range(HEADS // 2):
        window = slice(pair * LANES, (pair + 2) * LANES)
        begin = pair * (2 * HEAD_DIM - LANES)
        query = queries_t[window, :]
        both = [
            jnp.where((row >= begin + h * HEAD_DIM) & (row < begin + (h + 1) * HEAD_DIM), query, jnp.zeros((), bf16))
            for h in range(2)
        ]
        scores = dot(keys[:, window], jnp.concatenate(both, axis=1))
        weights = []
        for h in range(2):
            part = jnp.exp2(scores[:, h * tokens : (h + 1) * tokens] * EXP2_SCALE) * same[...]
            weights.append((part * (1.0 / jnp.sum(part, axis=0, keepdims=True))).astype(bf16))
        features = slice(pair * 2 * HEAD_DIM, (pair + 1) * 2 * HEAD_DIM)
        heads_out = dot(values_t[features, :], jnp.concatenate(weights, axis=1))
        for h in range(2):
            first = (2 * pair + h) * HEAD_DIM
            attended_t[first : first + HEAD_DIM, :] = heads_out[
                h * HEAD_DIM : (h + 1) * HEAD_DIM, h * tokens : (h + 1) * tokens
            ]
    attended[...] = attended_t[...].astype(bf16).T

    copies[2].wait()
    branch = dot(attended[...], wout[...])
    o_ref[...] = (x_ref[...].astype(f32) + branch.reshape(x_ref.shape)).astype(bf16)


def body(latent, ln_gain, q_gain, k_gain, w_qkv, w_out):
    device_count = lax.axis_size("frame")
    rows, columns, model = latent.shape
    tokens = rows * columns
    per_peer = tokens // device_count
    exchange = functools.partial(
        lax.all_to_all, axis_name="frame", split_axis=0, concat_axis=0, tiled=True
    )
    gathered = exchange(latent.reshape(device_count, per_peer, model))
    in_vmem = pl.BlockSpec(memory_space=pltpu.VMEM)
    in_hbm = pl.BlockSpec(memory_space=pltpu.HBM)
    bf16, f32 = jnp.bfloat16, jnp.float32
    held = [pltpu.with_memory_space_constraint(a, pltpu.HBM) for a in (ln_gain, q_gain, k_gain, w_qkv, w_out)]
    gain, head_gains, wq = pl.pallas_call(
        held_kernel,
        out_shape=(
            pltpu.VMEM((1, model), f32),
            pltpu.VMEM((2, HEAD_DIM, LANES), f32),
            pltpu.VMEM((model, model), bf16),
        ),
        in_specs=[in_hbm] * 4,
        out_specs=[in_vmem] * 3,
        scratch_shapes=[
            pltpu.VMEM((model,), f32),
            pltpu.VMEM((HEAD_DIM,), f32),
            pltpu.VMEM((HEAD_DIM,), f32),
            pltpu.SemaphoreType.DMA((4,)),
        ],
        compiler_params=pltpu.CompilerParams(vmem_limit_bytes=8 * 1024 * 1024),
        cost_estimate=pl.CostEstimate(flops=0, bytes_accessed=4 * model * model, transcendentals=0),
        name="held",
    )(*held[:4])
    result = pl.pallas_call(
        tokens_kernel,
        out_shape=jax.ShapeDtypeStruct(gathered.shape, bf16),
        in_specs=[in_vmem] * 4 + [in_hbm] * 2,
        out_specs=in_vmem,
        scratch_shapes=[
            pltpu.VMEM((model, 2 * model), bf16),
            pltpu.VMEM(w_out.shape, bf16),
            pltpu.VMEM((tokens, model), bf16),
            pltpu.VMEM((model, tokens), f32),
            pltpu.VMEM((model, tokens), bf16),
            pltpu.VMEM((model, tokens), bf16),
            pltpu.VMEM((tokens, model), bf16),
            pltpu.VMEM((model, tokens), bf16),
            pltpu.VMEM((model, tokens), f32),
            pltpu.VMEM((tokens, model), bf16),
            pltpu.VMEM((tokens, tokens), f32),
            pltpu.SemaphoreType.DMA((3,)),
        ],
        compiler_params=pltpu.CompilerParams(vmem_limit_bytes=40 * 1024 * 1024),
        name="tokens",
    )(gathered, gain, head_gains, wq, *held[3:])
    return exchange(result).reshape(latent.shape)


def solution(mesh):
    placed = (P(("groups", "frame"), None, None), P(), P(), P(), P(), P())
    return jax.shard_map(
        body,
        mesh=mesh,
        in_specs=placed,
        out_specs=P(("groups", "frame"), None, None),
        check_vma=False,
    )
```

```python
import functools
import math

import jax
import jax.numpy as jnp
from jax import lax
from jax.experimental import pallas as pl
from jax.experimental.pallas import tpu as pltpu
from jax.sharding import PartitionSpec as P

HEADS = 16
HEAD_DIM = 72
LANES = 128
EPS = 1e-06
EXP2_SCALE = HEAD_DIM**-0.5 * math.log2(math.e)


def dot(a, b):
    return jnp.dot(a, b, preferred_element_type=jnp.float32)


def held_kernel(
    ln_ref, qg_ref, kg_ref, wqkv_ref, gains_out, member_out, spread_out, wq_out, ln, qg, kg, sems
):
    width = wq_out.shape[1]
    pairs = [(ln_ref, ln), (qg_ref, qg), (kg_ref, kg), (wqkv_ref.at[:, pl.ds(0, width)], wq_out)]
    copies = [pltpu.make_async_copy(src, dst, sems.at[i]) for i, (src, dst) in enumerate(pairs)]
    for copy in copies:
        copy.start()

    def belongs(feature, lane):
        head = jnp.where(lane >= HEADS, lane - HEADS, lane)
        first = head * HEAD_DIM
        held = (feature >= first) & (feature < first + HEAD_DIM) & (lane < 2 * HEADS)
        return held.astype(jnp.float32).astype(jnp.bfloat16)

    for out, axis in ((member_out, 0), (spread_out, 1)):
        feature = lax.broadcasted_iota(jnp.int32, out.shape, axis)
        out[...] = belongs(feature, lax.broadcasted_iota(jnp.int32, out.shape, 1 - axis))
    for copy in copies[:3]:
        copy.wait()
    gains_out[0:1, :] = ln[...].reshape(1, width)
    gains_out[1:2, :] = jnp.concatenate([qg[...].reshape(1, HEAD_DIM)] * HEADS, axis=1)
    gains_out[2:3, :] = jnp.concatenate([kg[...].reshape(1, HEAD_DIM)] * HEADS, axis=1)
    copies[3].wait()


def tokens_kernel(
    x_ref,
    gains_ref,
    member_ref,
    spread_ref,
    wq,
    wqkv_hbm,
    wout_hbm,
    o_ref,
    wkv,
    wout,
    normed,
    mixed_q,
    mixed_k,
    queries,
    queries_t,
    keys,
    values_t,
    attended_t,
    attended,
    same,
    sems,
):
    frames, positions, width = x_ref.shape
    tokens = frames * positions
    bf16, f32 = jnp.bfloat16, jnp.float32

    pairs = [
        (wqkv_hbm.at[:, pl.ds(width, width)], wkv.at[:, pl.ds(0, width)]),
        (wqkv_hbm.at[:, pl.ds(2 * width, width)], wkv.at[:, pl.ds(width, width)]),
        (wout_hbm, wout),
    ]
    copies = [pltpu.make_async_copy(src, dst, sems.at[i]) for i, (src, dst) in enumerate(pairs)]
    copies[0].start()

    gain = gains_ref[0:1, :]
    step = max(1, 16 // positions)
    for frame in range(0, frames, step):
        x = x_ref[frame : frame + step].astype(f32).reshape(step * positions, width)
        center = x - jnp.mean(x, axis=-1, keepdims=True)
        spread = jnp.mean(center * center, axis=-1, keepdims=True)
        rows = slice(frame * positions, (frame + step) * positions)
        normed[rows, :] = (center * lax.rsqrt(spread + EPS) * gain).astype(bf16)

    def head_norm(mixed, row, out):
        squares = mixed[...] * mixed[...]
        high = squares.astype(bf16)
        low = (squares - high.astype(f32)).astype(bf16)
        total = dot(jnp.concatenate([high, low], axis=0), member_ref[...])
        total = total[:tokens] + total[tokens:]
        inverse = lax.rsqrt(total * (1.0 / HEAD_DIM) + EPS)
        high = inverse.astype(bf16)
        low = (inverse - high.astype(f32)).astype(bf16)
        lane = lax.broadcasted_iota(jnp.int32, inverse.shape, 1)
        parts = jnp.where(lane < HEADS, high, low)[:, : 2 * HEADS]
        out[...] = (mixed[...] * dot(parts, spread_ref[...]) * gains_ref[row : row + 1, :]).astype(bf16)

    copies[1].start()
    mixed_q[...] = dot(normed[...], wq[...])
    head_norm(mixed_q, 1, queries)
    copies[0].wait()
    copies[2].start()
    mixed_k[...] = dot(normed[...], wkv[:, :width])
    queries_t[...] = queries[...].T
    head_norm(mixed_k, 2, keys)
    copies[1].wait()
    values_t[...] = dot(normed[...], wkv[:, width:]).astype(bf16).T

    place = lax.broadcasted_iota(jnp.int32, (tokens, tokens), 0) % positions
    other = lax.broadcasted_iota(jnp.int32, (tokens, tokens), 1) % positions
    same[...] = (place == other).astype(f32)

    row = lax.broadcasted_iota(jnp.int32, (2 * LANES, tokens), 0)
    for pair in range(HEADS // 2):
        window = slice(pair * LANES, (pair + 2) * LANES)
        begin = pair * (2 * HEAD_DIM - LANES)
        query = queries_t[window, :]
        both = [
            jnp.where((row >= begin + h * HEAD_DIM) & (row < begin + (h + 1) * HEAD_DIM), query, jnp.zeros((), bf16))
            for h in range(2)
        ]
        scores = dot(keys[:, window], jnp.concatenate(both, axis=1))
        weights = []
        for h in range(2):
            part = jnp.exp2(scores[:, h * tokens : (h + 1) * tokens] * EXP2_SCALE) * same[...]
            weights.append((part * (1.0 / jnp.sum(part, axis=0, keepdims=True))).astype(bf16))
        features = slice(pair * 2 * HEAD_DIM, (pair + 1) * 2 * HEAD_DIM)
        heads_out = dot(values_t[features, :], jnp.concatenate(weights, axis=1))
        for h in range(2):
            first = (2 * pair + h) * HEAD_DIM
            attended_t[first : first + HEAD_DIM, :] = heads_out[
                h * HEAD_DIM : (h + 1) * HEAD_DIM, h * tokens : (h + 1) * tokens
            ]
    attended[...] = attended_t[...].astype(bf16).T

    copies[2].wait()
    branch = dot(attended[...], wout[...])
    o_ref[...] = (x_ref[...].astype(f32) + branch.reshape(x_ref.shape)).astype(bf16)


def body(latent, ln_gain, q_gain, k_gain, w_qkv, w_out):
    device_count = lax.axis_size("frame")
    rows, columns, model = latent.shape
    tokens = rows * columns
    per_peer = tokens // device_count
    half = device_count // 2
    order = [part * half + i for i in range(half) for part in range(2)]
    exchange = functools.partial(
        lax.all_to_all, axis_name="frame", split_axis=0, concat_axis=0, axis_index_groups=[order], tiled=True
    )
    gathered = exchange(latent.reshape(device_count, per_peer, model))
    in_vmem = pl.BlockSpec(memory_space=pltpu.VMEM)
    in_hbm = pl.BlockSpec(memory_space=pltpu.HBM)
    bf16, f32 = jnp.bfloat16, jnp.float32
    held = [pltpu.with_memory_space_constraint(a, pltpu.HBM) for a in (ln_gain, q_gain, k_gain, w_qkv, w_out)]
    gains, member, spread, wq = pl.pallas_call(
        held_kernel,
        out_shape=(
            pltpu.VMEM((8, model), f32),
            pltpu.VMEM((model, LANES), bf16),
            pltpu.VMEM((2 * HEADS, model), bf16),
            pltpu.VMEM((model, model), bf16),
        ),
        in_specs=[in_hbm] * 4,
        out_specs=[in_vmem] * 4,
        scratch_shapes=[
            pltpu.VMEM((model,), f32),
            pltpu.VMEM((HEAD_DIM,), f32),
            pltpu.VMEM((HEAD_DIM,), f32),
            pltpu.SemaphoreType.DMA((4,)),
        ],
        compiler_params=pltpu.CompilerParams(vmem_limit_bytes=8 * 1024 * 1024),
        cost_estimate=pl.CostEstimate(flops=0, bytes_accessed=4 * model * model, transcendentals=0),
        name="held",
    )(*held[:4])
    result = pl.pallas_call(
        tokens_kernel,
        out_shape=jax.ShapeDtypeStruct(gathered.shape, bf16),
        in_specs=[in_vmem] * 5 + [in_hbm] * 2,
        out_specs=in_vmem,
        scratch_shapes=[
            pltpu.VMEM((model, 2 * model), bf16),
            pltpu.VMEM(w_out.shape, bf16),
            pltpu.VMEM((tokens, model), bf16),
            pltpu.VMEM((tokens, model), f32),
            pltpu.VMEM((tokens, model), f32),
            pltpu.VMEM((tokens, model), bf16),
            pltpu.VMEM((model, tokens), bf16),
            pltpu.VMEM((tokens, model), bf16),
            pltpu.VMEM((model, tokens), bf16),
            pltpu.VMEM((model, tokens), f32),
            pltpu.VMEM((tokens, model), bf16),
            pltpu.VMEM((tokens, tokens), f32),
            pltpu.SemaphoreType.DMA((3,)),
        ],
        compiler_params=pltpu.CompilerParams(vmem_limit_bytes=40 * 1024 * 1024),
        name="tokens",
    )(gathered, gains, member, spread, wq, *held[3:])
    return exchange(result).reshape(latent.shape)


def solution(mesh):
    placed = (P(("groups", "frame"), None, None), P(), P(), P(), P(), P())
    return jax.shard_map(
        body,
        mesh=mesh,
        in_specs=placed,
        out_specs=P(("groups", "frame"), None, None),
        check_vma=False,
    )
```

```python
import functools
import math

import jax
import jax.numpy as jnp
from jax import lax
from jax.experimental import pallas as pl
from jax.experimental.pallas import tpu as pltpu
from jax.sharding import PartitionSpec as P

HEADS = 16
HEAD_DIM = 72
LANES = 128
EPS = 1e-06
EXP2_SCALE = HEAD_DIM**-0.5 * math.log2(math.e)


def dot(a, b):
    return jnp.dot(a, b, preferred_element_type=jnp.float32)


def held_kernel(
    ln_ref, qg_ref, kg_ref, wqkv_ref, gains_out, member_out, spread_out, wq_out, ln, qg, kg, sems
):
    width = wq_out.shape[1]
    pairs = [(ln_ref, ln), (qg_ref, qg), (kg_ref, kg), (wqkv_ref.at[:, pl.ds(0, width)], wq_out)]
    copies = [pltpu.make_async_copy(src, dst, sems.at[i]) for i, (src, dst) in enumerate(pairs)]
    for copy in copies:
        copy.start()

    def belongs(feature, lane):
        head = jnp.where(lane >= HEADS, lane - HEADS, lane)
        first = head * HEAD_DIM
        held = (feature >= first) & (feature < first + HEAD_DIM) & (lane < 2 * HEADS)
        return held.astype(jnp.float32).astype(jnp.bfloat16)

    for out, axis in ((member_out, 0), (spread_out, 1)):
        feature = lax.broadcasted_iota(jnp.int32, out.shape, axis)
        out[...] = belongs(feature, lax.broadcasted_iota(jnp.int32, out.shape, 1 - axis))
    for copy in copies[:3]:
        copy.wait()
    gains_out[0:1, :] = ln[...].reshape(1, width)
    gains_out[1:2, :] = jnp.concatenate([qg[...].reshape(1, HEAD_DIM)] * HEADS, axis=1)
    gains_out[2:3, :] = jnp.concatenate([kg[...].reshape(1, HEAD_DIM)] * HEADS, axis=1)
    copies[3].wait()


def tokens_kernel(
    x_ref,
    gains_ref,
    member_ref,
    spread_ref,
    wq,
    wqkv_hbm,
    wout_hbm,
    o_ref,
    wkv,
    wout,
    normed,
    mixed_q,
    mixed_k,
    queries,
    queries_t,
    keys,
    values_t,
    attended_t,
    attended,
    same,
    sems,
):
    frames, positions, width = x_ref.shape
    tokens = frames * positions
    bf16, f32 = jnp.bfloat16, jnp.float32

    pairs = [
        (wqkv_hbm.at[:, pl.ds(width, width)], wkv.at[:, pl.ds(0, width)]),
        (wqkv_hbm.at[:, pl.ds(2 * width, width)], wkv.at[:, pl.ds(width, width)]),
        (wout_hbm, wout),
    ]
    copies = [pltpu.make_async_copy(src, dst, sems.at[i]) for i, (src, dst) in enumerate(pairs)]
    copies[0].start()

    gain = gains_ref[0:1, :]
    step = max(1, 16 // positions)
    for frame in range(0, frames, step):
        x = x_ref[frame : frame + step].astype(f32).reshape(step * positions, width)
        center = x - jnp.mean(x, axis=-1, keepdims=True)
        spread = jnp.mean(center * center, axis=-1, keepdims=True)
        rows = slice(frame * positions, (frame + step) * positions)
        normed[rows, :] = (center * lax.rsqrt(spread + EPS) * gain).astype(bf16)

    def head_norm(mixed, row, out):
        squares = mixed[...] * mixed[...]
        high = squares.astype(bf16)
        low = (squares - high.astype(f32)).astype(bf16)
        total = dot(jnp.concatenate([high, low], axis=0), member_ref[...])
        total = total[:tokens] + total[tokens:]
        inverse = lax.rsqrt(total * (1.0 / HEAD_DIM) + EPS)
        high = inverse.astype(bf16)
        low = (inverse - high.astype(f32)).astype(bf16)
        lane = lax.broadcasted_iota(jnp.int32, inverse.shape, 1)
        parts = jnp.where(lane < HEADS, high, low)[:, : 2 * HEADS]
        out[...] = (mixed[...] * dot(parts, spread_ref[...]) * gains_ref[row : row + 1, :]).astype(bf16)

    copies[1].start()
    mixed_q[...] = dot(normed[...], wq[...])
    head_norm(mixed_q, 1, queries)
    copies[0].wait()
    copies[2].start()
    mixed_k[...] = dot(normed[...], wkv[:, :width])
    queries_t[...] = queries[...].T
    head_norm(mixed_k, 2, keys)
    copies[1].wait()
    values_t[...] = dot(normed[...], wkv[:, width:]).astype(bf16).T

    place = lax.broadcasted_iota(jnp.int32, (tokens, tokens), 0) % positions
    other = lax.broadcasted_iota(jnp.int32, (tokens, tokens), 1) % positions
    same[...] = (place == other).astype(f32)

    row = lax.broadcasted_iota(jnp.int32, (2 * LANES, tokens), 0)
    for pair in range(HEADS // 2):
        window = slice(pair * LANES, (pair + 2) * LANES)
        begin = pair * (2 * HEAD_DIM - LANES)
        query = queries_t[window, :]
        both = [
            jnp.where((row >= begin + h * HEAD_DIM) & (row < begin + (h + 1) * HEAD_DIM), query, jnp.zeros((), bf16))
            for h in range(2)
        ]
        scores = dot(keys[:, window], jnp.concatenate(both, axis=1))
        weights = []
        for h in range(2):
            part = jnp.exp2(scores[:, h * tokens : (h + 1) * tokens] * EXP2_SCALE) * same[...]
            weights.append((part * (1.0 / jnp.sum(part, axis=0, keepdims=True))).astype(bf16))
        features = slice(pair * 2 * HEAD_DIM, (pair + 1) * 2 * HEAD_DIM)
        heads_out = dot(values_t[features, :], jnp.concatenate(weights, axis=1))
        for h in range(2):
            first = (2 * pair + h) * HEAD_DIM
            attended_t[first : first + HEAD_DIM, :] = heads_out[
                h * HEAD_DIM : (h + 1) * HEAD_DIM, h * tokens : (h + 1) * tokens
            ]
    attended[...] = attended_t[...].astype(bf16).T

    copies[2].wait()
    branch = dot(attended[...], wout[...])
    o_ref[...] = (x_ref[...].astype(f32) + branch.reshape(x_ref.shape)).astype(bf16)


def in_place_kernel(x_ref, o_ref):
    pass


def body(latent, ln_gain, q_gain, k_gain, w_qkv, w_out):
    device_count = lax.axis_size("frame")
    rows, columns, model = latent.shape
    tokens = rows * columns
    per_peer = tokens // device_count
    exchange = functools.partial(
        lax.all_to_all, axis_name="frame", split_axis=0, concat_axis=0, tiled=True
    )
    gathered = exchange(latent.reshape(device_count, per_peer, model))
    in_vmem = pl.BlockSpec(memory_space=pltpu.VMEM)
    in_hbm = pl.BlockSpec(memory_space=pltpu.HBM)
    bf16, f32 = jnp.bfloat16, jnp.float32
    held = [pltpu.with_memory_space_constraint(a, pltpu.HBM) for a in (ln_gain, q_gain, k_gain, w_qkv, w_out)]
    gains, member, spread, wq = pl.pallas_call(
        held_kernel,
        out_shape=(
            pltpu.VMEM((8, model), f32),
            pltpu.VMEM((model, LANES), bf16),
            pltpu.VMEM((2 * HEADS, model), bf16),
            pltpu.VMEM((model, model), bf16),
        ),
        in_specs=[in_hbm] * 4,
        out_specs=[in_vmem] * 4,
        scratch_shapes=[
            pltpu.VMEM((model,), f32),
            pltpu.VMEM((HEAD_DIM,), f32),
            pltpu.VMEM((HEAD_DIM,), f32),
            pltpu.SemaphoreType.DMA((4,)),
        ],
        compiler_params=pltpu.CompilerParams(vmem_limit_bytes=8 * 1024 * 1024),
        cost_estimate=pl.CostEstimate(flops=0, bytes_accessed=4 * model * model, transcendentals=0),
        name="held",
    )(*held[:4])
    result = pl.pallas_call(
        tokens_kernel,
        out_shape=jax.ShapeDtypeStruct(gathered.shape, bf16),
        in_specs=[in_vmem] * 5 + [in_hbm] * 2,
        out_specs=in_vmem,
        scratch_shapes=[
            pltpu.VMEM((model, 2 * model), bf16),
            pltpu.VMEM(w_out.shape, bf16),
            pltpu.VMEM((tokens, model), bf16),
            pltpu.VMEM((tokens, model), f32),
            pltpu.VMEM((tokens, model), f32),
            pltpu.VMEM((tokens, model), bf16),
            pltpu.VMEM((model, tokens), bf16),
            pltpu.VMEM((tokens, model), bf16),
            pltpu.VMEM((model, tokens), bf16),
            pltpu.VMEM((model, tokens), f32),
            pltpu.VMEM((tokens, model), bf16),
            pltpu.VMEM((tokens, tokens), f32),
            pltpu.SemaphoreType.DMA((3,)),
        ],
        compiler_params=pltpu.CompilerParams(vmem_limit_bytes=40 * 1024 * 1024),
        name="tokens",
    )(gathered, gains, member, spread, wq, *held[3:])
    arrived = pltpu.with_memory_space_constraint(exchange(result).reshape(latent.shape), pltpu.HBM)
    return pl.pallas_call(
        in_place_kernel,
        out_shape=pltpu.HBM(latent.shape, bf16),
        in_specs=[in_hbm],
        out_specs=in_hbm,
        input_output_aliases={0: 0},
        name="in_place",
    )(arrived)


def solution(mesh):
    placed = (P(("groups", "frame"), None, None), P(), P(), P(), P(), P())
    return jax.shard_map(
        body,
        mesh=mesh,
        in_specs=placed,
        out_specs=P(("groups", "frame"), None, None),
        check_vma=False,
    )
```

```python
import functools
import math

import jax
import jax.numpy as jnp
from jax import lax
from jax.experimental import pallas as pl
from jax.experimental.pallas import tpu as pltpu
from jax.sharding import PartitionSpec as P

HEADS = 16
HEAD_DIM = 72
LANES = 128
EPS = 1e-06
EXP2_SCALE = HEAD_DIM**-0.5 * math.log2(math.e)


def dot(a, b):
    return jnp.dot(a, b, preferred_element_type=jnp.float32)


def held_kernel(
    ln_ref, qg_ref, kg_ref, wqkv_ref, gains_out, member_out, spread_out, wq_out, ln, qg, kg, sems
):
    width = wq_out.shape[1]
    pairs = [(ln_ref, ln), (qg_ref, qg), (kg_ref, kg), (wqkv_ref.at[:, pl.ds(0, width)], wq_out)]
    copies = [pltpu.make_async_copy(src, dst, sems.at[i]) for i, (src, dst) in enumerate(pairs)]
    for copy in copies:
        copy.start()

    def belongs(feature, lane):
        head = jnp.where(lane >= HEADS, lane - HEADS, lane)
        first = head * HEAD_DIM
        held = (feature >= first) & (feature < first + HEAD_DIM) & (lane < 2 * HEADS)
        return held.astype(jnp.float32).astype(jnp.bfloat16)

    for out, axis in ((member_out, 0), (spread_out, 1)):
        feature = lax.broadcasted_iota(jnp.int32, out.shape, axis)
        out[...] = belongs(feature, lax.broadcasted_iota(jnp.int32, out.shape, 1 - axis))
    for copy in copies[:3]:
        copy.wait()
    gains_out[0:1, :] = ln[...].reshape(1, width)
    gains_out[1:2, :] = jnp.concatenate([qg[...].reshape(1, HEAD_DIM)] * HEADS, axis=1)
    gains_out[2:3, :] = jnp.concatenate([kg[...].reshape(1, HEAD_DIM)] * HEADS, axis=1)
    copies[3].wait()


def tokens_kernel(
    x_ref,
    gains_ref,
    member_ref,
    spread_ref,
    wq,
    wqkv_hbm,
    wout_hbm,
    o_ref,
    wkv,
    wout,
    normed,
    mixed_q,
    mixed_k,
    queries,
    queries_t,
    keys,
    values_t,
    attended_t,
    attended,
    same,
    sems,
):
    frames, positions, width = x_ref.shape
    tokens = frames * positions
    bf16, f32 = jnp.bfloat16, jnp.float32

    cut = (width // LANES + 1) // 2 * LANES
    bounds = [(0, cut), (cut, width), (width, 2 * width)]
    pairs = [(wqkv_hbm.at[:, pl.ds(width + a, b - a)], wkv.at[:, pl.ds(a, b - a)]) for a, b in bounds]
    pairs += [(wout_hbm, wout)]
    copies = [pltpu.make_async_copy(src, dst, sems.at[i]) for i, (src, dst) in enumerate(pairs)]
    copies[0].start()

    gain = gains_ref[0:1, :]
    step = max(1, 16 // positions)
    for frame in range(0, frames, step):
        x = x_ref[frame : frame + step].astype(f32).reshape(step * positions, width)
        center = x - jnp.mean(x, axis=-1, keepdims=True)
        spread = jnp.mean(center * center, axis=-1, keepdims=True)
        rows = slice(frame * positions, (frame + step) * positions)
        normed[rows, :] = (center * lax.rsqrt(spread + EPS) * gain).astype(bf16)

    def head_norm(mixed, row, out):
        squares = mixed[...] * mixed[...]
        high = squares.astype(bf16)
        low = (squares - high.astype(f32)).astype(bf16)
        total = dot(jnp.concatenate([high, low], axis=0), member_ref[...])
        total = total[:tokens] + total[tokens:]
        inverse = lax.rsqrt(total * (1.0 / HEAD_DIM) + EPS)
        high = inverse.astype(bf16)
        low = (inverse - high.astype(f32)).astype(bf16)
        lane = lax.broadcasted_iota(jnp.int32, inverse.shape, 1)
        parts = jnp.where(lane < HEADS, high, low)[:, : 2 * HEADS]
        out[...] = (mixed[...] * dot(parts, spread_ref[...]) * gains_ref[row : row + 1, :]).astype(bf16)

    copies[1].start()
    mixed_q[...] = dot(normed[...], wq[...])
    copies[0].wait()
    copies[2].start()
    mixed_k[:, :cut] = dot(normed[...], wkv[:, :cut])
    head_norm(mixed_q, 1, queries)
    copies[1].wait()
    copies[3].start()
    mixed_k[:, cut:] = dot(normed[...], wkv[:, cut:width])
    queries_t[...] = queries[...].T
    copies[2].wait()
    values_t[...] = dot(normed[...], wkv[:, width:]).astype(bf16).T
    head_norm(mixed_k, 2, keys)

    place = lax.broadcasted_iota(jnp.int32, (tokens, tokens), 0) % positions
    other = lax.broadcasted_iota(jnp.int32, (tokens, tokens), 1) % positions
    same[...] = (place == other).astype(f32)

    row = lax.broadcasted_iota(jnp.int32, (2 * LANES, tokens), 0)
    for pair in range(HEADS // 2):
        window = slice(pair * LANES, (pair + 2) * LANES)
        begin = pair * (2 * HEAD_DIM - LANES)
        query = queries_t[window, :]
        both = [
            jnp.where((row >= begin + h * HEAD_DIM) & (row < begin + (h + 1) * HEAD_DIM), query, jnp.zeros((), bf16))
            for h in range(2)
        ]
        scores = dot(keys[:, window], jnp.concatenate(both, axis=1))
        weights = []
        for h in range(2):
            part = jnp.exp2(scores[:, h * tokens : (h + 1) * tokens] * EXP2_SCALE) * same[...]
            weights.append((part * (1.0 / jnp.sum(part, axis=0, keepdims=True))).astype(bf16))
        features = slice(pair * 2 * HEAD_DIM, (pair + 1) * 2 * HEAD_DIM)
        heads_out = dot(values_t[features, :], jnp.concatenate(weights, axis=1))
        for h in range(2):
            first = (2 * pair + h) * HEAD_DIM
            attended_t[first : first + HEAD_DIM, :] = heads_out[
                h * HEAD_DIM : (h + 1) * HEAD_DIM, h * tokens : (h + 1) * tokens
            ]
    attended[...] = attended_t[...].astype(bf16).T

    copies[3].wait()
    branch = dot(attended[...], wout[...])
    o_ref[...] = (x_ref[...].astype(f32) + branch.reshape(x_ref.shape)).astype(bf16)


def body(latent, ln_gain, q_gain, k_gain, w_qkv, w_out):
    device_count = lax.axis_size("frame")
    rows, columns, model = latent.shape
    tokens = rows * columns
    per_peer = tokens // device_count
    exchange = functools.partial(
        lax.all_to_all, axis_name="frame", split_axis=0, concat_axis=0, tiled=True
    )
    gathered = exchange(latent.reshape(device_count, per_peer, model))
    in_vmem = pl.BlockSpec(memory_space=pltpu.VMEM)
    in_hbm = pl.BlockSpec(memory_space=pltpu.HBM)
    bf16, f32 = jnp.bfloat16, jnp.float32
    held = [pltpu.with_memory_space_constraint(a, pltpu.HBM) for a in (ln_gain, q_gain, k_gain, w_qkv, w_out)]
    gains, member, spread, wq = pl.pallas_call(
        held_kernel,
        out_shape=(
            pltpu.VMEM((8, model), f32),
            pltpu.VMEM((model, LANES), bf16),
            pltpu.VMEM((2 * HEADS, model), bf16),
            pltpu.VMEM((model, model), bf16),
        ),
        in_specs=[in_hbm] * 4,
        out_specs=[in_vmem] * 4,
        scratch_shapes=[
            pltpu.VMEM((model,), f32),
            pltpu.VMEM((HEAD_DIM,), f32),
            pltpu.VMEM((HEAD_DIM,), f32),
            pltpu.SemaphoreType.DMA((4,)),
        ],
        compiler_params=pltpu.CompilerParams(vmem_limit_bytes=8 * 1024 * 1024),
        cost_estimate=pl.CostEstimate(flops=0, bytes_accessed=4 * model * model, transcendentals=0),
        name="held",
    )(*held[:4])
    result = pl.pallas_call(
        tokens_kernel,
        out_shape=jax.ShapeDtypeStruct(gathered.shape, bf16),
        in_specs=[in_vmem] * 5 + [in_hbm] * 2,
        out_specs=in_vmem,
        scratch_shapes=[
            pltpu.VMEM((model, 2 * model), bf16),
            pltpu.VMEM(w_out.shape, bf16),
            pltpu.VMEM((tokens, model), bf16),
            pltpu.VMEM((tokens, model), f32),
            pltpu.VMEM((tokens, model), f32),
            pltpu.VMEM((tokens, model), bf16),
            pltpu.VMEM((model, tokens), bf16),
            pltpu.VMEM((tokens, model), bf16),
            pltpu.VMEM((model, tokens), bf16),
            pltpu.VMEM((model, tokens), f32),
            pltpu.VMEM((tokens, model), bf16),
            pltpu.VMEM((tokens, tokens), f32),
            pltpu.SemaphoreType.DMA((4,)),
        ],
        compiler_params=pltpu.CompilerParams(vmem_limit_bytes=40 * 1024 * 1024),
        name="tokens",
    )(gathered, gains, member, spread, wq, *held[3:])
    return exchange(result).reshape(latent.shape)


def solution(mesh):
    placed = (P(("groups", "frame"), None, None), P(), P(), P(), P(), P())
    return jax.shard_map(
        body,
        mesh=mesh,
        in_specs=placed,
        out_specs=P(("groups", "frame"), None, None),
        check_vma=False,
    )
```

```python
import functools
import math

import jax
import jax.numpy as jnp
from jax import lax
from jax.experimental import pallas as pl
from jax.experimental.pallas import tpu as pltpu
from jax.sharding import PartitionSpec as P

HEADS = 16
HEAD_DIM = 72
LANES = 128
EPS = 1e-06
EXP2_SCALE = HEAD_DIM**-0.5 * math.log2(math.e)


def dot(a, b):
    return jnp.dot(a, b, preferred_element_type=jnp.float32)


def held_kernel(
    ln_ref, qg_ref, kg_ref, wqkv_ref, gains_out, member_out, spread_out, wq_out, ln, qg, kg, sems
):
    width = wq_out.shape[1]
    pairs = [(ln_ref, ln), (qg_ref, qg), (kg_ref, kg), (wqkv_ref.at[:, pl.ds(0, width)], wq_out)]
    copies = [pltpu.make_async_copy(src, dst, sems.at[i]) for i, (src, dst) in enumerate(pairs)]
    for copy in copies:
        copy.start()

    def belongs(feature, lane):
        head = jnp.where(lane >= HEADS, lane - HEADS, lane)
        first = head * HEAD_DIM
        held = (feature >= first) & (feature < first + HEAD_DIM) & (lane < 2 * HEADS)
        return held.astype(jnp.float32).astype(jnp.bfloat16)

    for out, axis in ((member_out, 0), (spread_out, 1)):
        feature = lax.broadcasted_iota(jnp.int32, out.shape, axis)
        out[...] = belongs(feature, lax.broadcasted_iota(jnp.int32, out.shape, 1 - axis))
    for copy in copies[:3]:
        copy.wait()
    gains_out[0:1, :] = ln[...].reshape(1, width)
    gains_out[1:2, :] = jnp.concatenate([qg[...].reshape(1, HEAD_DIM)] * HEADS, axis=1)
    gains_out[2:3, :] = jnp.concatenate([kg[...].reshape(1, HEAD_DIM)] * HEADS, axis=1)
    copies[3].wait()


def tokens_kernel(
    x_ref,
    gains_ref,
    member_ref,
    spread_ref,
    wq,
    wqkv_hbm,
    wout_hbm,
    o_ref,
    wkv,
    wout,
    normed,
    mixed_q,
    mixed_k,
    queries,
    queries_t,
    keys,
    values_t,
    attended_t,
    attended,
    same,
    stacks,
    weights,
    sems,
):
    frames, positions, width = x_ref.shape
    tokens = frames * positions
    bf16, f32 = jnp.bfloat16, jnp.float32

    pairs = [
        (wqkv_hbm.at[:, pl.ds(width, width)], wkv.at[:, pl.ds(0, width)]),
        (wqkv_hbm.at[:, pl.ds(2 * width, width)], wkv.at[:, pl.ds(width, width)]),
        (wout_hbm, wout),
    ]
    copies = [pltpu.make_async_copy(src, dst, sems.at[i]) for i, (src, dst) in enumerate(pairs)]
    copies[0].start()

    gain = gains_ref[0:1, :]
    step = max(1, 16 // positions)
    for frame in range(0, frames, step):
        x = x_ref[frame : frame + step].astype(f32).reshape(step * positions, width)
        center = x - jnp.mean(x, axis=-1, keepdims=True)
        spread = jnp.mean(center * center, axis=-1, keepdims=True)
        rows = slice(frame * positions, (frame + step) * positions)
        normed[rows, :] = (center * lax.rsqrt(spread + EPS) * gain).astype(bf16)

    def head_norm(mixed, row, out):
        squares = mixed[...] * mixed[...]
        high = squares.astype(bf16)
        low = (squares - high.astype(f32)).astype(bf16)
        total = dot(jnp.concatenate([high, low], axis=0), member_ref[...])
        total = total[:tokens] + total[tokens:]
        inverse = lax.rsqrt(total * (1.0 / HEAD_DIM) + EPS)
        high = inverse.astype(bf16)
        low = (inverse - high.astype(f32)).astype(bf16)
        lane = lax.broadcasted_iota(jnp.int32, inverse.shape, 1)
        parts = jnp.where(lane < HEADS, high, low)[:, : 2 * HEADS]
        out[...] = (mixed[...] * dot(parts, spread_ref[...]) * gains_ref[row : row + 1, :]).astype(bf16)

    copies[1].start()
    mixed_q[...] = dot(normed[...], wq[...])
    head_norm(mixed_q, 1, queries)
    queries_t[...] = queries[...].T

    row = lax.broadcasted_iota(jnp.int32, (2 * LANES, tokens), 0)
    for pair in range(HEADS // 2):
        begin = pair * (2 * HEAD_DIM - LANES)
        query = queries_t[pair * LANES : (pair + 2) * LANES, :]
        for h in range(2):
            mine = (row >= begin + h * HEAD_DIM) & (row < begin + (h + 1) * HEAD_DIM)
            stacks[pair, :, h * tokens : (h + 1) * tokens] = jnp.where(mine, query, jnp.zeros((), bf16))

    place = lax.broadcasted_iota(jnp.int32, (tokens, tokens), 0) % positions
    other = lax.broadcasted_iota(jnp.int32, (tokens, tokens), 1) % positions
    same[...] = (place == other).astype(f32)

    copies[0].wait()
    copies[2].start()
    mixed_k[...] = dot(normed[...], wkv[:, :width])
    head_norm(mixed_k, 2, keys)

    for pair in range(HEADS // 2):
        scores = dot(keys[:, pair * LANES : (pair + 2) * LANES], stacks[pair])
        for h in range(2):
            lanes = slice(h * tokens, (h + 1) * tokens)
            part = jnp.exp2(scores[:, lanes] * EXP2_SCALE) * same[...]
            weights[pair, :, lanes] = (part * (1.0 / jnp.sum(part, axis=0, keepdims=True))).astype(bf16)

    copies[1].wait()
    values_t[...] = dot(normed[...], wkv[:, width:]).astype(bf16).T
    for pair in range(HEADS // 2):
        heads_out = dot(values_t[pair * 2 * HEAD_DIM : (pair + 1) * 2 * HEAD_DIM, :], weights[pair])
        for h in range(2):
            first = (2 * pair + h) * HEAD_DIM
            attended_t[first : first + HEAD_DIM, :] = heads_out[
                h * HEAD_DIM : (h + 1) * HEAD_DIM, h * tokens : (h + 1) * tokens
            ]
    attended[...] = attended_t[...].astype(bf16).T

    copies[2].wait()
    branch = dot(attended[...], wout[...])
    o_ref[...] = (x_ref[...].astype(f32) + branch.reshape(x_ref.shape)).astype(bf16)


def body(latent, ln_gain, q_gain, k_gain, w_qkv, w_out):
    device_count = lax.axis_size("frame")
    rows, columns, model = latent.shape
    tokens = rows * columns
    per_peer = tokens // device_count
    exchange = functools.partial(
        lax.all_to_all, axis_name="frame", split_axis=0, concat_axis=0, tiled=True
    )
    gathered = exchange(latent.reshape(device_count, per_peer, model))
    in_vmem = pl.BlockSpec(memory_space=pltpu.VMEM)
    in_hbm = pl.BlockSpec(memory_space=pltpu.HBM)
    bf16, f32 = jnp.bfloat16, jnp.float32
    held = [pltpu.with_memory_space_constraint(a, pltpu.HBM) for a in (ln_gain, q_gain, k_gain, w_qkv, w_out)]
    gains, member, spread, wq = pl.pallas_call(
        held_kernel,
        out_shape=(
            pltpu.VMEM((8, model), f32),
            pltpu.VMEM((model, LANES), bf16),
            pltpu.VMEM((2 * HEADS, model), bf16),
            pltpu.VMEM((model, model), bf16),
        ),
        in_specs=[in_hbm] * 4,
        out_specs=[in_vmem] * 4,
        scratch_shapes=[
            pltpu.VMEM((model,), f32),
            pltpu.VMEM((HEAD_DIM,), f32),
            pltpu.VMEM((HEAD_DIM,), f32),
            pltpu.SemaphoreType.DMA((4,)),
        ],
        compiler_params=pltpu.CompilerParams(vmem_limit_bytes=8 * 1024 * 1024),
        cost_estimate=pl.CostEstimate(flops=0, bytes_accessed=4 * model * model, transcendentals=0),
        name="held",
    )(*held[:4])
    result = pl.pallas_call(
        tokens_kernel,
        out_shape=jax.ShapeDtypeStruct(gathered.shape, bf16),
        in_specs=[in_vmem] * 5 + [in_hbm] * 2,
        out_specs=in_vmem,
        scratch_shapes=[
            pltpu.VMEM((model, 2 * model), bf16),
            pltpu.VMEM(w_out.shape, bf16),
            pltpu.VMEM((tokens, model), bf16),
            pltpu.VMEM((tokens, model), f32),
            pltpu.VMEM((tokens, model), f32),
            pltpu.VMEM((tokens, model), bf16),
            pltpu.VMEM((model, tokens), bf16),
            pltpu.VMEM((tokens, model), bf16),
            pltpu.VMEM((model, tokens), bf16),
            pltpu.VMEM((model, tokens), f32),
            pltpu.VMEM((tokens, model), bf16),
            pltpu.VMEM((tokens, tokens), f32),
            pltpu.VMEM((HEADS // 2, 2 * LANES, 2 * tokens), bf16),
            pltpu.VMEM((HEADS // 2, tokens, 2 * tokens), bf16),
            pltpu.SemaphoreType.DMA((3,)),
        ],
        compiler_params=pltpu.CompilerParams(vmem_limit_bytes=40 * 1024 * 1024),
        name="tokens",
    )(gathered, gains, member, spread, wq, *held[3:])
    return exchange(result).reshape(latent.shape)


def solution(mesh):
    placed = (P(("groups", "frame"), None, None), P(), P(), P(), P(), P())
    return jax.shard_map(
        body,
        mesh=mesh,
        in_specs=placed,
        out_specs=P(("groups", "frame"), None, None),
        check_vma=False,
    )
```

```python
import functools
import math

import jax
import jax.numpy as jnp
from jax import lax
from jax.experimental import pallas as pl
from jax.experimental.pallas import tpu as pltpu
from jax.sharding import PartitionSpec as P

HEADS = 16
HEAD_DIM = 72
LANES = 128
EPS = 1e-06
EXP2_SCALE = HEAD_DIM**-0.5 * math.log2(math.e)


def dot(a, b):
    return jnp.dot(a, b, preferred_element_type=jnp.float32)


def held_kernel(
    ln_ref, qg_ref, kg_ref, wqkv_ref, gains_out, columns_out, member_out, spread_out, wq_out, ln, qg, kg, sems
):
    width = wq_out.shape[1]
    pairs = [(ln_ref, ln), (qg_ref, qg), (kg_ref, kg), (wqkv_ref.at[:, pl.ds(0, width)], wq_out)]
    copies = [pltpu.make_async_copy(src, dst, sems.at[i]) for i, (src, dst) in enumerate(pairs)]
    for copy in copies:
        copy.start()

    def belongs(feature, lane):
        head = jnp.where(lane >= HEADS, lane - HEADS, lane)
        first = head * HEAD_DIM
        held = (feature >= first) & (feature < first + HEAD_DIM) & (lane < 2 * HEADS)
        return held.astype(jnp.float32).astype(jnp.bfloat16)

    for out, axis in ((member_out, 0), (spread_out, 1)):
        feature = lax.broadcasted_iota(jnp.int32, out.shape, axis)
        out[...] = belongs(feature, lax.broadcasted_iota(jnp.int32, out.shape, 1 - axis))
    for copy in copies[:3]:
        copy.wait()
    gains_out[0:1, :] = ln[...].reshape(1, width)
    row = jnp.concatenate([qg[...].reshape(1, HEAD_DIM), jnp.zeros((1, LANES - HEAD_DIM), jnp.float32)], axis=1)
    columns_out[...] = jnp.broadcast_to(row, (LANES, LANES)).T[:HEAD_DIM]
    gains_out[1:2, :] = jnp.concatenate([kg[...].reshape(1, HEAD_DIM)] * HEADS, axis=1)
    copies[3].wait()


def tokens_kernel(
    x_ref,
    gains_ref,
    columns_ref,
    member_ref,
    spread_ref,
    wq,
    wqkv_hbm,
    wout_hbm,
    o_ref,
    wkv,
    wout,
    normed,
    mixed_q,
    mixed_k,
    queries_t,
    keys,
    values_t,
    attended_t,
    attended,
    same,
    sems,
):
    frames, positions, width = x_ref.shape
    tokens = frames * positions
    bf16, f32 = jnp.bfloat16, jnp.float32

    pairs = [
        (wqkv_hbm.at[:, pl.ds(width, width)], wkv.at[:, pl.ds(0, width)]),
        (wqkv_hbm.at[:, pl.ds(2 * width, width)], wkv.at[:, pl.ds(width, width)]),
        (wout_hbm, wout),
    ]
    copies = [pltpu.make_async_copy(src, dst, sems.at[i]) for i, (src, dst) in enumerate(pairs)]
    copies[0].start()

    gain = gains_ref[0:1, :]
    step = max(1, 16 // positions)
    for frame in range(0, frames, step):
        x = x_ref[frame : frame + step].astype(f32).reshape(step * positions, width)
        center = x - jnp.mean(x, axis=-1, keepdims=True)
        spread = jnp.mean(center * center, axis=-1, keepdims=True)
        rows = slice(frame * positions, (frame + step) * positions)
        normed[rows, :] = (center * lax.rsqrt(spread + EPS) * gain).astype(bf16)

    def head_norm(mixed, row, out):
        squares = mixed[...] * mixed[...]
        high = squares.astype(bf16)
        low = (squares - high.astype(f32)).astype(bf16)
        total = dot(jnp.concatenate([high, low], axis=0), member_ref[...])
        total = total[:tokens] + total[tokens:]
        inverse = lax.rsqrt(total * (1.0 / HEAD_DIM) + EPS)
        high = inverse.astype(bf16)
        low = (inverse - high.astype(f32)).astype(bf16)
        lane = lax.broadcasted_iota(jnp.int32, inverse.shape, 1)
        parts = jnp.where(lane < HEADS, high, low)[:, : 2 * HEADS]
        out[...] = (mixed[...] * dot(parts, spread_ref[...]) * gains_ref[row : row + 1, :]).astype(bf16)

    copies[1].start()
    mixed_q[...] = dot(normed[...], wq[...]).T
    for pair in range(HEADS // 2):
        heads = []
        for first in (2 * pair * HEAD_DIM, (2 * pair + 1) * HEAD_DIM):
            head = mixed_q[first : first + HEAD_DIM, :]
            total = jnp.sum(head * head, axis=0, keepdims=True)
            heads.append(head * lax.rsqrt(total * (1.0 / HEAD_DIM) + EPS) * columns_ref[...])
        rows = slice(2 * pair * HEAD_DIM, (2 * pair + 2) * HEAD_DIM)
        queries_t[rows, :] = jnp.concatenate(heads, axis=0).astype(bf16)
    copies[0].wait()
    copies[2].start()
    mixed_k[...] = dot(normed[...], wkv[:, :width])
    head_norm(mixed_k, 1, keys)
    copies[1].wait()
    values_t[...] = dot(normed[...], wkv[:, width:]).astype(bf16).T

    place = lax.broadcasted_iota(jnp.int32, (tokens, tokens), 0) % positions
    other = lax.broadcasted_iota(jnp.int32, (tokens, tokens), 1) % positions
    same[...] = (place == other).astype(f32)

    row = lax.broadcasted_iota(jnp.int32, (2 * LANES, tokens), 0)
    for pair in range(HEADS // 2):
        window = slice(pair * LANES, (pair + 2) * LANES)
        begin = pair * (2 * HEAD_DIM - LANES)
        query = queries_t[window, :]
        both = [
            jnp.where((row >= begin + h * HEAD_DIM) & (row < begin + (h + 1) * HEAD_DIM), query, jnp.zeros((), bf16))
            for h in range(2)
        ]
        scores = dot(keys[:, window], jnp.concatenate(both, axis=1))
        weights = []
        for h in range(2):
            part = jnp.exp2(scores[:, h * tokens : (h + 1) * tokens] * EXP2_SCALE) * same[...]
            weights.append((part * (1.0 / jnp.sum(part, axis=0, keepdims=True))).astype(bf16))
        features = slice(pair * 2 * HEAD_DIM, (pair + 1) * 2 * HEAD_DIM)
        heads_out = dot(values_t[features, :], jnp.concatenate(weights, axis=1))
        for h in range(2):
            first = (2 * pair + h) * HEAD_DIM
            attended_t[first : first + HEAD_DIM, :] = heads_out[
                h * HEAD_DIM : (h + 1) * HEAD_DIM, h * tokens : (h + 1) * tokens
            ]
    attended[...] = attended_t[...].astype(bf16).T

    copies[2].wait()
    branch = dot(attended[...], wout[...])
    o_ref[...] = (x_ref[...].astype(f32) + branch.reshape(x_ref.shape)).astype(bf16)


def body(latent, ln_gain, q_gain, k_gain, w_qkv, w_out):
    device_count = lax.axis_size("frame")
    rows, columns, model = latent.shape
    tokens = rows * columns
    per_peer = tokens // device_count
    exchange = functools.partial(
        lax.all_to_all, axis_name="frame", split_axis=0, concat_axis=0, tiled=True
    )
    gathered = exchange(latent.reshape(device_count, per_peer, model))
    in_vmem = pl.BlockSpec(memory_space=pltpu.VMEM)
    in_hbm = pl.BlockSpec(memory_space=pltpu.HBM)
    bf16, f32 = jnp.bfloat16, jnp.float32
    held = [pltpu.with_memory_space_constraint(a, pltpu.HBM) for a in (ln_gain, q_gain, k_gain, w_qkv, w_out)]
    gains, columns, member, spread, wq = pl.pallas_call(
        held_kernel,
        out_shape=(
            pltpu.VMEM((8, model), f32),
            pltpu.VMEM((HEAD_DIM, LANES), f32),
            pltpu.VMEM((model, LANES), bf16),
            pltpu.VMEM((2 * HEADS, model), bf16),
            pltpu.VMEM((model, model), bf16),
        ),
        in_specs=[in_hbm] * 4,
        out_specs=[in_vmem] * 5,
        scratch_shapes=[
            pltpu.VMEM((model,), f32),
            pltpu.VMEM((HEAD_DIM,), f32),
            pltpu.VMEM((HEAD_DIM,), f32),
            pltpu.SemaphoreType.DMA((4,)),
        ],
        compiler_params=pltpu.CompilerParams(vmem_limit_bytes=8 * 1024 * 1024),
        cost_estimate=pl.CostEstimate(flops=0, bytes_accessed=4 * model * model, transcendentals=0),
        name="held",
    )(*held[:4])
    result = pl.pallas_call(
        tokens_kernel,
        out_shape=jax.ShapeDtypeStruct(gathered.shape, bf16),
        in_specs=[in_vmem] * 6 + [in_hbm] * 2,
        out_specs=in_vmem,
        scratch_shapes=[
            pltpu.VMEM((model, 2 * model), bf16),
            pltpu.VMEM(w_out.shape, bf16),
            pltpu.VMEM((tokens, model), bf16),
            pltpu.VMEM((model, tokens), f32),
            pltpu.VMEM((tokens, model), f32),
            pltpu.VMEM((model, tokens), bf16),
            pltpu.VMEM((tokens, model), bf16),
            pltpu.VMEM((model, tokens), bf16),
            pltpu.VMEM((model, tokens), f32),
            pltpu.VMEM((tokens, model), bf16),
            pltpu.VMEM((tokens, tokens), f32),
            pltpu.SemaphoreType.DMA((3,)),
        ],
        compiler_params=pltpu.CompilerParams(vmem_limit_bytes=40 * 1024 * 1024),
        name="tokens",
    )(gathered, gains, columns, member, spread, wq, *held[3:])
    return exchange(result).reshape(latent.shape)


def solution(mesh):
    placed = (P(("groups", "frame"), None, None), P(), P(), P(), P(), P())
    return jax.shard_map(
        body,
        mesh=mesh,
        in_specs=placed,
        out_specs=P(("groups", "frame"), None, None),
        check_vma=False,
    )
```

```python
import functools
import math

import jax
import jax.numpy as jnp
from jax import lax
from jax.experimental import pallas as pl
from jax.experimental.pallas import tpu as pltpu
from jax.sharding import PartitionSpec as P

HEADS = 16
HEAD_DIM = 72
LANES = 128
EPS = 1e-06
EXP2_SCALE = HEAD_DIM**-0.5 * math.log2(math.e)


def dot(a, b):
    return jnp.dot(a, b, preferred_element_type=jnp.float32)


def held_kernel(
    ln_ref, qg_ref, kg_ref, wqkv_ref, gains_out, columns_out, member_out, spread_out, wq_out, ln, qg, kg, sems
):
    width = wq_out.shape[1]
    pairs = [(ln_ref, ln), (qg_ref, qg), (kg_ref, kg), (wqkv_ref.at[:, pl.ds(0, width)], wq_out)]
    copies = [pltpu.make_async_copy(src, dst, sems.at[i]) for i, (src, dst) in enumerate(pairs)]
    for copy in copies:
        copy.start()

    def belongs(feature, lane):
        head = jnp.where(lane >= HEADS, lane - HEADS, lane)
        first = head * HEAD_DIM
        held = (feature >= first) & (feature < first + HEAD_DIM) & (lane < 2 * HEADS)
        return held.astype(jnp.float32).astype(jnp.bfloat16)

    for out, axis in ((member_out, 0), (spread_out, 1)):
        feature = lax.broadcasted_iota(jnp.int32, out.shape, axis)
        out[...] = belongs(feature, lax.broadcasted_iota(jnp.int32, out.shape, 1 - axis))
    for copy in copies[:3]:
        copy.wait()
    gains_out[0:1, :] = ln[...].reshape(1, width)
    row = jnp.concatenate([qg[...].reshape(1, HEAD_DIM), jnp.zeros((1, LANES - HEAD_DIM), jnp.float32)], axis=1)
    columns_out[...] = jnp.broadcast_to(row, (LANES, LANES)).T[:HEAD_DIM]
    gains_out[1:2, :] = jnp.concatenate([kg[...].reshape(1, HEAD_DIM)] * HEADS, axis=1)
    copies[3].wait()


def tokens_kernel(
    x_ref,
    gains_ref,
    columns_ref,
    member_ref,
    spread_ref,
    wq,
    wqkv_hbm,
    wout_hbm,
    o_ref,
    wkv,
    wout,
    normed,
    mixed_q,
    mixed_k,
    queries_t,
    keys,
    values_t,
    attended_t,
    attended,
    same,
    sems,
):
    frames, positions, width = x_ref.shape
    tokens = frames * positions
    bf16, f32 = jnp.bfloat16, jnp.float32

    blocks = 4
    depth = width // blocks
    parts = [
        (wqkv_hbm.at[:, pl.ds(width, width)], wkv.at[:, pl.ds(0, width)]),
        (wqkv_hbm.at[:, pl.ds(2 * width, width)], wkv.at[:, pl.ds(width, width)]),
        (wout_hbm, wout),
    ]

    def copies_of(part):
        src, dst = parts[part]
        return [
            pltpu.make_async_copy(
                src.at[pl.ds(i * depth, depth)], dst.at[pl.ds(i * depth, depth)], sems.at[part, i]
            )
            for i in range(blocks)
        ]

    copies = [copies_of(part) for part in range(len(parts))]

    def start(part):
        for copy in copies[part]:
            copy.start()

    def wait(part):
        for copy in copies[part]:
            copy.wait()

    start(0)

    gain = gains_ref[0:1, :]
    step = max(1, 16 // positions)
    for frame in range(0, frames, step):
        x = x_ref[frame : frame + step].astype(f32).reshape(step * positions, width)
        center = x - jnp.mean(x, axis=-1, keepdims=True)
        spread = jnp.mean(center * center, axis=-1, keepdims=True)
        rows = slice(frame * positions, (frame + step) * positions)
        normed[rows, :] = (center * lax.rsqrt(spread + EPS) * gain).astype(bf16)

    def head_norm(mixed, row, out):
        squares = mixed[...] * mixed[...]
        high = squares.astype(bf16)
        low = (squares - high.astype(f32)).astype(bf16)
        total = dot(jnp.concatenate([high, low], axis=0), member_ref[...])
        total = total[:tokens] + total[tokens:]
        inverse = lax.rsqrt(total * (1.0 / HEAD_DIM) + EPS)
        high = inverse.astype(bf16)
        low = (inverse - high.astype(f32)).astype(bf16)
        lane = lax.broadcasted_iota(jnp.int32, inverse.shape, 1)
        parts = jnp.where(lane < HEADS, high, low)[:, : 2 * HEADS]
        out[...] = (mixed[...] * dot(parts, spread_ref[...]) * gains_ref[row : row + 1, :]).astype(bf16)

    start(1)
    mixed_q[...] = dot(normed[...], wq[...]).T
    for pair in range(HEADS // 2):
        heads = []
        for first in (2 * pair * HEAD_DIM, (2 * pair + 1) * HEAD_DIM):
            head = mixed_q[first : first + HEAD_DIM, :]
            total = jnp.sum(head * head, axis=0, keepdims=True)
            heads.append(head * lax.rsqrt(total * (1.0 / HEAD_DIM) + EPS) * columns_ref[...])
        rows = slice(2 * pair * HEAD_DIM, (2 * pair + 2) * HEAD_DIM)
        queries_t[rows, :] = jnp.concatenate(heads, axis=0).astype(bf16)
    wait(0)
    start(2)
    mixed_k[...] = dot(normed[...], wkv[:, :width])
    head_norm(mixed_k, 1, keys)
    wait(1)
    values_t[...] = dot(normed[...], wkv[:, width:]).astype(bf16).T

    place = lax.broadcasted_iota(jnp.int32, (tokens, tokens), 0) % positions
    other = lax.broadcasted_iota(jnp.int32, (tokens, tokens), 1) % positions
    same[...] = (place == other).astype(f32)

    row = lax.broadcasted_iota(jnp.int32, (2 * LANES, tokens), 0)
    for pair in range(HEADS // 2):
        window = slice(pair * LANES, (pair + 2) * LANES)
        begin = pair * (2 * HEAD_DIM - LANES)
        query = queries_t[window, :]
        both = [
            jnp.where((row >= begin + h * HEAD_DIM) & (row < begin + (h + 1) * HEAD_DIM), query, jnp.zeros((), bf16))
            for h in range(2)
        ]
        scores = dot(keys[:, window], jnp.concatenate(both, axis=1))
        weights = []
        for h in range(2):
            part = jnp.exp2(scores[:, h * tokens : (h + 1) * tokens] * EXP2_SCALE) * same[...]
            weights.append((part * (1.0 / jnp.sum(part, axis=0, keepdims=True))).astype(bf16))
        features = slice(pair * 2 * HEAD_DIM, (pair + 1) * 2 * HEAD_DIM)
        heads_out = dot(values_t[features, :], jnp.concatenate(weights, axis=1))
        for h in range(2):
            first = (2 * pair + h) * HEAD_DIM
            attended_t[first : first + HEAD_DIM, :] = heads_out[
                h * HEAD_DIM : (h + 1) * HEAD_DIM, h * tokens : (h + 1) * tokens
            ]
    attended[...] = attended_t[...].astype(bf16).T

    wait(2)
    branch = dot(attended[...], wout[...])
    o_ref[...] = (x_ref[...].astype(f32) + branch.reshape(x_ref.shape)).astype(bf16)


def body(latent, ln_gain, q_gain, k_gain, w_qkv, w_out):
    device_count = lax.axis_size("frame")
    rows, columns, model = latent.shape
    tokens = rows * columns
    per_peer = tokens // device_count
    exchange = functools.partial(
        lax.all_to_all, axis_name="frame", split_axis=0, concat_axis=0, tiled=True
    )
    gathered = exchange(latent.reshape(device_count, per_peer, model))
    in_vmem = pl.BlockSpec(memory_space=pltpu.VMEM)
    in_hbm = pl.BlockSpec(memory_space=pltpu.HBM)
    bf16, f32 = jnp.bfloat16, jnp.float32
    held = [pltpu.with_memory_space_constraint(a, pltpu.HBM) for a in (ln_gain, q_gain, k_gain, w_qkv, w_out)]
    gains, columns, member, spread, wq = pl.pallas_call(
        held_kernel,
        out_shape=(
            pltpu.VMEM((8, model), f32),
            pltpu.VMEM((HEAD_DIM, LANES), f32),
            pltpu.VMEM((model, LANES), bf16),
            pltpu.VMEM((2 * HEADS, model), bf16),
            pltpu.VMEM((model, model), bf16),
        ),
        in_specs=[in_hbm] * 4,
        out_specs=[in_vmem] * 5,
        scratch_shapes=[
            pltpu.VMEM((model,), f32),
            pltpu.VMEM((HEAD_DIM,), f32),
            pltpu.VMEM((HEAD_DIM,), f32),
            pltpu.SemaphoreType.DMA((4,)),
        ],
        compiler_params=pltpu.CompilerParams(vmem_limit_bytes=8 * 1024 * 1024),
        cost_estimate=pl.CostEstimate(flops=0, bytes_accessed=4 * model * model, transcendentals=0),
        name="held",
    )(*held[:4])
    result = pl.pallas_call(
        tokens_kernel,
        out_shape=jax.ShapeDtypeStruct(gathered.shape, bf16),
        in_specs=[in_vmem] * 6 + [in_hbm] * 2,
        out_specs=in_vmem,
        scratch_shapes=[
            pltpu.VMEM((model, 2 * model), bf16),
            pltpu.VMEM(w_out.shape, bf16),
            pltpu.VMEM((tokens, model), bf16),
            pltpu.VMEM((model, tokens), f32),
            pltpu.VMEM((tokens, model), f32),
            pltpu.VMEM((model, tokens), bf16),
            pltpu.VMEM((tokens, model), bf16),
            pltpu.VMEM((model, tokens), bf16),
            pltpu.VMEM((model, tokens), f32),
            pltpu.VMEM((tokens, model), bf16),
            pltpu.VMEM((tokens, tokens), f32),
            pltpu.SemaphoreType.DMA((3, 4)),
        ],
        compiler_params=pltpu.CompilerParams(vmem_limit_bytes=40 * 1024 * 1024),
        name="tokens",
    )(gathered, gains, columns, member, spread, wq, *held[3:])
    return exchange(result).reshape(latent.shape)


def solution(mesh):
    placed = (P(("groups", "frame"), None, None), P(), P(), P(), P(), P())
    return jax.shard_map(
        body,
        mesh=mesh,
        in_specs=placed,
        out_specs=P(("groups", "frame"), None, None),
        check_vma=False,
    )
```

```python
import functools
import math

import jax
import jax.numpy as jnp
from jax import lax
from jax.experimental import pallas as pl
from jax.experimental.pallas import tpu as pltpu
from jax.sharding import PartitionSpec as P

HEADS = 16
HEAD_DIM = 72
LANES = 128
EPS = 1e-06
EXP2_SCALE = HEAD_DIM**-0.5 * math.log2(math.e)


def dot(a, b):
    return jnp.dot(a, b, preferred_element_type=jnp.float32)


def held_kernel(
    ln_ref, qg_ref, kg_ref, wqkv_ref, gains_out, columns_out, member_out, spread_out, wq_out, ln, qg, kg, sems
):
    width = wq_out.shape[1]
    pairs = [(ln_ref, ln), (qg_ref, qg), (kg_ref, kg), (wqkv_ref.at[:, pl.ds(0, width)], wq_out)]
    copies = [pltpu.make_async_copy(src, dst, sems.at[i]) for i, (src, dst) in enumerate(pairs)]
    for copy in copies:
        copy.start()

    def belongs(feature, lane):
        head = jnp.where(lane >= HEADS, lane - HEADS, lane)
        first = head * HEAD_DIM
        held = (feature >= first) & (feature < first + HEAD_DIM) & (lane < 2 * HEADS)
        return held.astype(jnp.float32).astype(jnp.bfloat16)

    for out, axis in ((member_out, 0), (spread_out, 1)):
        feature = lax.broadcasted_iota(jnp.int32, out.shape, axis)
        out[...] = belongs(feature, lax.broadcasted_iota(jnp.int32, out.shape, 1 - axis))
    for copy in copies[:3]:
        copy.wait()
    gains_out[0:1, :] = ln[...].reshape(1, width)
    row = jnp.concatenate([qg[...].reshape(1, HEAD_DIM), jnp.zeros((1, LANES - HEAD_DIM), jnp.float32)], axis=1)
    columns_out[...] = jnp.broadcast_to(row, (LANES, LANES)).T[:HEAD_DIM]
    gains_out[1:2, :] = jnp.concatenate([kg[...].reshape(1, HEAD_DIM)] * HEADS, axis=1)
    copies[3].wait()


def tokens_kernel(
    x_ref,
    gains_ref,
    columns_ref,
    member_ref,
    spread_ref,
    wq,
    wqkv_hbm,
    wout_hbm,
    o_ref,
    wkv,
    wout,
    normed,
    mixed_q,
    mixed_k,
    queries_t,
    keys,
    values_t,
    attended_t,
    attended,
    same,
    sems,
):
    frames, positions, width = x_ref.shape
    tokens = frames * positions
    bf16, f32 = jnp.bfloat16, jnp.float32

    bounds = [(0, 32), (32, width - 32)]
    pairs = [
        (wqkv_hbm.at[pl.ds(row, rows), pl.ds(part * width, width)], wkv.at[pl.ds(row, rows), pl.ds((part - 1) * width, width)])
        for part in (1, 2)
        for row, rows in bounds
    ]
    pairs += [(wout_hbm, wout)]
    copies = [pltpu.make_async_copy(src, dst, sems.at[i]) for i, (src, dst) in enumerate(pairs)]
    copies[0].start()
    copies[1].start()

    gain = gains_ref[0:1, :]
    step = max(1, 16 // positions)
    for frame in range(0, frames, step):
        x = x_ref[frame : frame + step].astype(f32).reshape(step * positions, width)
        center = x - jnp.mean(x, axis=-1, keepdims=True)
        spread = jnp.mean(center * center, axis=-1, keepdims=True)
        rows = slice(frame * positions, (frame + step) * positions)
        normed[rows, :] = (center * lax.rsqrt(spread + EPS) * gain).astype(bf16)

    def head_norm(mixed, row, out):
        squares = mixed[...] * mixed[...]
        high = squares.astype(bf16)
        low = (squares - high.astype(f32)).astype(bf16)
        total = dot(jnp.concatenate([high, low], axis=0), member_ref[...])
        total = total[:tokens] + total[tokens:]
        inverse = lax.rsqrt(total * (1.0 / HEAD_DIM) + EPS)
        high = inverse.astype(bf16)
        low = (inverse - high.astype(f32)).astype(bf16)
        lane = lax.broadcasted_iota(jnp.int32, inverse.shape, 1)
        parts = jnp.where(lane < HEADS, high, low)[:, : 2 * HEADS]
        out[...] = (mixed[...] * dot(parts, spread_ref[...]) * gains_ref[row : row + 1, :]).astype(bf16)

    mixed_q[...] = dot(normed[...], wq[...]).T
    copies[0].wait()
    copies[2].start()
    copies[3].start()
    for pair in range(HEADS // 2):
        heads = []
        for first in (2 * pair * HEAD_DIM, (2 * pair + 1) * HEAD_DIM):
            head = mixed_q[first : first + HEAD_DIM, :]
            total = jnp.sum(head * head, axis=0, keepdims=True)
            heads.append(head * lax.rsqrt(total * (1.0 / HEAD_DIM) + EPS) * columns_ref[...])
        rows = slice(2 * pair * HEAD_DIM, (2 * pair + 2) * HEAD_DIM)
        queries_t[rows, :] = jnp.concatenate(heads, axis=0).astype(bf16)
    copies[1].wait()
    mixed_k[...] = dot(normed[...], wkv[:, :width])
    copies[2].wait()
    copies[4].start()
    head_norm(mixed_k, 1, keys)
    copies[3].wait()
    values_t[...] = dot(normed[...], wkv[:, width:]).astype(bf16).T

    place = lax.broadcasted_iota(jnp.int32, (tokens, tokens), 0) % positions
    other = lax.broadcasted_iota(jnp.int32, (tokens, tokens), 1) % positions
    same[...] = (place == other).astype(f32)

    row = lax.broadcasted_iota(jnp.int32, (2 * LANES, tokens), 0)
    for pair in range(HEADS // 2):
        window = slice(pair * LANES, (pair + 2) * LANES)
        begin = pair * (2 * HEAD_DIM - LANES)
        query = queries_t[window, :]
        both = [
            jnp.where((row >= begin + h * HEAD_DIM) & (row < begin + (h + 1) * HEAD_DIM), query, jnp.zeros((), bf16))
            for h in range(2)
        ]
        scores = dot(keys[:, window], jnp.concatenate(both, axis=1))
        weights = []
        for h in range(2):
            part = jnp.exp2(scores[:, h * tokens : (h + 1) * tokens] * EXP2_SCALE) * same[...]
            weights.append((part * (1.0 / jnp.sum(part, axis=0, keepdims=True))).astype(bf16))
        features = slice(pair * 2 * HEAD_DIM, (pair + 1) * 2 * HEAD_DIM)
        heads_out = dot(values_t[features, :], jnp.concatenate(weights, axis=1))
        for h in range(2):
            first = (2 * pair + h) * HEAD_DIM
            attended_t[first : first + HEAD_DIM, :] = heads_out[
                h * HEAD_DIM : (h + 1) * HEAD_DIM, h * tokens : (h + 1) * tokens
            ]
    attended[...] = attended_t[...].astype(bf16).T

    copies[4].wait()
    branch = dot(attended[...], wout[...])
    o_ref[...] = (x_ref[...].astype(f32) + branch.reshape(x_ref.shape)).astype(bf16)


def body(latent, ln_gain, q_gain, k_gain, w_qkv, w_out):
    device_count = lax.axis_size("frame")
    rows, columns, model = latent.shape
    tokens = rows * columns
    per_peer = tokens // device_count
    exchange = functools.partial(
        lax.all_to_all, axis_name="frame", split_axis=0, concat_axis=0, tiled=True
    )
    gathered = exchange(latent.reshape(device_count, per_peer, model))
    in_vmem = pl.BlockSpec(memory_space=pltpu.VMEM)
    in_hbm = pl.BlockSpec(memory_space=pltpu.HBM)
    bf16, f32 = jnp.bfloat16, jnp.float32
    held = [pltpu.with_memory_space_constraint(a, pltpu.HBM) for a in (ln_gain, q_gain, k_gain, w_qkv, w_out)]
    gains, columns, member, spread, wq = pl.pallas_call(
        held_kernel,
        out_shape=(
            pltpu.VMEM((8, model), f32),
            pltpu.VMEM((HEAD_DIM, LANES), f32),
            pltpu.VMEM((model, LANES), bf16),
            pltpu.VMEM((2 * HEADS, model), bf16),
            pltpu.VMEM((model, model), bf16),
        ),
        in_specs=[in_hbm] * 4,
        out_specs=[in_vmem] * 5,
        scratch_shapes=[
            pltpu.VMEM((model,), f32),
            pltpu.VMEM((HEAD_DIM,), f32),
            pltpu.VMEM((HEAD_DIM,), f32),
            pltpu.SemaphoreType.DMA((4,)),
        ],
        compiler_params=pltpu.CompilerParams(vmem_limit_bytes=8 * 1024 * 1024),
        cost_estimate=pl.CostEstimate(flops=0, bytes_accessed=4 * model * model, transcendentals=0),
        name="held",
    )(*held[:4])
    result = pl.pallas_call(
        tokens_kernel,
        out_shape=jax.ShapeDtypeStruct(gathered.shape, bf16),
        in_specs=[in_vmem] * 6 + [in_hbm] * 2,
        out_specs=in_vmem,
        scratch_shapes=[
            pltpu.VMEM((model, 2 * model), bf16),
            pltpu.VMEM(w_out.shape, bf16),
            pltpu.VMEM((tokens, model), bf16),
            pltpu.VMEM((model, tokens), f32),
            pltpu.VMEM((tokens, model), f32),
            pltpu.VMEM((model, tokens), bf16),
            pltpu.VMEM((tokens, model), bf16),
            pltpu.VMEM((model, tokens), bf16),
            pltpu.VMEM((model, tokens), f32),
            pltpu.VMEM((tokens, model), bf16),
            pltpu.VMEM((tokens, tokens), f32),
            pltpu.SemaphoreType.DMA((5,)),
        ],
        compiler_params=pltpu.CompilerParams(vmem_limit_bytes=40 * 1024 * 1024),
        name="tokens",
    )(gathered, gains, columns, member, spread, wq, *held[3:])
    return exchange(result).reshape(latent.shape)


def solution(mesh):
    placed = (P(("groups", "frame"), None, None), P(), P(), P(), P(), P())
    return jax.shard_map(
        body,
        mesh=mesh,
        in_specs=placed,
        out_specs=P(("groups", "frame"), None, None),
        check_vma=False,
    )
```

```python
import functools
import math

import jax
import jax.numpy as jnp
from jax import lax
from jax.experimental import pallas as pl
from jax.experimental.pallas import tpu as pltpu
from jax.sharding import PartitionSpec as P

HEADS = 16
HEAD_DIM = 72
LANES = 128
EPS = 1e-06
EXP2_SCALE = HEAD_DIM**-0.5 * math.log2(math.e)


def dot(a, b):
    return jnp.dot(a, b, preferred_element_type=jnp.float32)


def held_kernel(
    ln_ref, qg_ref, kg_ref, wqkv_ref, gains_out, columns_out, member_out, spread_out, wq_out, ln, qg, kg, sems
):
    width = wq_out.shape[1]
    pairs = [(ln_ref, ln), (qg_ref, qg), (kg_ref, kg), (wqkv_ref.at[:, pl.ds(0, width)], wq_out)]
    copies = [pltpu.make_async_copy(src, dst, sems.at[i]) for i, (src, dst) in enumerate(pairs)]
    for copy in copies:
        copy.start()

    def belongs(feature, lane):
        head = jnp.where(lane >= HEADS, lane - HEADS, lane)
        first = head * HEAD_DIM
        held = (feature >= first) & (feature < first + HEAD_DIM) & (lane < 2 * HEADS)
        return held.astype(jnp.float32).astype(jnp.bfloat16)

    for out, axis in ((member_out, 0), (spread_out, 1)):
        feature = lax.broadcasted_iota(jnp.int32, out.shape, axis)
        out[...] = belongs(feature, lax.broadcasted_iota(jnp.int32, out.shape, 1 - axis))
    for copy in copies[:3]:
        copy.wait()
    gains_out[0:1, :] = ln[...].reshape(1, width)
    row = jnp.concatenate([qg[...].reshape(1, HEAD_DIM), jnp.zeros((1, LANES - HEAD_DIM), jnp.float32)], axis=1)
    columns_out[...] = jnp.broadcast_to(row, (LANES, LANES)).T[:HEAD_DIM]
    gains_out[1:2, :] = jnp.concatenate([kg[...].reshape(1, HEAD_DIM)] * HEADS, axis=1)
    copies[3].wait()


def tokens_kernel(
    x_ref,
    gains_ref,
    columns_ref,
    member_ref,
    spread_ref,
    wq,
    wqkv_hbm,
    wout_hbm,
    o_ref,
    wkv,
    wout,
    normed,
    mixed_q,
    mixed_k,
    queries_t,
    keys,
    values_t,
    attended_t,
    attended,
    same,
    sems,
):
    frames, positions, width = x_ref.shape
    tokens = frames * positions
    bf16, f32 = jnp.bfloat16, jnp.float32

    pairs = [
        (wqkv_hbm.at[:, pl.ds(width, width)], wkv.at[:, pl.ds(0, width)]),
        (wqkv_hbm.at[:, pl.ds(2 * width, width)], wkv.at[:, pl.ds(width, width)]),
        (wout_hbm, wout),
    ]
    copies = [pltpu.make_async_copy(src, dst, sems.at[i]) for i, (src, dst) in enumerate(pairs)]
    copies[0].start()

    gain = gains_ref[0:1, :]
    step = max(1, 16 // positions)
    for frame in range(0, frames, step):
        x = x_ref[frame : frame + step].astype(f32).reshape(step * positions, width)
        center = x - jnp.mean(x, axis=-1, keepdims=True)
        spread = jnp.mean(center * center, axis=-1, keepdims=True)
        rows = slice(frame * positions, (frame + step) * positions)
        normed[rows, :] = (center * lax.rsqrt(spread + EPS) * gain).astype(bf16)

    def head_norm(mixed, row, out):
        squares = mixed[...] * mixed[...]
        high = squares.astype(bf16)
        low = (squares - high.astype(f32)).astype(bf16)
        total = dot(jnp.concatenate([high, low], axis=0), member_ref[...])
        total = total[:tokens] + total[tokens:]
        inverse = lax.rsqrt(total * (1.0 / HEAD_DIM) + EPS)
        high = inverse.astype(bf16)
        low = (inverse - high.astype(f32)).astype(bf16)
        lane = lax.broadcasted_iota(jnp.int32, inverse.shape, 1)
        parts = jnp.where(lane < HEADS, high, low)[:, : 2 * HEADS]
        out[...] = (mixed[...] * dot(parts, spread_ref[...]) * gains_ref[row : row + 1, :]).astype(bf16)

    copies[1].start()
    mixed_q[...] = dot(normed[...], wq[...]).T
    for pair in range(HEADS // 2):
        heads = []
        for first in (2 * pair * HEAD_DIM, (2 * pair + 1) * HEAD_DIM):
            head = mixed_q[first : first + HEAD_DIM, :]
            total = jnp.sum(head * head, axis=0, keepdims=True)
            heads.append(head * lax.rsqrt(total * (1.0 / HEAD_DIM) + EPS) * columns_ref[...])
        rows = slice(2 * pair * HEAD_DIM, (2 * pair + 2) * HEAD_DIM)
        queries_t[rows, :] = jnp.concatenate(heads, axis=0).astype(bf16)
    copies[0].wait()
    copies[2].start()
    mixed_k[...] = dot(normed[...], wkv[:, :width])
    head_norm(mixed_k, 1, keys)
    copies[1].wait()
    values_t[...] = dot(normed[...], wkv[:, width:]).astype(bf16).T

    place = lax.broadcasted_iota(jnp.int32, (tokens, tokens), 0) % positions
    other = lax.broadcasted_iota(jnp.int32, (tokens, tokens), 1) % positions
    same[...] = (place == other).astype(f32)

    row = lax.broadcasted_iota(jnp.int32, (2 * LANES, tokens), 0)
    for pair in range(HEADS // 2):
        window = slice(pair * LANES, (pair + 2) * LANES)
        begin = pair * (2 * HEAD_DIM - LANES)
        query = queries_t[window, :]
        both = [
            jnp.where((row >= begin + h * HEAD_DIM) & (row < begin + (h + 1) * HEAD_DIM), query, jnp.zeros((), bf16))
            for h in range(2)
        ]
        scores = dot(keys[:, window], jnp.concatenate(both, axis=1))
        weights = []
        for h in range(2):
            part = jnp.exp2(scores[:, h * tokens : (h + 1) * tokens] * EXP2_SCALE) * same[...]
            weights.append((part * (1.0 / jnp.sum(part, axis=0, keepdims=True))).astype(bf16))
        features = slice(pair * 2 * HEAD_DIM, (pair + 1) * 2 * HEAD_DIM)
        heads_out = dot(values_t[features, :], jnp.concatenate(weights, axis=1))
        for h in range(2):
            first = (2 * pair + h) * HEAD_DIM
            attended_t[first : first + HEAD_DIM, :] = heads_out[
                h * HEAD_DIM : (h + 1) * HEAD_DIM, h * tokens : (h + 1) * tokens
            ]
    attended[...] = attended_t[...].astype(bf16).T

    copies[2].wait()
    branch = dot(attended[...], wout[...])
    o_ref[...] = (x_ref[...].astype(f32) + branch.reshape(x_ref.shape)).astype(bf16)


def body(latent, ln_gain, q_gain, k_gain, w_qkv, w_out):
    device_count = lax.axis_size("frame")
    rows, columns, model = latent.shape
    tokens = rows * columns
    per_peer = tokens // device_count
    order = [4 * i + 2 * row + core for row in range(2) for i in range(device_count // 4) for core in range(2)]
    exchange = functools.partial(
        lax.all_to_all, axis_name="frame", split_axis=0, concat_axis=0, axis_index_groups=[order], tiled=True
    )
    gathered = exchange(latent.reshape(device_count, per_peer, model))
    in_vmem = pl.BlockSpec(memory_space=pltpu.VMEM)
    in_hbm = pl.BlockSpec(memory_space=pltpu.HBM)
    bf16, f32 = jnp.bfloat16, jnp.float32
    held = [pltpu.with_memory_space_constraint(a, pltpu.HBM) for a in (ln_gain, q_gain, k_gain, w_qkv, w_out)]
    gains, columns, member, spread, wq = pl.pallas_call(
        held_kernel,
        out_shape=(
            pltpu.VMEM((8, model), f32),
            pltpu.VMEM((HEAD_DIM, LANES), f32),
            pltpu.VMEM((model, LANES), bf16),
            pltpu.VMEM((2 * HEADS, model), bf16),
            pltpu.VMEM((model, model), bf16),
        ),
        in_specs=[in_hbm] * 4,
        out_specs=[in_vmem] * 5,
        scratch_shapes=[
            pltpu.VMEM((model,), f32),
            pltpu.VMEM((HEAD_DIM,), f32),
            pltpu.VMEM((HEAD_DIM,), f32),
            pltpu.SemaphoreType.DMA((4,)),
        ],
        compiler_params=pltpu.CompilerParams(vmem_limit_bytes=8 * 1024 * 1024),
        cost_estimate=pl.CostEstimate(flops=0, bytes_accessed=4 * model * model, transcendentals=0),
        name="held",
    )(*held[:4])
    result = pl.pallas_call(
        tokens_kernel,
        out_shape=jax.ShapeDtypeStruct(gathered.shape, bf16),
        in_specs=[in_vmem] * 6 + [in_hbm] * 2,
        out_specs=in_vmem,
        scratch_shapes=[
            pltpu.VMEM((model, 2 * model), bf16),
            pltpu.VMEM(w_out.shape, bf16),
            pltpu.VMEM((tokens, model), bf16),
            pltpu.VMEM((model, tokens), f32),
            pltpu.VMEM((tokens, model), f32),
            pltpu.VMEM((model, tokens), bf16),
            pltpu.VMEM((tokens, model), bf16),
            pltpu.VMEM((model, tokens), bf16),
            pltpu.VMEM((model, tokens), f32),
            pltpu.VMEM((tokens, model), bf16),
            pltpu.VMEM((tokens, tokens), f32),
            pltpu.SemaphoreType.DMA((3,)),
        ],
        compiler_params=pltpu.CompilerParams(vmem_limit_bytes=40 * 1024 * 1024),
        name="tokens",
    )(gathered, gains, columns, member, spread, wq, *held[3:])
    return exchange(result).reshape(latent.shape)


def solution(mesh):
    placed = (P(("groups", "frame"), None, None), P(), P(), P(), P(), P())
    return jax.shard_map(
        body,
        mesh=mesh,
        in_specs=placed,
        out_specs=P(("groups", "frame"), None, None),
        check_vma=False,
    )
```

```python
import functools
import math

import jax
import jax.numpy as jnp
from jax import lax
from jax.experimental import pallas as pl
from jax.experimental.pallas import tpu as pltpu
from jax.sharding import PartitionSpec as P

HEADS = 16
HEAD_DIM = 72
LANES = 128
EPS = 1e-06
EXP2_SCALE = HEAD_DIM**-0.5 * math.log2(math.e)


def dot(a, b):
    return jnp.dot(a, b, preferred_element_type=jnp.float32)


def held_kernel(
    ln_ref, qg_ref, kg_ref, wqkv_ref, gains_out, columns_out, member_out, spread_out, wq_out, ln, qg, kg, sems
):
    width = wq_out.shape[1]
    pairs = [(ln_ref, ln), (qg_ref, qg), (kg_ref, kg), (wqkv_ref.at[:, pl.ds(0, width)], wq_out)]
    copies = [pltpu.make_async_copy(src, dst, sems.at[i]) for i, (src, dst) in enumerate(pairs)]
    for copy in copies:
        copy.start()

    def belongs(feature, lane):
        head = jnp.where(lane >= HEADS, lane - HEADS, lane)
        first = head * HEAD_DIM
        held = (feature >= first) & (feature < first + HEAD_DIM) & (lane < 2 * HEADS)
        return held.astype(jnp.float32).astype(jnp.bfloat16)

    for out, axis in ((member_out, 0), (spread_out, 1)):
        feature = lax.broadcasted_iota(jnp.int32, out.shape, axis)
        out[...] = belongs(feature, lax.broadcasted_iota(jnp.int32, out.shape, 1 - axis))
    for copy in copies[:3]:
        copy.wait()
    gains_out[0:1, :] = ln[...].reshape(1, width)
    row = jnp.concatenate([qg[...].reshape(1, HEAD_DIM), jnp.zeros((1, LANES - HEAD_DIM), jnp.float32)], axis=1)
    columns_out[...] = jnp.broadcast_to(row, (LANES, LANES)).T[:HEAD_DIM]
    gains_out[1:2, :] = jnp.concatenate([kg[...].reshape(1, HEAD_DIM)] * HEADS, axis=1)
    copies[3].wait()


def tokens_kernel(
    x_ref,
    gains_ref,
    columns_ref,
    member_ref,
    spread_ref,
    wq,
    wqkv_hbm,
    o_ref,
    wkv,
    normed,
    mixed_q,
    mixed_k,
    queries_t,
    keys,
    values_t,
    attended_t,
    same,
    sems,
):
    frames, positions, width = x_ref.shape
    tokens = frames * positions
    bf16, f32 = jnp.bfloat16, jnp.float32

    pairs = [
        (wqkv_hbm.at[:, pl.ds(width, width)], wkv.at[:, pl.ds(0, width)]),
        (wqkv_hbm.at[:, pl.ds(2 * width, width)], wkv.at[:, pl.ds(width, width)]),
    ]
    copies = [pltpu.make_async_copy(src, dst, sems.at[i]) for i, (src, dst) in enumerate(pairs)]
    copies[0].start()

    gain = gains_ref[0:1, :]
    step = max(1, 16 // positions)
    for frame in range(0, frames, step):
        x = x_ref[frame : frame + step].astype(f32).reshape(step * positions, width)
        center = x - jnp.mean(x, axis=-1, keepdims=True)
        spread = jnp.mean(center * center, axis=-1, keepdims=True)
        rows = slice(frame * positions, (frame + step) * positions)
        normed[rows, :] = (center * lax.rsqrt(spread + EPS) * gain).astype(bf16)

    def head_norm(mixed, row, out):
        squares = mixed[...] * mixed[...]
        high = squares.astype(bf16)
        low = (squares - high.astype(f32)).astype(bf16)
        total = dot(jnp.concatenate([high, low], axis=0), member_ref[...])
        total = total[:tokens] + total[tokens:]
        inverse = lax.rsqrt(total * (1.0 / HEAD_DIM) + EPS)
        high = inverse.astype(bf16)
        low = (inverse - high.astype(f32)).astype(bf16)
        lane = lax.broadcasted_iota(jnp.int32, inverse.shape, 1)
        parts = jnp.where(lane < HEADS, high, low)[:, : 2 * HEADS]
        out[...] = (mixed[...] * dot(parts, spread_ref[...]) * gains_ref[row : row + 1, :]).astype(bf16)

    copies[1].start()
    mixed_q[...] = dot(normed[...], wq[...]).T
    for pair in range(HEADS // 2):
        heads = []
        for first in (2 * pair * HEAD_DIM, (2 * pair + 1) * HEAD_DIM):
            head = mixed_q[first : first + HEAD_DIM, :]
            total = jnp.sum(head * head, axis=0, keepdims=True)
            heads.append(head * lax.rsqrt(total * (1.0 / HEAD_DIM) + EPS) * columns_ref[...])
        rows = slice(2 * pair * HEAD_DIM, (2 * pair + 2) * HEAD_DIM)
        queries_t[rows, :] = jnp.concatenate(heads, axis=0).astype(bf16)
    copies[0].wait()
    mixed_k[...] = dot(normed[...], wkv[:, :width])
    head_norm(mixed_k, 1, keys)
    copies[1].wait()
    values_t[...] = dot(normed[...], wkv[:, width:]).astype(bf16).T

    place = lax.broadcasted_iota(jnp.int32, (tokens, tokens), 0) % positions
    other = lax.broadcasted_iota(jnp.int32, (tokens, tokens), 1) % positions
    same[...] = (place == other).astype(f32)

    row = lax.broadcasted_iota(jnp.int32, (2 * LANES, tokens), 0)
    for pair in range(HEADS // 2):
        window = slice(pair * LANES, (pair + 2) * LANES)
        begin = pair * (2 * HEAD_DIM - LANES)
        query = queries_t[window, :]
        both = [
            jnp.where((row >= begin + h * HEAD_DIM) & (row < begin + (h + 1) * HEAD_DIM), query, jnp.zeros((), bf16))
            for h in range(2)
        ]
        scores = dot(keys[:, window], jnp.concatenate(both, axis=1))
        weights = []
        for h in range(2):
            part = jnp.exp2(scores[:, h * tokens : (h + 1) * tokens] * EXP2_SCALE) * same[...]
            weights.append((part * (1.0 / jnp.sum(part, axis=0, keepdims=True))).astype(bf16))
        features = slice(pair * 2 * HEAD_DIM, (pair + 1) * 2 * HEAD_DIM)
        heads_out = dot(values_t[features, :], jnp.concatenate(weights, axis=1))
        for h in range(2):
            first = (2 * pair + h) * HEAD_DIM
            attended_t[first : first + HEAD_DIM, :] = heads_out[
                h * HEAD_DIM : (h + 1) * HEAD_DIM, h * tokens : (h + 1) * tokens
            ]
    o_ref[...] = attended_t[...].astype(bf16).T.reshape(o_ref.shape)


def body(latent, ln_gain, q_gain, k_gain, w_qkv, w_out):
    device_count = lax.axis_size("frame")
    rows, columns, model = latent.shape
    tokens = rows * columns
    per_peer = tokens // device_count
    order = [4 * i + 2 * row + core for row in range(2) for i in range(device_count // 4) for core in range(2)]
    exchange = functools.partial(
        lax.all_to_all, axis_name="frame", split_axis=0, concat_axis=0, axis_index_groups=[order], tiled=True
    )
    gathered = exchange(latent.reshape(device_count, per_peer, model))
    in_vmem = pl.BlockSpec(memory_space=pltpu.VMEM)
    in_hbm = pl.BlockSpec(memory_space=pltpu.HBM)
    bf16, f32 = jnp.bfloat16, jnp.float32
    held = [pltpu.with_memory_space_constraint(a, pltpu.HBM) for a in (ln_gain, q_gain, k_gain, w_qkv)]
    gains, columns, member, spread, wq = pl.pallas_call(
        held_kernel,
        out_shape=(
            pltpu.VMEM((8, model), f32),
            pltpu.VMEM((HEAD_DIM, LANES), f32),
            pltpu.VMEM((model, LANES), bf16),
            pltpu.VMEM((2 * HEADS, model), bf16),
            pltpu.VMEM((model, model), bf16),
        ),
        in_specs=[in_hbm] * 4,
        out_specs=[in_vmem] * 5,
        scratch_shapes=[
            pltpu.VMEM((model,), f32),
            pltpu.VMEM((HEAD_DIM,), f32),
            pltpu.VMEM((HEAD_DIM,), f32),
            pltpu.SemaphoreType.DMA((4,)),
        ],
        compiler_params=pltpu.CompilerParams(vmem_limit_bytes=8 * 1024 * 1024),
        cost_estimate=pl.CostEstimate(flops=0, bytes_accessed=4 * model * model, transcendentals=0),
        name="held",
    )(*held[:4])
    attended = pl.pallas_call(
        tokens_kernel,
        out_shape=jax.ShapeDtypeStruct(gathered.shape, bf16),
        in_specs=[in_vmem] * 6 + [in_hbm],
        out_specs=in_vmem,
        scratch_shapes=[
            pltpu.VMEM((model, 2 * model), bf16),
            pltpu.VMEM((tokens, model), bf16),
            pltpu.VMEM((model, tokens), f32),
            pltpu.VMEM((tokens, model), f32),
            pltpu.VMEM((model, tokens), bf16),
            pltpu.VMEM((tokens, model), bf16),
            pltpu.VMEM((model, tokens), bf16),
            pltpu.VMEM((model, tokens), f32),
            pltpu.VMEM((tokens, tokens), f32),
            pltpu.SemaphoreType.DMA((2,)),
        ],
        compiler_params=pltpu.CompilerParams(vmem_limit_bytes=40 * 1024 * 1024),
        name="tokens",
    )(gathered, gains, columns, member, spread, wq, *held[3:])
    branch = jnp.dot(exchange(attended).reshape(tokens, model), w_out, preferred_element_type=f32)
    return (latent.astype(f32) + branch.reshape(latent.shape)).astype(bf16)


def solution(mesh):
    placed = (P(("groups", "frame"), None, None), P(), P(), P(), P(), P())
    return jax.shard_map(
        body,
        mesh=mesh,
        in_specs=placed,
        out_specs=P(("groups", "frame"), None, None),
        check_vma=False,
    )
```

```python
import functools
import math

import jax
import jax.numpy as jnp
from jax import lax
from jax.experimental import pallas as pl
from jax.experimental.pallas import tpu as pltpu
from jax.sharding import PartitionSpec as P

HEADS = 16
HEAD_DIM = 72
LANES = 128
EPS = 1e-06
EXP2_SCALE = HEAD_DIM**-0.5 * math.log2(math.e)


def dot(a, b):
    return jnp.dot(a, b, preferred_element_type=jnp.float32)


def held_kernel(
    positions, ln_ref, qg_ref, kg_ref, wqkv_ref, gains_out, columns_out, same_out, member_out, spread_out, wq_out, ln, qg, kg, sems
):
    width = wq_out.shape[1]
    pairs = [(ln_ref, ln), (qg_ref, qg), (kg_ref, kg), (wqkv_ref.at[:, pl.ds(0, width)], wq_out)]
    copies = [pltpu.make_async_copy(src, dst, sems.at[i]) for i, (src, dst) in enumerate(pairs)]
    for copy in copies:
        copy.start()

    def belongs(feature, lane):
        head = jnp.where(lane >= HEADS, lane - HEADS, lane)
        first = head * HEAD_DIM
        held = (feature >= first) & (feature < first + HEAD_DIM) & (lane < 2 * HEADS)
        return held.astype(jnp.float32).astype(jnp.bfloat16)

    for out, axis in ((member_out, 0), (spread_out, 1)):
        feature = lax.broadcasted_iota(jnp.int32, out.shape, axis)
        out[...] = belongs(feature, lax.broadcasted_iota(jnp.int32, out.shape, 1 - axis))
    place = lax.broadcasted_iota(jnp.int32, same_out.shape, 0) % positions
    other = lax.broadcasted_iota(jnp.int32, same_out.shape, 1) % positions
    same_out[...] = (place == other).astype(jnp.float32)
    for copy in copies[:3]:
        copy.wait()
    gains_out[0:1, :] = ln[...].reshape(1, width)
    row = jnp.concatenate([qg[...].reshape(1, HEAD_DIM), jnp.zeros((1, LANES - HEAD_DIM), jnp.float32)], axis=1)
    columns_out[...] = jnp.broadcast_to(row, (LANES, LANES)).T[:HEAD_DIM]
    gains_out[1:2, :] = jnp.concatenate([kg[...].reshape(1, HEAD_DIM)] * HEADS, axis=1)
    copies[3].wait()


def tokens_kernel(
    x_ref,
    gains_ref,
    columns_ref,
    same,
    member_ref,
    spread_ref,
    wq,
    wqkv_hbm,
    wout_hbm,
    o_ref,
    wkv,
    wout,
    normed,
    mixed_q,
    mixed_k,
    keys,
    values_t,
    attended_t,
    attended,
    stacks,
    sems,
):
    frames, positions, width = x_ref.shape
    tokens = frames * positions
    bf16, f32 = jnp.bfloat16, jnp.float32

    pairs = [
        (wqkv_hbm.at[:, pl.ds(width, width)], wkv.at[:, pl.ds(0, width)]),
        (wqkv_hbm.at[:, pl.ds(2 * width, width)], wkv.at[:, pl.ds(width, width)]),
        (wout_hbm, wout),
    ]
    copies = [pltpu.make_async_copy(src, dst, sems.at[i]) for i, (src, dst) in enumerate(pairs)]
    copies[0].start()

    gain = gains_ref[0:1, :]
    step = max(1, 16 // positions)
    for frame in range(0, frames, step):
        x = x_ref[frame : frame + step].astype(f32).reshape(step * positions, width)
        center = x - jnp.mean(x, axis=-1, keepdims=True)
        spread = jnp.mean(center * center, axis=-1, keepdims=True)
        rows = slice(frame * positions, (frame + step) * positions)
        normed[rows, :] = (center * lax.rsqrt(spread + EPS) * gain).astype(bf16)

    def head_norm(mixed, row, out):
        squares = mixed[...] * mixed[...]
        high = squares.astype(bf16)
        low = (squares - high.astype(f32)).astype(bf16)
        total = dot(jnp.concatenate([high, low], axis=0), member_ref[...])
        total = total[:tokens] + total[tokens:]
        inverse = lax.rsqrt(total * (1.0 / HEAD_DIM) + EPS)
        high = inverse.astype(bf16)
        low = (inverse - high.astype(f32)).astype(bf16)
        lane = lax.broadcasted_iota(jnp.int32, inverse.shape, 1)
        parts = jnp.where(lane < HEADS, high, low)[:, : 2 * HEADS]
        out[...] = (mixed[...] * dot(parts, spread_ref[...]) * gains_ref[row : row + 1, :]).astype(bf16)

    copies[1].start()
    mixed_q[...] = dot(normed[...], wq[...]).T
    for pair in range(HEADS // 2):
        heads = []
        for first in (2 * pair * HEAD_DIM, (2 * pair + 1) * HEAD_DIM):
            head = mixed_q[first : first + HEAD_DIM, :]
            total = jnp.sum(head * head, axis=0, keepdims=True)
            heads.append(head * lax.rsqrt(total * (1.0 / HEAD_DIM) + EPS) * columns_ref[...])
        begin = pair * (2 * HEAD_DIM - LANES)
        for h, head in enumerate(heads):
            above = begin + h * HEAD_DIM
            below = 2 * LANES - above - HEAD_DIM
            rows = [jnp.zeros((n, tokens), f32) for n in (above, below)]
            rows = [part for part in (rows[0], head, rows[1]) if part.shape[0]]
            stacks[pair, :, h * tokens : (h + 1) * tokens] = jnp.concatenate(rows, axis=0).astype(bf16)
    copies[0].wait()
    copies[2].start()
    mixed_k[...] = dot(normed[...], wkv[:, :width])
    head_norm(mixed_k, 1, keys)
    copies[1].wait()
    values_t[...] = dot(normed[...], wkv[:, width:]).astype(bf16).T

    for pair in range(HEADS // 2):
        scores = dot(keys[:, pair * LANES : (pair + 2) * LANES], stacks[pair])
        weights = []
        for h in range(2):
            part = jnp.exp2(scores[:, h * tokens : (h + 1) * tokens] * EXP2_SCALE) * same[...]
            weights.append((part * (1.0 / jnp.sum(part, axis=0, keepdims=True))).astype(bf16))
        features = slice(pair * 2 * HEAD_DIM, (pair + 1) * 2 * HEAD_DIM)
        heads_out = dot(values_t[features, :], jnp.concatenate(weights, axis=1))
        for h in range(2):
            first = (2 * pair + h) * HEAD_DIM
            attended_t[first : first + HEAD_DIM, :] = heads_out[
                h * HEAD_DIM : (h + 1) * HEAD_DIM, h * tokens : (h + 1) * tokens
            ]
    attended[...] = attended_t[...].astype(bf16).T

    copies[2].wait()
    branch = dot(attended[...], wout[...])
    o_ref[...] = (x_ref[...].astype(f32) + branch.reshape(x_ref.shape)).astype(bf16)


def body(latent, ln_gain, q_gain, k_gain, w_qkv, w_out):
    device_count = lax.axis_size("frame")
    rows, columns, model = latent.shape
    tokens = rows * columns
    per_peer = tokens // device_count
    order = [4 * i + 2 * row + core for row in range(2) for i in range(device_count // 4) for core in range(2)]
    exchange = functools.partial(
        lax.all_to_all, axis_name="frame", split_axis=0, concat_axis=0, axis_index_groups=[order], tiled=True
    )
    gathered = exchange(latent.reshape(device_count, per_peer, model))
    in_vmem = pl.BlockSpec(memory_space=pltpu.VMEM)
    in_hbm = pl.BlockSpec(memory_space=pltpu.HBM)
    bf16, f32 = jnp.bfloat16, jnp.float32
    held = [pltpu.with_memory_space_constraint(a, pltpu.HBM) for a in (ln_gain, q_gain, k_gain, w_qkv, w_out)]
    gains, columns, same, member, spread, wq = pl.pallas_call(
        functools.partial(held_kernel, per_peer),
        out_shape=(
            pltpu.VMEM((8, model), f32),
            pltpu.VMEM((HEAD_DIM, LANES), f32),
            pltpu.VMEM((tokens, tokens), f32),
            pltpu.VMEM((model, LANES), bf16),
            pltpu.VMEM((2 * HEADS, model), bf16),
            pltpu.VMEM((model, model), bf16),
        ),
        in_specs=[in_hbm] * 4,
        out_specs=[in_vmem] * 6,
        scratch_shapes=[
            pltpu.VMEM((model,), f32),
            pltpu.VMEM((HEAD_DIM,), f32),
            pltpu.VMEM((HEAD_DIM,), f32),
            pltpu.SemaphoreType.DMA((4,)),
        ],
        compiler_params=pltpu.CompilerParams(vmem_limit_bytes=8 * 1024 * 1024),
        cost_estimate=pl.CostEstimate(flops=0, bytes_accessed=4 * model * model, transcendentals=0),
        name="held",
    )(*held[:4])
    result = pl.pallas_call(
        tokens_kernel,
        out_shape=jax.ShapeDtypeStruct(gathered.shape, bf16),
        in_specs=[in_vmem] * 7 + [in_hbm] * 2,
        out_specs=in_vmem,
        scratch_shapes=[
            pltpu.VMEM((model, 2 * model), bf16),
            pltpu.VMEM(w_out.shape, bf16),
            pltpu.VMEM((tokens, model), bf16),
            pltpu.VMEM((model, tokens), f32),
            pltpu.VMEM((tokens, model), f32),
            pltpu.VMEM((tokens, model), bf16),
            pltpu.VMEM((model, tokens), bf16),
            pltpu.VMEM((model, tokens), f32),
            pltpu.VMEM((tokens, model), bf16),
            pltpu.VMEM((HEADS // 2, 2 * LANES, 2 * tokens), bf16),
            pltpu.SemaphoreType.DMA((3,)),
        ],
        compiler_params=pltpu.CompilerParams(vmem_limit_bytes=40 * 1024 * 1024),
        name="tokens",
    )(gathered, gains, columns, same, member, spread, wq, *held[3:])
    return exchange(result).reshape(latent.shape)


def solution(mesh):
    placed = (P(("groups", "frame"), None, None), P(), P(), P(), P(), P())
    return jax.shard_map(
        body,
        mesh=mesh,
        in_specs=placed,
        out_specs=P(("groups", "frame"), None, None),
        check_vma=False,
    )
```

```python
import functools
import math

import jax
import jax.numpy as jnp
from jax import lax
from jax.experimental import pallas as pl
from jax.experimental.pallas import tpu as pltpu
from jax.sharding import PartitionSpec as P

HEADS = 16
HEAD_DIM = 72
LANES = 128
EPS = 1e-06
EXP2_SCALE = HEAD_DIM**-0.5 * math.log2(math.e)


def dot(a, b):
    return jnp.dot(a, b, preferred_element_type=jnp.float32)


def held_kernel(
    positions, ln_ref, qg_ref, kg_ref, wqkv_ref, gains_out, columns_out, same_out, member_out, spread_out, wk_out, ln, qg, kg, sems
):
    width = wk_out.shape[1]
    pairs = [(ln_ref, ln), (qg_ref, qg), (kg_ref, kg), (wqkv_ref.at[:, pl.ds(width, width)], wk_out)]
    copies = [pltpu.make_async_copy(src, dst, sems.at[i]) for i, (src, dst) in enumerate(pairs)]
    for copy in copies:
        copy.start()

    def belongs(feature, lane):
        head = jnp.where(lane >= HEADS, lane - HEADS, lane)
        first = head * HEAD_DIM
        held = (feature >= first) & (feature < first + HEAD_DIM) & (lane < 2 * HEADS)
        return held.astype(jnp.float32).astype(jnp.bfloat16)

    for out, axis in ((member_out, 0), (spread_out, 1)):
        feature = lax.broadcasted_iota(jnp.int32, out.shape, axis)
        out[...] = belongs(feature, lax.broadcasted_iota(jnp.int32, out.shape, 1 - axis))
    place = lax.broadcasted_iota(jnp.int32, same_out.shape, 0) % positions
    other = lax.broadcasted_iota(jnp.int32, same_out.shape, 1) % positions
    same_out[...] = (place == other).astype(jnp.float32)
    for copy in copies[:3]:
        copy.wait()
    gains_out[0:1, :] = ln[...].reshape(1, width)
    row = jnp.concatenate([qg[...].reshape(1, HEAD_DIM), jnp.zeros((1, LANES - HEAD_DIM), jnp.float32)], axis=1)
    columns_out[...] = jnp.broadcast_to(row, (LANES, LANES)).T[:HEAD_DIM]
    gains_out[1:2, :] = jnp.concatenate([kg[...].reshape(1, HEAD_DIM)] * HEADS, axis=1)
    copies[3].wait()


def tokens_kernel(
    x_ref,
    gains_ref,
    columns_ref,
    same,
    member_ref,
    spread_ref,
    wk,
    wqkv_hbm,
    wout_hbm,
    o_ref,
    wqv,
    wout,
    normed,
    mixed_q,
    mixed_k,
    keys,
    values_t,
    attended_t,
    attended,
    stacks,
    sems,
):
    frames, positions, width = x_ref.shape
    tokens = frames * positions
    bf16, f32 = jnp.bfloat16, jnp.float32

    pairs = [
        (wqkv_hbm.at[:, pl.ds(0, width)], wqv.at[:, pl.ds(0, width)]),
        (wqkv_hbm.at[:, pl.ds(2 * width, width)], wqv.at[:, pl.ds(width, width)]),
        (wout_hbm, wout),
    ]
    copies = [pltpu.make_async_copy(src, dst, sems.at[i]) for i, (src, dst) in enumerate(pairs)]
    copies[0].start()

    gain = gains_ref[0:1, :]
    step = max(1, 16 // positions)
    for frame in range(0, frames, step):
        x = x_ref[frame : frame + step].astype(f32).reshape(step * positions, width)
        center = x - jnp.mean(x, axis=-1, keepdims=True)
        spread = jnp.mean(center * center, axis=-1, keepdims=True)
        rows = slice(frame * positions, (frame + step) * positions)
        normed[rows, :] = (center * lax.rsqrt(spread + EPS) * gain).astype(bf16)

    def head_norm(mixed, row, out):
        squares = mixed[...] * mixed[...]
        high = squares.astype(bf16)
        low = (squares - high.astype(f32)).astype(bf16)
        total = dot(jnp.concatenate([high, low], axis=0), member_ref[...])
        total = total[:tokens] + total[tokens:]
        inverse = lax.rsqrt(total * (1.0 / HEAD_DIM) + EPS)
        high = inverse.astype(bf16)
        low = (inverse - high.astype(f32)).astype(bf16)
        lane = lax.broadcasted_iota(jnp.int32, inverse.shape, 1)
        parts = jnp.where(lane < HEADS, high, low)[:, : 2 * HEADS]
        out[...] = (mixed[...] * dot(parts, spread_ref[...]) * gains_ref[row : row + 1, :]).astype(bf16)

    copies[1].start()
    mixed_k[...] = dot(normed[...], wk[...])
    head_norm(mixed_k, 1, keys)
    copies[0].wait()
    copies[2].start()
    mixed_q[...] = dot(normed[...], wqv[:, :width]).T
    copies[1].wait()
    values_t[...] = dot(normed[...], wqv[:, width:]).astype(bf16).T
    for pair in range(HEADS // 2):
        heads = []
        for first in (2 * pair * HEAD_DIM, (2 * pair + 1) * HEAD_DIM):
            head = mixed_q[first : first + HEAD_DIM, :]
            total = jnp.sum(head * head, axis=0, keepdims=True)
            heads.append(head * lax.rsqrt(total * (1.0 / HEAD_DIM) + EPS) * columns_ref[...])
        begin = pair * (2 * HEAD_DIM - LANES)
        for h, head in enumerate(heads):
            above = begin + h * HEAD_DIM
            below = 2 * LANES - above - HEAD_DIM
            rows = [jnp.zeros((n, tokens), f32) for n in (above, below)]
            rows = [part for part in (rows[0], head, rows[1]) if part.shape[0]]
            stacks[pair, :, h * tokens : (h + 1) * tokens] = jnp.concatenate(rows, axis=0).astype(bf16)

    for pair in range(HEADS // 2):
        scores = dot(keys[:, pair * LANES : (pair + 2) * LANES], stacks[pair])
        weights = []
        for h in range(2):
            part = jnp.exp2(scores[:, h * tokens : (h + 1) * tokens] * EXP2_SCALE) * same[...]
            weights.append((part * (1.0 / jnp.sum(part, axis=0, keepdims=True))).astype(bf16))
        features = slice(pair * 2 * HEAD_DIM, (pair + 1) * 2 * HEAD_DIM)
        heads_out = dot(values_t[features, :], jnp.concatenate(weights, axis=1))
        for h in range(2):
            first = (2 * pair + h) * HEAD_DIM
            attended_t[first : first + HEAD_DIM, :] = heads_out[
                h * HEAD_DIM : (h + 1) * HEAD_DIM, h * tokens : (h + 1) * tokens
            ]
    attended[...] = attended_t[...].astype(bf16).T

    copies[2].wait()
    branch = dot(attended[...], wout[...])
    o_ref[...] = (x_ref[...].astype(f32) + branch.reshape(x_ref.shape)).astype(bf16)


def body(latent, ln_gain, q_gain, k_gain, w_qkv, w_out):
    device_count = lax.axis_size("frame")
    rows, columns, model = latent.shape
    tokens = rows * columns
    per_peer = tokens // device_count
    order = [4 * i + 2 * row + core for row in range(2) for i in range(device_count // 4) for core in range(2)]
    exchange = functools.partial(
        lax.all_to_all, axis_name="frame", split_axis=0, concat_axis=0, axis_index_groups=[order], tiled=True
    )
    gathered = exchange(latent.reshape(device_count, per_peer, model))
    in_vmem = pl.BlockSpec(memory_space=pltpu.VMEM)
    in_hbm = pl.BlockSpec(memory_space=pltpu.HBM)
    bf16, f32 = jnp.bfloat16, jnp.float32
    held = [pltpu.with_memory_space_constraint(a, pltpu.HBM) for a in (ln_gain, q_gain, k_gain, w_qkv, w_out)]
    gains, columns, same, member, spread, wk = pl.pallas_call(
        functools.partial(held_kernel, per_peer),
        out_shape=(
            pltpu.VMEM((8, model), f32),
            pltpu.VMEM((HEAD_DIM, LANES), f32),
            pltpu.VMEM((tokens, tokens), f32),
            pltpu.VMEM((model, LANES), bf16),
            pltpu.VMEM((2 * HEADS, model), bf16),
            pltpu.VMEM((model, model), bf16),
        ),
        in_specs=[in_hbm] * 4,
        out_specs=[in_vmem] * 6,
        scratch_shapes=[
            pltpu.VMEM((model,), f32),
            pltpu.VMEM((HEAD_DIM,), f32),
            pltpu.VMEM((HEAD_DIM,), f32),
            pltpu.SemaphoreType.DMA((4,)),
        ],
        compiler_params=pltpu.CompilerParams(vmem_limit_bytes=8 * 1024 * 1024),
        cost_estimate=pl.CostEstimate(flops=0, bytes_accessed=4 * model * model, transcendentals=0),
        name="held",
    )(*held[:4])
    result = pl.pallas_call(
        tokens_kernel,
        out_shape=jax.ShapeDtypeStruct(gathered.shape, bf16),
        in_specs=[in_vmem] * 7 + [in_hbm] * 2,
        out_specs=in_vmem,
        scratch_shapes=[
            pltpu.VMEM((model, 2 * model), bf16),
            pltpu.VMEM(w_out.shape, bf16),
            pltpu.VMEM((tokens, model), bf16),
            pltpu.VMEM((model, tokens), f32),
            pltpu.VMEM((tokens, model), f32),
            pltpu.VMEM((tokens, model), bf16),
            pltpu.VMEM((model, tokens), bf16),
            pltpu.VMEM((model, tokens), f32),
            pltpu.VMEM((tokens, model), bf16),
            pltpu.VMEM((HEADS // 2, 2 * LANES, 2 * tokens), bf16),
            pltpu.SemaphoreType.DMA((3,)),
        ],
        compiler_params=pltpu.CompilerParams(vmem_limit_bytes=40 * 1024 * 1024),
        name="tokens",
    )(gathered, gains, columns, same, member, spread, wk, *held[3:])
    return exchange(result).reshape(latent.shape)


def solution(mesh):
    placed = (P(("groups", "frame"), None, None), P(), P(), P(), P(), P())
    return jax.shard_map(
        body,
        mesh=mesh,
        in_specs=placed,
        out_specs=P(("groups", "frame"), None, None),
        check_vma=False,
    )
```

```python
import functools
import math

import jax
import jax.numpy as jnp
from jax import lax
from jax.experimental import pallas as pl
from jax.experimental.pallas import tpu as pltpu
from jax.sharding import PartitionSpec as P

HEADS = 16
HEAD_DIM = 72
LANES = 128
EPS = 1e-06
EXP2_SCALE = HEAD_DIM**-0.5 * math.log2(math.e)


def dot(a, b):
    return jnp.dot(a, b, preferred_element_type=jnp.float32)


def held_kernel(
    ln_ref, qg_ref, kg_ref, wqkv_ref, gains_out, columns_out, member_out, spread_out, wq_out, wkv_out, ln, qg, kg, wkv, sems
):
    width = wq_out.shape[1]
    pairs = [(ln_ref, ln), (qg_ref, qg), (kg_ref, kg), (wqkv_ref.at[:, pl.ds(0, width)], wq_out)]
    pairs += [(wqkv_ref.at[:, pl.ds((i + 1) * width, width)], wkv.at[i]) for i in range(2)]
    pairs += [(wkv.at[i], wkv_out.at[i]) for i in range(2)]
    copies = [pltpu.make_async_copy(src, dst, sems.at[i]) for i, (src, dst) in enumerate(pairs)]
    for copy in copies[:6]:
        copy.start()

    def belongs(feature, lane):
        head = jnp.where(lane >= HEADS, lane - HEADS, lane)
        first = head * HEAD_DIM
        held = (feature >= first) & (feature < first + HEAD_DIM) & (lane < 2 * HEADS)
        return held.astype(jnp.float32).astype(jnp.bfloat16)

    for out, axis in ((member_out, 0), (spread_out, 1)):
        feature = lax.broadcasted_iota(jnp.int32, out.shape, axis)
        out[...] = belongs(feature, lax.broadcasted_iota(jnp.int32, out.shape, 1 - axis))
    for copy in copies[:3]:
        copy.wait()
    gains_out[0:1, :] = ln[...].reshape(1, width)
    row = jnp.concatenate([qg[...].reshape(1, HEAD_DIM), jnp.zeros((1, LANES - HEAD_DIM), jnp.float32)], axis=1)
    columns_out[...] = jnp.broadcast_to(row, (LANES, LANES)).T[:HEAD_DIM]
    gains_out[1:2, :] = jnp.concatenate([kg[...].reshape(1, HEAD_DIM)] * HEADS, axis=1)
    for i in range(2):
        copies[4 + i].wait()
        copies[6 + i].start()
    for copy in (copies[3], copies[6], copies[7]):
        copy.wait()


def tokens_kernel(
    x_ref,
    gains_ref,
    columns_ref,
    member_ref,
    spread_ref,
    wq,
    wkv_hbm,
    wout_hbm,
    o_ref,
    wkv,
    wout,
    normed,
    mixed_q,
    mixed_k,
    queries_t,
    keys,
    values_t,
    attended_t,
    attended,
    same,
    sems,
):
    frames, positions, width = x_ref.shape
    tokens = frames * positions
    bf16, f32 = jnp.bfloat16, jnp.float32

    pairs = [
        (wkv_hbm.at[0], wkv.at[0]),
        (wkv_hbm.at[1], wkv.at[1]),
        (wout_hbm, wout),
    ]
    copies = [pltpu.make_async_copy(src, dst, sems.at[i]) for i, (src, dst) in enumerate(pairs)]
    copies[0].start()

    gain = gains_ref[0:1, :]
    step = max(1, 16 // positions)
    for frame in range(0, frames, step):
        x = x_ref[frame : frame + step].astype(f32).reshape(step * positions, width)
        center = x - jnp.mean(x, axis=-1, keepdims=True)
        spread = jnp.mean(center * center, axis=-1, keepdims=True)
        rows = slice(frame * positions, (frame + step) * positions)
        normed[rows, :] = (center * lax.rsqrt(spread + EPS) * gain).astype(bf16)

    def head_norm(mixed, row, out):
        squares = mixed[...] * mixed[...]
        high = squares.astype(bf16)
        low = (squares - high.astype(f32)).astype(bf16)
        total = dot(jnp.concatenate([high, low], axis=0), member_ref[...])
        total = total[:tokens] + total[tokens:]
        inverse = lax.rsqrt(total * (1.0 / HEAD_DIM) + EPS)
        high = inverse.astype(bf16)
        low = (inverse - high.astype(f32)).astype(bf16)
        lane = lax.broadcasted_iota(jnp.int32, inverse.shape, 1)
        parts = jnp.where(lane < HEADS, high, low)[:, : 2 * HEADS]
        out[...] = (mixed[...] * dot(parts, spread_ref[...]) * gains_ref[row : row + 1, :]).astype(bf16)

    copies[1].start()
    mixed_q[...] = dot(normed[...], wq[...]).T
    for pair in range(HEADS // 2):
        heads = []
        for first in (2 * pair * HEAD_DIM, (2 * pair + 1) * HEAD_DIM):
            head = mixed_q[first : first + HEAD_DIM, :]
            total = jnp.sum(head * head, axis=0, keepdims=True)
            heads.append(head * lax.rsqrt(total * (1.0 / HEAD_DIM) + EPS) * columns_ref[...])
        rows = slice(2 * pair * HEAD_DIM, (2 * pair + 2) * HEAD_DIM)
        queries_t[rows, :] = jnp.concatenate(heads, axis=0).astype(bf16)
    copies[0].wait()
    copies[2].start()
    mixed_k[...] = dot(normed[...], wkv[0])
    head_norm(mixed_k, 1, keys)
    copies[1].wait()
    values_t[...] = dot(normed[...], wkv[1]).astype(bf16).T

    place = lax.broadcasted_iota(jnp.int32, (tokens, tokens), 0) % positions
    other = lax.broadcasted_iota(jnp.int32, (tokens, tokens), 1) % positions
    same[...] = (place == other).astype(f32)

    row = lax.broadcasted_iota(jnp.int32, (2 * LANES, tokens), 0)
    for pair in range(HEADS // 2):
        window = slice(pair * LANES, (pair + 2) * LANES)
        begin = pair * (2 * HEAD_DIM - LANES)
        query = queries_t[window, :]
        both = [
            jnp.where((row >= begin + h * HEAD_DIM) & (row < begin + (h + 1) * HEAD_DIM), query, jnp.zeros((), bf16))
            for h in range(2)
        ]
        scores = dot(keys[:, window], jnp.concatenate(both, axis=1))
        weights = []
        for h in range(2):
            part = jnp.exp2(scores[:, h * tokens : (h + 1) * tokens] * EXP2_SCALE) * same[...]
            weights.append((part * (1.0 / jnp.sum(part, axis=0, keepdims=True))).astype(bf16))
        features = slice(pair * 2 * HEAD_DIM, (pair + 1) * 2 * HEAD_DIM)
        heads_out = dot(values_t[features, :], jnp.concatenate(weights, axis=1))
        for h in range(2):
            first = (2 * pair + h) * HEAD_DIM
            attended_t[first : first + HEAD_DIM, :] = heads_out[
                h * HEAD_DIM : (h + 1) * HEAD_DIM, h * tokens : (h + 1) * tokens
            ]
    attended[...] = attended_t[...].astype(bf16).T

    copies[2].wait()
    branch = dot(attended[...], wout[...])
    o_ref[...] = (x_ref[...].astype(f32) + branch.reshape(x_ref.shape)).astype(bf16)


def body(latent, ln_gain, q_gain, k_gain, w_qkv, w_out):
    device_count = lax.axis_size("frame")
    rows, columns, model = latent.shape
    tokens = rows * columns
    per_peer = tokens // device_count
    order = [4 * i + 2 * row + core for row in range(2) for i in range(device_count // 4) for core in range(2)]
    exchange = functools.partial(
        lax.all_to_all, axis_name="frame", split_axis=0, concat_axis=0, axis_index_groups=[order], tiled=True
    )
    gathered = exchange(latent.reshape(device_count, per_peer, model))
    in_vmem = pl.BlockSpec(memory_space=pltpu.VMEM)
    in_hbm = pl.BlockSpec(memory_space=pltpu.HBM)
    bf16, f32 = jnp.bfloat16, jnp.float32
    held = [pltpu.with_memory_space_constraint(a, pltpu.HBM) for a in (ln_gain, q_gain, k_gain, w_qkv, w_out)]
    gains, columns, member, spread, wq, wkv = pl.pallas_call(
        held_kernel,
        out_shape=(
            pltpu.VMEM((8, model), f32),
            pltpu.VMEM((HEAD_DIM, LANES), f32),
            pltpu.VMEM((model, LANES), bf16),
            pltpu.VMEM((2 * HEADS, model), bf16),
            pltpu.VMEM((model, model), bf16),
            pltpu.HBM((2, model, model), bf16),
        ),
        in_specs=[in_hbm] * 4,
        out_specs=[in_vmem] * 5 + [in_hbm],
        scratch_shapes=[
            pltpu.VMEM((model,), f32),
            pltpu.VMEM((HEAD_DIM,), f32),
            pltpu.VMEM((HEAD_DIM,), f32),
            pltpu.VMEM((2, model, model), bf16),
            pltpu.SemaphoreType.DMA((8,)),
        ],
        compiler_params=pltpu.CompilerParams(vmem_limit_bytes=16 * 1024 * 1024),
        cost_estimate=pl.CostEstimate(flops=0, bytes_accessed=12 * model * model, transcendentals=0),
        name="held",
    )(*held[:4])
    result = pl.pallas_call(
        tokens_kernel,
        out_shape=jax.ShapeDtypeStruct(gathered.shape, bf16),
        in_specs=[in_vmem] * 6 + [in_hbm] * 2,
        out_specs=in_vmem,
        scratch_shapes=[
            pltpu.VMEM((2, model, model), bf16),
            pltpu.VMEM(w_out.shape, bf16),
            pltpu.VMEM((tokens, model), bf16),
            pltpu.VMEM((model, tokens), f32),
            pltpu.VMEM((tokens, model), f32),
            pltpu.VMEM((model, tokens), bf16),
            pltpu.VMEM((tokens, model), bf16),
            pltpu.VMEM((model, tokens), bf16),
            pltpu.VMEM((model, tokens), f32),
            pltpu.VMEM((tokens, model), bf16),
            pltpu.VMEM((tokens, tokens), f32),
            pltpu.SemaphoreType.DMA((3,)),
        ],
        compiler_params=pltpu.CompilerParams(vmem_limit_bytes=40 * 1024 * 1024),
        name="tokens",
    )(gathered, gains, columns, member, spread, wq, pltpu.with_memory_space_constraint(wkv, pltpu.HBM), held[4])
    return exchange(result).reshape(latent.shape)


def solution(mesh):
    placed = (P(("groups", "frame"), None, None), P(), P(), P(), P(), P())
    return jax.shard_map(
        body,
        mesh=mesh,
        in_specs=placed,
        out_specs=P(("groups", "frame"), None, None),
        check_vma=False,
    )
```

```python
import functools
import math

import jax
import jax.numpy as jnp
from jax import lax
from jax.experimental import pallas as pl
from jax.experimental.pallas import tpu as pltpu
from jax.sharding import PartitionSpec as P

HEADS = 16
HEAD_DIM = 72
LANES = 128
EPS = 1e-06
EXP2_SCALE = HEAD_DIM**-0.5 * math.log2(math.e)


def column_blocks(width):
    return [slice(i, min(i + 2 * LANES, width)) for i in range(0, width, 2 * LANES)]


def dot(a, b):
    return jnp.dot(a, b, preferred_element_type=jnp.float32)


def held_kernel(
    ln_ref, qg_ref, kg_ref, wqkv_ref, gains_out, columns_out, member_out, spread_out, wq_out, ln, qg, kg, sems
):
    width = wq_out.shape[1]
    pairs = [(ln_ref, ln), (qg_ref, qg), (kg_ref, kg), (wqkv_ref.at[:, pl.ds(0, width)], wq_out)]
    copies = [pltpu.make_async_copy(src, dst, sems.at[i]) for i, (src, dst) in enumerate(pairs)]
    for copy in copies:
        copy.start()

    def belongs(feature, lane):
        head = jnp.where(lane >= HEADS, lane - HEADS, lane)
        first = head * HEAD_DIM
        held = (feature >= first) & (feature < first + HEAD_DIM) & (lane < 2 * HEADS)
        return held.astype(jnp.float32).astype(jnp.bfloat16)

    for out, axis in ((member_out, 0), (spread_out, 1)):
        feature = lax.broadcasted_iota(jnp.int32, out.shape, axis)
        out[...] = belongs(feature, lax.broadcasted_iota(jnp.int32, out.shape, 1 - axis))
    for copy in copies[:3]:
        copy.wait()
    gains_out[0:1, :] = ln[...].reshape(1, width)
    row = jnp.concatenate([qg[...].reshape(1, HEAD_DIM), jnp.zeros((1, LANES - HEAD_DIM), jnp.float32)], axis=1)
    columns_out[...] = jnp.broadcast_to(row, (LANES, LANES)).T[:HEAD_DIM]
    gains_out[1:2, :] = jnp.concatenate([kg[...].reshape(1, HEAD_DIM)] * HEADS, axis=1)
    copies[3].wait()


def tokens_kernel(
    x_ref,
    gains_ref,
    columns_ref,
    member_ref,
    spread_ref,
    wq,
    wqkv_hbm,
    wout_hbm,
    o_ref,
    wkv,
    wout,
    normed,
    mixed_q,
    mixed_k,
    queries_t,
    keys,
    values_t,
    attended_t,
    attended,
    same,
    sems,
):
    frames, positions, width = x_ref.shape
    tokens = frames * positions
    bf16, f32 = jnp.bfloat16, jnp.float32

    pairs = [
        (wqkv_hbm.at[:, pl.ds(width, width)], wkv.at[:, pl.ds(0, width)]),
        (wqkv_hbm.at[:, pl.ds(2 * width, width)], wkv.at[:, pl.ds(width, width)]),
        (wout_hbm, wout),
    ]
    copies = [pltpu.make_async_copy(src, dst, sems.at[i]) for i, (src, dst) in enumerate(pairs)]
    copies[0].start()

    gain = gains_ref[0:1, :]
    step = max(1, 16 // positions)
    for frame in range(0, frames, step):
        x = x_ref[frame : frame + step].astype(f32).reshape(step * positions, width)
        center = x - jnp.mean(x, axis=-1, keepdims=True)
        spread = jnp.mean(center * center, axis=-1, keepdims=True)
        rows = slice(frame * positions, (frame + step) * positions)
        normed[rows, :] = (center * lax.rsqrt(spread + EPS) * gain).astype(bf16)

    def head_norm(mixed, row, out):
        squares = mixed[...] * mixed[...]
        high = squares.astype(bf16)
        low = (squares - high.astype(f32)).astype(bf16)
        total = dot(jnp.concatenate([high, low], axis=0), member_ref[...])
        total = total[:tokens] + total[tokens:]
        inverse = lax.rsqrt(total * (1.0 / HEAD_DIM) + EPS)
        high = inverse.astype(bf16)
        low = (inverse - high.astype(f32)).astype(bf16)
        lane = lax.broadcasted_iota(jnp.int32, inverse.shape, 1)
        parts = jnp.where(lane < HEADS, high, low)[:, : 2 * HEADS]
        out[...] = (mixed[...] * dot(parts, spread_ref[...]) * gains_ref[row : row + 1, :]).astype(bf16)

    copies[1].start()
    for block in column_blocks(width):
        mixed_q[block, :] = dot(normed[...], wq[:, block]).T
    for pair in range(HEADS // 2):
        heads = []
        for first in (2 * pair * HEAD_DIM, (2 * pair + 1) * HEAD_DIM):
            head = mixed_q[first : first + HEAD_DIM, :]
            total = jnp.sum(head * head, axis=0, keepdims=True)
            heads.append(head * lax.rsqrt(total * (1.0 / HEAD_DIM) + EPS) * columns_ref[...])
        rows = slice(2 * pair * HEAD_DIM, (2 * pair + 2) * HEAD_DIM)
        queries_t[rows, :] = jnp.concatenate(heads, axis=0).astype(bf16)
    copies[0].wait()
    copies[2].start()
    for block in column_blocks(width):
        mixed_k[:, block] = dot(normed[...], wkv[:, block])
    head_norm(mixed_k, 1, keys)
    copies[1].wait()
    for block in column_blocks(width):
        part = wkv[:, width + block.start : width + block.stop]
        values_t[block, :] = dot(normed[...], part).astype(bf16).T

    place = lax.broadcasted_iota(jnp.int32, (tokens, tokens), 0) % positions
    other = lax.broadcasted_iota(jnp.int32, (tokens, tokens), 1) % positions
    same[...] = (place == other).astype(f32)

    row = lax.broadcasted_iota(jnp.int32, (2 * LANES, tokens), 0)
    for pair in range(HEADS // 2):
        window = slice(pair * LANES, (pair + 2) * LANES)
        begin = pair * (2 * HEAD_DIM - LANES)
        query = queries_t[window, :]
        both = [
            jnp.where((row >= begin + h * HEAD_DIM) & (row < begin + (h + 1) * HEAD_DIM), query, jnp.zeros((), bf16))
            for h in range(2)
        ]
        scores = dot(keys[:, window], jnp.concatenate(both, axis=1))
        weights = []
        for h in range(2):
            part = jnp.exp2(scores[:, h * tokens : (h + 1) * tokens] * EXP2_SCALE) * same[...]
            weights.append((part * (1.0 / jnp.sum(part, axis=0, keepdims=True))).astype(bf16))
        features = slice(pair * 2 * HEAD_DIM, (pair + 1) * 2 * HEAD_DIM)
        heads_out = dot(values_t[features, :], jnp.concatenate(weights, axis=1))
        for h in range(2):
            first = (2 * pair + h) * HEAD_DIM
            attended_t[first : first + HEAD_DIM, :] = heads_out[
                h * HEAD_DIM : (h + 1) * HEAD_DIM, h * tokens : (h + 1) * tokens
            ]
    attended[...] = attended_t[...].astype(bf16).T

    copies[2].wait()
    for block in column_blocks(width):
        branch = dot(attended[...], wout[:, block]).reshape(frames, positions, -1)
        o_ref[:, :, block] = (x_ref[:, :, block].astype(f32) + branch).astype(bf16)


def body(latent, ln_gain, q_gain, k_gain, w_qkv, w_out):
    device_count = lax.axis_size("frame")
    rows, columns, model = latent.shape
    tokens = rows * columns
    per_peer = tokens // device_count
    order = [4 * i + 2 * row + core for row in range(2) for i in range(device_count // 4) for core in range(2)]
    exchange = functools.partial(
        lax.all_to_all, axis_name="frame", split_axis=0, concat_axis=0, axis_index_groups=[order], tiled=True
    )
    gathered = exchange(latent.reshape(device_count, per_peer, model))
    in_vmem = pl.BlockSpec(memory_space=pltpu.VMEM)
    in_hbm = pl.BlockSpec(memory_space=pltpu.HBM)
    bf16, f32 = jnp.bfloat16, jnp.float32
    held = [pltpu.with_memory_space_constraint(a, pltpu.HBM) for a in (ln_gain, q_gain, k_gain, w_qkv, w_out)]
    gains, columns, member, spread, wq = pl.pallas_call(
        held_kernel,
        out_shape=(
            pltpu.VMEM((8, model), f32),
            pltpu.VMEM((HEAD_DIM, LANES), f32),
            pltpu.VMEM((model, LANES), bf16),
            pltpu.VMEM((2 * HEADS, model), bf16),
            pltpu.VMEM((model, model), bf16),
        ),
        in_specs=[in_hbm] * 4,
        out_specs=[in_vmem] * 5,
        scratch_shapes=[
            pltpu.VMEM((model,), f32),
            pltpu.VMEM((HEAD_DIM,), f32),
            pltpu.VMEM((HEAD_DIM,), f32),
            pltpu.SemaphoreType.DMA((4,)),
        ],
        compiler_params=pltpu.CompilerParams(vmem_limit_bytes=8 * 1024 * 1024),
        cost_estimate=pl.CostEstimate(flops=0, bytes_accessed=4 * model * model, transcendentals=0),
        name="held",
    )(*held[:4])
    result = pl.pallas_call(
        tokens_kernel,
        out_shape=jax.ShapeDtypeStruct(gathered.shape, bf16),
        in_specs=[in_vmem] * 6 + [in_hbm] * 2,
        out_specs=in_vmem,
        scratch_shapes=[
            pltpu.VMEM((model, 2 * model), bf16),
            pltpu.VMEM(w_out.shape, bf16),
            pltpu.VMEM((tokens, model), bf16),
            pltpu.VMEM((model, tokens), f32),
            pltpu.VMEM((tokens, model), f32),
            pltpu.VMEM((model, tokens), bf16),
            pltpu.VMEM((tokens, model), bf16),
            pltpu.VMEM((model, tokens), bf16),
            pltpu.VMEM((model, tokens), f32),
            pltpu.VMEM((tokens, model), bf16),
            pltpu.VMEM((tokens, tokens), f32),
            pltpu.SemaphoreType.DMA((3,)),
        ],
        compiler_params=pltpu.CompilerParams(vmem_limit_bytes=40 * 1024 * 1024),
        name="tokens",
    )(gathered, gains, columns, member, spread, wq, *held[3:])
    return exchange(result).reshape(latent.shape)


def solution(mesh):
    placed = (P(("groups", "frame"), None, None), P(), P(), P(), P(), P())
    return jax.shard_map(
        body,
        mesh=mesh,
        in_specs=placed,
        out_specs=P(("groups", "frame"), None, None),
        check_vma=False,
    )
```

```python
import functools
import math

import jax
import jax.numpy as jnp
from jax import lax
from jax.experimental import pallas as pl
from jax.experimental.pallas import tpu as pltpu
from jax.sharding import PartitionSpec as P

HEADS = 16
HEAD_DIM = 72
LANES = 128
EPS = 1e-06
EXP2_SCALE = HEAD_DIM**-0.5 * math.log2(math.e)


def dot(a, b):
    return jnp.dot(a, b, preferred_element_type=jnp.float32)


def held_kernel(
    ln_ref, qg_ref, kg_ref, wqkv_ref, gains_out, columns_out, member_out, spread_out, wq_out, ln, qg, kg, sems
):
    width = wq_out.shape[1]
    pairs = [(ln_ref, ln), (qg_ref, qg), (kg_ref, kg), (wqkv_ref.at[:, pl.ds(0, width)], wq_out)]
    copies = [pltpu.make_async_copy(src, dst, sems.at[i]) for i, (src, dst) in enumerate(pairs)]
    for copy in copies:
        copy.start()

    def belongs(feature, lane):
        head = jnp.where(lane >= HEADS, lane - HEADS, lane)
        first = head * HEAD_DIM
        held = (feature >= first) & (feature < first + HEAD_DIM) & (lane < 2 * HEADS)
        return held.astype(jnp.float32).astype(jnp.bfloat16)

    for out, axis in ((member_out, 0), (spread_out, 1)):
        feature = lax.broadcasted_iota(jnp.int32, out.shape, axis)
        out[...] = belongs(feature, lax.broadcasted_iota(jnp.int32, out.shape, 1 - axis))
    for copy in copies[:3]:
        copy.wait()
    gains_out[0:1, :] = ln[...].reshape(1, width)
    row = jnp.concatenate([qg[...].reshape(1, HEAD_DIM), jnp.zeros((1, LANES - HEAD_DIM), jnp.float32)], axis=1)
    columns_out[...] = jnp.broadcast_to(row, (LANES, LANES)).T[:HEAD_DIM]
    gains_out[1:2, :] = jnp.concatenate([kg[...].reshape(1, HEAD_DIM)] * HEADS, axis=1)
    copies[3].wait()


def tokens_kernel(
    x_ref,
    gains_ref,
    columns_ref,
    member_ref,
    spread_ref,
    wq,
    wqkv_hbm,
    wout_hbm,
    o_ref,
    wkv,
    wout,
    normed,
    mixed_q,
    mixed_k,
    queries_t,
    keys,
    values_t,
    attended_t,
    attended,
    same,
    sems,
):
    frames, positions, width = x_ref.shape
    tokens = frames * positions
    bf16, f32 = jnp.bfloat16, jnp.float32

    pairs = [
        (wqkv_hbm.at[:, pl.ds(width, width)], wkv.at[:, pl.ds(0, width)]),
        (wqkv_hbm.at[:, pl.ds(2 * width, width)], wkv.at[:, pl.ds(width, width)]),
        (wout_hbm, wout),
    ]
    copies = [pltpu.make_async_copy(src, dst, sems.at[i]) for i, (src, dst) in enumerate(pairs)]
    for part, copy in enumerate(copies):
        copy.start(priority=min(part, 1))

    gain = gains_ref[0:1, :]
    step = max(1, 16 // positions)
    for frame in range(0, frames, step):
        x = x_ref[frame : frame + step].astype(f32).reshape(step * positions, width)
        center = x - jnp.mean(x, axis=-1, keepdims=True)
        spread = jnp.mean(center * center, axis=-1, keepdims=True)
        rows = slice(frame * positions, (frame + step) * positions)
        normed[rows, :] = (center * lax.rsqrt(spread + EPS) * gain).astype(bf16)

    def head_norm(mixed, row, out):
        squares = mixed[...] * mixed[...]
        high = squares.astype(bf16)
        low = (squares - high.astype(f32)).astype(bf16)
        total = dot(jnp.concatenate([high, low], axis=0), member_ref[...])
        total = total[:tokens] + total[tokens:]
        inverse = lax.rsqrt(total * (1.0 / HEAD_DIM) + EPS)
        high = inverse.astype(bf16)
        low = (inverse - high.astype(f32)).astype(bf16)
        lane = lax.broadcasted_iota(jnp.int32, inverse.shape, 1)
        parts = jnp.where(lane < HEADS, high, low)[:, : 2 * HEADS]
        out[...] = (mixed[...] * dot(parts, spread_ref[...]) * gains_ref[row : row + 1, :]).astype(bf16)

    mixed_q[...] = dot(normed[...], wq[...]).T
    for pair in range(HEADS // 2):
        heads = []
        for first in (2 * pair * HEAD_DIM, (2 * pair + 1) * HEAD_DIM):
            head = mixed_q[first : first + HEAD_DIM, :]
            total = jnp.sum(head * head, axis=0, keepdims=True)
            heads.append(head * lax.rsqrt(total * (1.0 / HEAD_DIM) + EPS) * columns_ref[...])
        rows = slice(2 * pair * HEAD_DIM, (2 * pair + 2) * HEAD_DIM)
        queries_t[rows, :] = jnp.concatenate(heads, axis=0).astype(bf16)
    copies[0].wait()
    mixed_k[...] = dot(normed[...], wkv[:, :width])
    head_norm(mixed_k, 1, keys)
    copies[1].wait()
    values_t[...] = dot(normed[...], wkv[:, width:]).astype(bf16).T

    place = lax.broadcasted_iota(jnp.int32, (tokens, tokens), 0) % positions
    other = lax.broadcasted_iota(jnp.int32, (tokens, tokens), 1) % positions
    same[...] = (place == other).astype(f32)

    row = lax.broadcasted_iota(jnp.int32, (2 * LANES, tokens), 0)
    for pair in range(HEADS // 2):
        window = slice(pair * LANES, (pair + 2) * LANES)
        begin = pair * (2 * HEAD_DIM - LANES)
        query = queries_t[window, :]
        both = [
            jnp.where((row >= begin + h * HEAD_DIM) & (row < begin + (h + 1) * HEAD_DIM), query, jnp.zeros((), bf16))
            for h in range(2)
        ]
        scores = dot(keys[:, window], jnp.concatenate(both, axis=1))
        weights = []
        for h in range(2):
            part = jnp.exp2(scores[:, h * tokens : (h + 1) * tokens] * EXP2_SCALE) * same[...]
            weights.append((part * (1.0 / jnp.sum(part, axis=0, keepdims=True))).astype(bf16))
        features = slice(pair * 2 * HEAD_DIM, (pair + 1) * 2 * HEAD_DIM)
        heads_out = dot(values_t[features, :], jnp.concatenate(weights, axis=1))
        for h in range(2):
            first = (2 * pair + h) * HEAD_DIM
            attended_t[first : first + HEAD_DIM, :] = heads_out[
                h * HEAD_DIM : (h + 1) * HEAD_DIM, h * tokens : (h + 1) * tokens
            ]
    attended[...] = attended_t[...].astype(bf16).T

    copies[2].wait()
    branch = dot(attended[...], wout[...])
    o_ref[...] = (x_ref[...].astype(f32) + branch.reshape(x_ref.shape)).astype(bf16)


def body(latent, ln_gain, q_gain, k_gain, w_qkv, w_out):
    device_count = lax.axis_size("frame")
    rows, columns, model = latent.shape
    tokens = rows * columns
    per_peer = tokens // device_count
    order = [4 * i + 2 * row + core for row in range(2) for i in range(device_count // 4) for core in range(2)]
    exchange = functools.partial(
        lax.all_to_all, axis_name="frame", split_axis=0, concat_axis=0, axis_index_groups=[order], tiled=True
    )
    gathered = exchange(latent.reshape(device_count, per_peer, model))
    in_vmem = pl.BlockSpec(memory_space=pltpu.VMEM)
    in_hbm = pl.BlockSpec(memory_space=pltpu.HBM)
    bf16, f32 = jnp.bfloat16, jnp.float32
    held = [pltpu.with_memory_space_constraint(a, pltpu.HBM) for a in (ln_gain, q_gain, k_gain, w_qkv, w_out)]
    gains, columns, member, spread, wq = pl.pallas_call(
        held_kernel,
        out_shape=(
            pltpu.VMEM((8, model), f32),
            pltpu.VMEM((HEAD_DIM, LANES), f32),
            pltpu.VMEM((model, LANES), bf16),
            pltpu.VMEM((2 * HEADS, model), bf16),
            pltpu.VMEM((model, model), bf16),
        ),
        in_specs=[in_hbm] * 4,
        out_specs=[in_vmem] * 5,
        scratch_shapes=[
            pltpu.VMEM((model,), f32),
            pltpu.VMEM((HEAD_DIM,), f32),
            pltpu.VMEM((HEAD_DIM,), f32),
            pltpu.SemaphoreType.DMA((4,)),
        ],
        compiler_params=pltpu.CompilerParams(vmem_limit_bytes=8 * 1024 * 1024),
        cost_estimate=pl.CostEstimate(flops=0, bytes_accessed=4 * model * model, transcendentals=0),
        name="held",
    )(*held[:4])
    result = pl.pallas_call(
        tokens_kernel,
        out_shape=jax.ShapeDtypeStruct(gathered.shape, bf16),
        in_specs=[in_vmem] * 6 + [in_hbm] * 2,
        out_specs=in_vmem,
        scratch_shapes=[
            pltpu.VMEM((model, 2 * model), bf16),
            pltpu.VMEM(w_out.shape, bf16),
            pltpu.VMEM((tokens, model), bf16),
            pltpu.VMEM((model, tokens), f32),
            pltpu.VMEM((tokens, model), f32),
            pltpu.VMEM((model, tokens), bf16),
            pltpu.VMEM((tokens, model), bf16),
            pltpu.VMEM((model, tokens), bf16),
            pltpu.VMEM((model, tokens), f32),
            pltpu.VMEM((tokens, model), bf16),
            pltpu.VMEM((tokens, tokens), f32),
            pltpu.SemaphoreType.DMA((3,)),
        ],
        compiler_params=pltpu.CompilerParams(vmem_limit_bytes=40 * 1024 * 1024),
        name="tokens",
    )(gathered, gains, columns, member, spread, wq, *held[3:])
    return exchange(result).reshape(latent.shape)


def solution(mesh):
    placed = (P(("groups", "frame"), None, None), P(), P(), P(), P(), P())
    return jax.shard_map(
        body,
        mesh=mesh,
        in_specs=placed,
        out_specs=P(("groups", "frame"), None, None),
        check_vma=False,
    )
```

```python
import functools
import math

import jax
import jax.numpy as jnp
from jax import lax
from jax.experimental import pallas as pl
from jax.experimental.pallas import tpu as pltpu
from jax.sharding import PartitionSpec as P

HEADS = 16
HEAD_DIM = 72
LANES = 128
EPS = 1e-06
EXP2_SCALE = HEAD_DIM**-0.5 * math.log2(math.e)


def dot(a, b):
    return jnp.dot(a, b, preferred_element_type=jnp.float32)


def held_kernel(
    ln_ref, qg_ref, kg_ref, wqkv_ref, gains_out, columns_out, member_out, spread_out, wq_out, ln, qg, kg, sems
):
    width = wq_out.shape[1]
    pairs = [(ln_ref, ln), (qg_ref, qg), (kg_ref, kg), (wqkv_ref.at[:, pl.ds(0, width)], wq_out)]
    copies = [pltpu.make_async_copy(src, dst, sems.at[i]) for i, (src, dst) in enumerate(pairs)]
    for copy in copies:
        copy.start()

    def belongs(feature, lane):
        head = jnp.where(lane >= HEADS, lane - HEADS, lane)
        first = head * HEAD_DIM
        held = (feature >= first) & (feature < first + HEAD_DIM) & (lane < 2 * HEADS)
        return held.astype(jnp.float32).astype(jnp.bfloat16)

    for out, axis in ((member_out, 0), (spread_out, 1)):
        feature = lax.broadcasted_iota(jnp.int32, out.shape, axis)
        out[...] = belongs(feature, lax.broadcasted_iota(jnp.int32, out.shape, 1 - axis))
    for copy in copies[:3]:
        copy.wait()
    gains_out[0:1, :] = ln[...].reshape(1, width)
    row = jnp.concatenate([qg[...].reshape(1, HEAD_DIM), jnp.zeros((1, LANES - HEAD_DIM), jnp.float32)], axis=1)
    columns_out[...] = jnp.broadcast_to(row, (LANES, LANES)).T[:HEAD_DIM]
    gains_out[1:2, :] = jnp.concatenate([kg[...].reshape(1, HEAD_DIM)] * HEADS, axis=1)
    copies[3].wait()


def tokens_kernel(
    x_ref,
    gains_ref,
    columns_ref,
    member_ref,
    spread_ref,
    wq,
    wqkv_hbm,
    wout_hbm,
    o_ref,
    wkv,
    wout,
    normed,
    mixed_q,
    mixed_k,
    queries_t,
    keys,
    values_t,
    attended_t,
    attended,
    same,
    sems,
):
    frames, positions, width = x_ref.shape
    tokens = frames * positions
    bf16, f32 = jnp.bfloat16, jnp.float32

    pairs = [
        (wqkv_hbm.at[:, pl.ds(width, width)], wkv.at[:, pl.ds(0, width)]),
        (wqkv_hbm.at[:, pl.ds(2 * width, width)], wkv.at[:, pl.ds(width, width)]),
        (wout_hbm, wout),
    ]
    copies = [pltpu.make_async_copy(src, dst, sems.at[i]) for i, (src, dst) in enumerate(pairs)]
    for part, copy in enumerate(copies):
        copy.start(priority=int(part == 0))

    gain = gains_ref[0:1, :]
    step = max(1, 16 // positions)
    for frame in range(0, frames, step):
        x = x_ref[frame : frame + step].astype(f32).reshape(step * positions, width)
        center = x - jnp.mean(x, axis=-1, keepdims=True)
        spread = jnp.mean(center * center, axis=-1, keepdims=True)
        rows = slice(frame * positions, (frame + step) * positions)
        normed[rows, :] = (center * lax.rsqrt(spread + EPS) * gain).astype(bf16)

    def head_norm(mixed, row, out):
        squares = mixed[...] * mixed[...]
        high = squares.astype(bf16)
        low = (squares - high.astype(f32)).astype(bf16)
        total = dot(jnp.concatenate([high, low], axis=0), member_ref[...])
        total = total[:tokens] + total[tokens:]
        inverse = lax.rsqrt(total * (1.0 / HEAD_DIM) + EPS)
        high = inverse.astype(bf16)
        low = (inverse - high.astype(f32)).astype(bf16)
        lane = lax.broadcasted_iota(jnp.int32, inverse.shape, 1)
        parts = jnp.where(lane < HEADS, high, low)[:, : 2 * HEADS]
        out[...] = (mixed[...] * dot(parts, spread_ref[...]) * gains_ref[row : row + 1, :]).astype(bf16)

    mixed_q[...] = dot(normed[...], wq[...]).T
    for pair in range(HEADS // 2):
        heads = []
        for first in (2 * pair * HEAD_DIM, (2 * pair + 1) * HEAD_DIM):
            head = mixed_q[first : first + HEAD_DIM, :]
            total = jnp.sum(head * head, axis=0, keepdims=True)
            heads.append(head * lax.rsqrt(total * (1.0 / HEAD_DIM) + EPS) * columns_ref[...])
        rows = slice(2 * pair * HEAD_DIM, (2 * pair + 2) * HEAD_DIM)
        queries_t[rows, :] = jnp.concatenate(heads, axis=0).astype(bf16)
    copies[0].wait()
    mixed_k[...] = dot(normed[...], wkv[:, :width])
    head_norm(mixed_k, 1, keys)
    copies[1].wait()
    values_t[...] = dot(normed[...], wkv[:, width:]).astype(bf16).T

    place = lax.broadcasted_iota(jnp.int32, (tokens, tokens), 0) % positions
    other = lax.broadcasted_iota(jnp.int32, (tokens, tokens), 1) % positions
    same[...] = (place == other).astype(f32)

    row = lax.broadcasted_iota(jnp.int32, (2 * LANES, tokens), 0)
    for pair in range(HEADS // 2):
        window = slice(pair * LANES, (pair + 2) * LANES)
        begin = pair * (2 * HEAD_DIM - LANES)
        query = queries_t[window, :]
        both = [
            jnp.where((row >= begin + h * HEAD_DIM) & (row < begin + (h + 1) * HEAD_DIM), query, jnp.zeros((), bf16))
            for h in range(2)
        ]
        scores = dot(keys[:, window], jnp.concatenate(both, axis=1))
        weights = []
        for h in range(2):
            part = jnp.exp2(scores[:, h * tokens : (h + 1) * tokens] * EXP2_SCALE) * same[...]
            weights.append((part * (1.0 / jnp.sum(part, axis=0, keepdims=True))).astype(bf16))
        features = slice(pair * 2 * HEAD_DIM, (pair + 1) * 2 * HEAD_DIM)
        heads_out = dot(values_t[features, :], jnp.concatenate(weights, axis=1))
        for h in range(2):
            first = (2 * pair + h) * HEAD_DIM
            attended_t[first : first + HEAD_DIM, :] = heads_out[
                h * HEAD_DIM : (h + 1) * HEAD_DIM, h * tokens : (h + 1) * tokens
            ]
    attended[...] = attended_t[...].astype(bf16).T

    copies[2].wait()
    branch = dot(attended[...], wout[...])
    o_ref[...] = (x_ref[...].astype(f32) + branch.reshape(x_ref.shape)).astype(bf16)


def body(latent, ln_gain, q_gain, k_gain, w_qkv, w_out):
    device_count = lax.axis_size("frame")
    rows, columns, model = latent.shape
    tokens = rows * columns
    per_peer = tokens // device_count
    order = [4 * i + 2 * row + core for row in range(2) for i in range(device_count // 4) for core in range(2)]
    exchange = functools.partial(
        lax.all_to_all, axis_name="frame", split_axis=0, concat_axis=0, axis_index_groups=[order], tiled=True
    )
    gathered = exchange(latent.reshape(device_count, per_peer, model))
    in_vmem = pl.BlockSpec(memory_space=pltpu.VMEM)
    in_hbm = pl.BlockSpec(memory_space=pltpu.HBM)
    bf16, f32 = jnp.bfloat16, jnp.float32
    held = [pltpu.with_memory_space_constraint(a, pltpu.HBM) for a in (ln_gain, q_gain, k_gain, w_qkv, w_out)]
    gains, columns, member, spread, wq = pl.pallas_call(
        held_kernel,
        out_shape=(
            pltpu.VMEM((8, model), f32),
            pltpu.VMEM((HEAD_DIM, LANES), f32),
            pltpu.VMEM((model, LANES), bf16),
            pltpu.VMEM((2 * HEADS, model), bf16),
            pltpu.VMEM((model, model), bf16),
        ),
        in_specs=[in_hbm] * 4,
        out_specs=[in_vmem] * 5,
        scratch_shapes=[
            pltpu.VMEM((model,), f32),
            pltpu.VMEM((HEAD_DIM,), f32),
            pltpu.VMEM((HEAD_DIM,), f32),
            pltpu.SemaphoreType.DMA((4,)),
        ],
        compiler_params=pltpu.CompilerParams(vmem_limit_bytes=8 * 1024 * 1024),
        cost_estimate=pl.CostEstimate(flops=0, bytes_accessed=4 * model * model, transcendentals=0),
        name="held",
    )(*held[:4])
    result = pl.pallas_call(
        tokens_kernel,
        out_shape=jax.ShapeDtypeStruct(gathered.shape, bf16),
        in_specs=[in_vmem] * 6 + [in_hbm] * 2,
        out_specs=in_vmem,
        scratch_shapes=[
            pltpu.VMEM((model, 2 * model), bf16),
            pltpu.VMEM(w_out.shape, bf16),
            pltpu.VMEM((tokens, model), bf16),
            pltpu.VMEM((model, tokens), f32),
            pltpu.VMEM((tokens, model), f32),
            pltpu.VMEM((model, tokens), bf16),
            pltpu.VMEM((tokens, model), bf16),
            pltpu.VMEM((model, tokens), bf16),
            pltpu.VMEM((model, tokens), f32),
            pltpu.VMEM((tokens, model), bf16),
            pltpu.VMEM((tokens, tokens), f32),
            pltpu.SemaphoreType.DMA((3,)),
        ],
        compiler_params=pltpu.CompilerParams(vmem_limit_bytes=40 * 1024 * 1024),
        name="tokens",
    )(gathered, gains, columns, member, spread, wq, *held[3:])
    return exchange(result).reshape(latent.shape)


def solution(mesh):
    placed = (P(("groups", "frame"), None, None), P(), P(), P(), P(), P())
    return jax.shard_map(
        body,
        mesh=mesh,
        in_specs=placed,
        out_specs=P(("groups", "frame"), None, None),
        check_vma=False,
    )
```

```python
import functools
import math

import jax
import jax.numpy as jnp
from jax import lax
from jax.experimental import pallas as pl
from jax.experimental.pallas import tpu as pltpu
from jax.sharding import PartitionSpec as P

HEADS = 16
HEAD_DIM = 72
LANES = 128
EPS = 1e-06
EXP2_SCALE = HEAD_DIM**-0.5 * math.log2(math.e)


def dot(a, b):
    return jnp.dot(a, b, preferred_element_type=jnp.float32)


def held_kernel(
    ln_ref, qg_ref, kg_ref, wqkv_ref, gains_out, columns_out, member_out, spread_out, wq_out, ln, qg, kg, sems
):
    width = wq_out.shape[1]
    pairs = [(ln_ref, ln), (qg_ref, qg), (kg_ref, kg), (wqkv_ref.at[:, pl.ds(0, width)], wq_out)]
    copies = [pltpu.make_async_copy(src, dst, sems.at[i]) for i, (src, dst) in enumerate(pairs)]
    for copy in copies:
        copy.start()

    def belongs(feature, lane):
        head = jnp.where(lane >= HEADS, lane - HEADS, lane)
        first = head * HEAD_DIM
        held = (feature >= first) & (feature < first + HEAD_DIM) & (lane < 2 * HEADS)
        return held.astype(jnp.float32).astype(jnp.bfloat16)

    for out, axis in ((member_out, 0), (spread_out, 1)):
        feature = lax.broadcasted_iota(jnp.int32, out.shape, axis)
        out[...] = belongs(feature, lax.broadcasted_iota(jnp.int32, out.shape, 1 - axis))
    for copy in copies[:3]:
        copy.wait()
    gains_out[0:1, :] = ln[...].reshape(1, width)
    row = jnp.concatenate([qg[...].reshape(1, HEAD_DIM), jnp.zeros((1, LANES - HEAD_DIM), jnp.float32)], axis=1)
    columns_out[...] = jnp.broadcast_to(row, (LANES, LANES)).T[:HEAD_DIM]
    gains_out[1:2, :] = jnp.concatenate([kg[...].reshape(1, HEAD_DIM)] * HEADS, axis=1)
    copies[3].wait()


def tokens_kernel(
    x_ref,
    gains_ref,
    columns_ref,
    member_ref,
    spread_ref,
    wq,
    wqkv_hbm,
    wout_hbm,
    o_ref,
    wkv,
    wout,
    normed,
    mixed_q,
    mixed_k,
    queries_t,
    keys,
    values_t,
    attended_t,
    attended,
    same,
    sems,
):
    frames, positions, width = x_ref.shape
    tokens = frames * positions
    bf16, f32 = jnp.bfloat16, jnp.float32

    pairs = [
        (wqkv_hbm.at[:, pl.ds(width, width)], wkv.at[:, pl.ds(0, width)]),
        (wqkv_hbm.at[:, pl.ds(2 * width, width)], wkv.at[:, pl.ds(width, width)]),
        (wout_hbm, wout),
    ]
    copies = [pltpu.make_async_copy(src, dst, sems.at[i]) for i, (src, dst) in enumerate(pairs)]
    copies[0].start()
    copies[2].start(priority=1)

    gain = gains_ref[0:1, :]
    step = max(1, 16 // positions)
    for frame in range(0, frames, step):
        x = x_ref[frame : frame + step].astype(f32).reshape(step * positions, width)
        center = x - jnp.mean(x, axis=-1, keepdims=True)
        spread = jnp.mean(center * center, axis=-1, keepdims=True)
        rows = slice(frame * positions, (frame + step) * positions)
        normed[rows, :] = (center * lax.rsqrt(spread + EPS) * gain).astype(bf16)

    def head_norm(mixed, row, out):
        squares = mixed[...] * mixed[...]
        high = squares.astype(bf16)
        low = (squares - high.astype(f32)).astype(bf16)
        total = dot(jnp.concatenate([high, low], axis=0), member_ref[...])
        total = total[:tokens] + total[tokens:]
        inverse = lax.rsqrt(total * (1.0 / HEAD_DIM) + EPS)
        high = inverse.astype(bf16)
        low = (inverse - high.astype(f32)).astype(bf16)
        lane = lax.broadcasted_iota(jnp.int32, inverse.shape, 1)
        parts = jnp.where(lane < HEADS, high, low)[:, : 2 * HEADS]
        out[...] = (mixed[...] * dot(parts, spread_ref[...]) * gains_ref[row : row + 1, :]).astype(bf16)

    copies[1].start()
    mixed_q[...] = dot(normed[...], wq[...]).T
    for pair in range(HEADS // 2):
        heads = []
        for first in (2 * pair * HEAD_DIM, (2 * pair + 1) * HEAD_DIM):
            head = mixed_q[first : first + HEAD_DIM, :]
            total = jnp.sum(head * head, axis=0, keepdims=True)
            heads.append(head * lax.rsqrt(total * (1.0 / HEAD_DIM) + EPS) * columns_ref[...])
        rows = slice(2 * pair * HEAD_DIM, (2 * pair + 2) * HEAD_DIM)
        queries_t[rows, :] = jnp.concatenate(heads, axis=0).astype(bf16)
    copies[0].wait()
    mixed_k[...] = dot(normed[...], wkv[:, :width])
    head_norm(mixed_k, 1, keys)
    copies[1].wait()
    values_t[...] = dot(normed[...], wkv[:, width:]).astype(bf16).T

    place = lax.broadcasted_iota(jnp.int32, (tokens, tokens), 0) % positions
    other = lax.broadcasted_iota(jnp.int32, (tokens, tokens), 1) % positions
    same[...] = (place == other).astype(f32)

    row = lax.broadcasted_iota(jnp.int32, (2 * LANES, tokens), 0)
    for pair in range(HEADS // 2):
        window = slice(pair * LANES, (pair + 2) * LANES)
        begin = pair * (2 * HEAD_DIM - LANES)
        query = queries_t[window, :]
        both = [
            jnp.where((row >= begin + h * HEAD_DIM) & (row < begin + (h + 1) * HEAD_DIM), query, jnp.zeros((), bf16))
            for h in range(2)
        ]
        scores = dot(keys[:, window], jnp.concatenate(both, axis=1))
        weights = []
        for h in range(2):
            part = jnp.exp2(scores[:, h * tokens : (h + 1) * tokens] * EXP2_SCALE) * same[...]
            weights.append((part * (1.0 / jnp.sum(part, axis=0, keepdims=True))).astype(bf16))
        features = slice(pair * 2 * HEAD_DIM, (pair + 1) * 2 * HEAD_DIM)
        heads_out = dot(values_t[features, :], jnp.concatenate(weights, axis=1))
        for h in range(2):
            first = (2 * pair + h) * HEAD_DIM
            attended_t[first : first + HEAD_DIM, :] = heads_out[
                h * HEAD_DIM : (h + 1) * HEAD_DIM, h * tokens : (h + 1) * tokens
            ]
    attended[...] = attended_t[...].astype(bf16).T

    copies[2].wait()
    branch = dot(attended[...], wout[...])
    o_ref[...] = (x_ref[...].astype(f32) + branch.reshape(x_ref.shape)).astype(bf16)


def body(latent, ln_gain, q_gain, k_gain, w_qkv, w_out):
    device_count = lax.axis_size("frame")
    rows, columns, model = latent.shape
    tokens = rows * columns
    per_peer = tokens // device_count
    order = [4 * i + 2 * row + core for row in range(2) for i in range(device_count // 4) for core in range(2)]
    exchange = functools.partial(
        lax.all_to_all, axis_name="frame", split_axis=0, concat_axis=0, axis_index_groups=[order], tiled=True
    )
    gathered = exchange(latent.reshape(device_count, per_peer, model))
    in_vmem = pl.BlockSpec(memory_space=pltpu.VMEM)
    in_hbm = pl.BlockSpec(memory_space=pltpu.HBM)
    bf16, f32 = jnp.bfloat16, jnp.float32
    held = [pltpu.with_memory_space_constraint(a, pltpu.HBM) for a in (ln_gain, q_gain, k_gain, w_qkv, w_out)]
    gains, columns, member, spread, wq = pl.pallas_call(
        held_kernel,
        out_shape=(
            pltpu.VMEM((8, model), f32),
            pltpu.VMEM((HEAD_DIM, LANES), f32),
            pltpu.VMEM((model, LANES), bf16),
            pltpu.VMEM((2 * HEADS, model), bf16),
            pltpu.VMEM((model, model), bf16),
        ),
        in_specs=[in_hbm] * 4,
        out_specs=[in_vmem] * 5,
        scratch_shapes=[
            pltpu.VMEM((model,), f32),
            pltpu.VMEM((HEAD_DIM,), f32),
            pltpu.VMEM((HEAD_DIM,), f32),
            pltpu.SemaphoreType.DMA((4,)),
        ],
        compiler_params=pltpu.CompilerParams(vmem_limit_bytes=8 * 1024 * 1024),
        cost_estimate=pl.CostEstimate(flops=0, bytes_accessed=4 * model * model, transcendentals=0),
        name="held",
    )(*held[:4])
    result = pl.pallas_call(
        tokens_kernel,
        out_shape=jax.ShapeDtypeStruct(gathered.shape, bf16),
        in_specs=[in_vmem] * 6 + [in_hbm] * 2,
        out_specs=in_vmem,
        scratch_shapes=[
            pltpu.VMEM((model, 2 * model), bf16),
            pltpu.VMEM(w_out.shape, bf16),
            pltpu.VMEM((tokens, model), bf16),
            pltpu.VMEM((model, tokens), f32),
            pltpu.VMEM((tokens, model), f32),
            pltpu.VMEM((model, tokens), bf16),
            pltpu.VMEM((tokens, model), bf16),
            pltpu.VMEM((model, tokens), bf16),
            pltpu.VMEM((model, tokens), f32),
            pltpu.VMEM((tokens, model), bf16),
            pltpu.VMEM((tokens, tokens), f32),
            pltpu.SemaphoreType.DMA((3,)),
        ],
        compiler_params=pltpu.CompilerParams(vmem_limit_bytes=40 * 1024 * 1024),
        name="tokens",
    )(gathered, gains, columns, member, spread, wq, *held[3:])
    return exchange(result).reshape(latent.shape)


def solution(mesh):
    placed = (P(("groups", "frame"), None, None), P(), P(), P(), P(), P())
    return jax.shard_map(
        body,
        mesh=mesh,
        in_specs=placed,
        out_specs=P(("groups", "frame"), None, None),
        check_vma=False,
    )
```

```python
import functools
import math

import jax
import jax.numpy as jnp
from jax import lax
from jax.experimental import pallas as pl
from jax.experimental.pallas import tpu as pltpu
from jax.sharding import PartitionSpec as P

HEADS = 16
HEAD_DIM = 72
LANES = 128
EPS = 1e-06
EXP2_SCALE = HEAD_DIM**-0.5 * math.log2(math.e)


def dot(a, b):
    return jnp.dot(a, b, preferred_element_type=jnp.float32)


def held_kernel(
    ln_ref, qg_ref, kg_ref, wqkv_ref, gains_out, columns_out, member_out, spread_out, wq_out, ln, qg, kg, sems
):
    width = wq_out.shape[1]
    pairs = [(ln_ref, ln), (qg_ref, qg), (kg_ref, kg), (wqkv_ref.at[:, pl.ds(0, width)], wq_out)]
    copies = [pltpu.make_async_copy(src, dst, sems.at[i]) for i, (src, dst) in enumerate(pairs)]
    for copy in copies:
        copy.start()

    def belongs(feature, lane):
        head = jnp.where(lane >= HEADS, lane - HEADS, lane)
        first = head * HEAD_DIM
        held = (feature >= first) & (feature < first + HEAD_DIM) & (lane < 2 * HEADS)
        return held.astype(jnp.float32).astype(jnp.bfloat16)

    for out, axis in ((member_out, 0), (spread_out, 1)):
        feature = lax.broadcasted_iota(jnp.int32, out.shape, axis)
        out[...] = belongs(feature, lax.broadcasted_iota(jnp.int32, out.shape, 1 - axis))
    for copy in copies[:3]:
        copy.wait()
    gains_out[0:1, :] = ln[...].reshape(1, width)
    row = jnp.concatenate([qg[...].reshape(1, HEAD_DIM), jnp.zeros((1, LANES - HEAD_DIM), jnp.float32)], axis=1)
    columns_out[...] = jnp.broadcast_to(row, (LANES, LANES)).T[:HEAD_DIM]
    gains_out[1:2, :] = jnp.concatenate([kg[...].reshape(1, HEAD_DIM)] * HEADS, axis=1)
    copies[3].wait()


def tokens_kernel(
    x_ref,
    gains_ref,
    columns_ref,
    member_ref,
    spread_ref,
    wq,
    wqkv_hbm,
    wout_hbm,
    o_ref,
    wkv,
    wout,
    normed,
    mixed_q,
    mixed_k,
    queries_t,
    keys,
    values_t,
    attended_t,
    attended,
    branch,
    same,
    sems,
):
    frames, positions, width = x_ref.shape
    tokens = frames * positions
    bf16, f32 = jnp.bfloat16, jnp.float32

    pairs = [
        (wqkv_hbm.at[:, pl.ds(width, width)], wkv.at[:, pl.ds(0, width)]),
        (wqkv_hbm.at[:, pl.ds(2 * width, width)], wkv.at[:, pl.ds(width, width)]),
        (wout_hbm, wout),
    ]
    copies = [pltpu.make_async_copy(src, dst, sems.at[i]) for i, (src, dst) in enumerate(pairs)]
    copies[0].start()
    copies[2].start(priority=1)

    gain = gains_ref[0:1, :]
    step = max(1, 16 // positions)
    for frame in range(0, frames, step):
        x = x_ref[frame : frame + step].astype(f32).reshape(step * positions, width)
        center = x - jnp.mean(x, axis=-1, keepdims=True)
        spread = jnp.mean(center * center, axis=-1, keepdims=True)
        rows = slice(frame * positions, (frame + step) * positions)
        normed[rows, :] = (center * lax.rsqrt(spread + EPS) * gain).astype(bf16)

    def head_norm(mixed, row, out):
        squares = mixed[...] * mixed[...]
        high = squares.astype(bf16)
        low = (squares - high.astype(f32)).astype(bf16)
        total = dot(jnp.concatenate([high, low], axis=0), member_ref[...])
        total = total[:tokens] + total[tokens:]
        inverse = lax.rsqrt(total * (1.0 / HEAD_DIM) + EPS)
        high = inverse.astype(bf16)
        low = (inverse - high.astype(f32)).astype(bf16)
        lane = lax.broadcasted_iota(jnp.int32, inverse.shape, 1)
        parts = jnp.where(lane < HEADS, high, low)[:, : 2 * HEADS]
        out[...] = (mixed[...] * dot(parts, spread_ref[...]) * gains_ref[row : row + 1, :]).astype(bf16)

    copies[1].start()
    mixed_q[...] = dot(normed[...], wq[...]).T
    for pair in range(HEADS // 2):
        heads = []
        for first in (2 * pair * HEAD_DIM, (2 * pair + 1) * HEAD_DIM):
            head = mixed_q[first : first + HEAD_DIM, :]
            total = jnp.sum(head * head, axis=0, keepdims=True)
            heads.append(head * lax.rsqrt(total * (1.0 / HEAD_DIM) + EPS) * columns_ref[...])
        rows = slice(2 * pair * HEAD_DIM, (2 * pair + 2) * HEAD_DIM)
        queries_t[rows, :] = jnp.concatenate(heads, axis=0).astype(bf16)
    copies[0].wait()
    mixed_k[...] = dot(normed[...], wkv[:, :width])
    head_norm(mixed_k, 1, keys)
    copies[1].wait()
    values_t[...] = dot(normed[...], wkv[:, width:]).astype(bf16).T

    place = lax.broadcasted_iota(jnp.int32, (tokens, tokens), 0) % positions
    other = lax.broadcasted_iota(jnp.int32, (tokens, tokens), 1) % positions
    same[...] = (place == other).astype(f32)

    row = lax.broadcasted_iota(jnp.int32, (2 * LANES, tokens), 0)
    done = HEADS // 4 * LANES
    for pair in range(HEADS // 2):
        if pair == HEADS // 4:
            copies[2].wait()
            attended[:, :done] = attended_t[:done, :].astype(bf16).T
            branch[...] = dot(attended[:, :done], wout[:done, :])
        window = slice(pair * LANES, (pair + 2) * LANES)
        begin = pair * (2 * HEAD_DIM - LANES)
        query = queries_t[window, :]
        both = [
            jnp.where((row >= begin + h * HEAD_DIM) & (row < begin + (h + 1) * HEAD_DIM), query, jnp.zeros((), bf16))
            for h in range(2)
        ]
        scores = dot(keys[:, window], jnp.concatenate(both, axis=1))
        weights = []
        for h in range(2):
            part = jnp.exp2(scores[:, h * tokens : (h + 1) * tokens] * EXP2_SCALE) * same[...]
            weights.append((part * (1.0 / jnp.sum(part, axis=0, keepdims=True))).astype(bf16))
        features = slice(pair * 2 * HEAD_DIM, (pair + 1) * 2 * HEAD_DIM)
        heads_out = dot(values_t[features, :], jnp.concatenate(weights, axis=1))
        for h in range(2):
            first = (2 * pair + h) * HEAD_DIM
            attended_t[first : first + HEAD_DIM, :] = heads_out[
                h * HEAD_DIM : (h + 1) * HEAD_DIM, h * tokens : (h + 1) * tokens
            ]
    attended[:, done:] = attended_t[done:, :].astype(bf16).T
    total = branch[...] + dot(attended[:, done:], wout[done:, :])
    o_ref[...] = (x_ref[...].astype(f32) + total.reshape(x_ref.shape)).astype(bf16)


def body(latent, ln_gain, q_gain, k_gain, w_qkv, w_out):
    device_count = lax.axis_size("frame")
    rows, columns, model = latent.shape
    tokens = rows * columns
    per_peer = tokens // device_count
    order = [4 * i + 2 * row + core for row in range(2) for i in range(device_count // 4) for core in range(2)]
    exchange = functools.partial(
        lax.all_to_all, axis_name="frame", split_axis=0, concat_axis=0, axis_index_groups=[order], tiled=True
    )
    gathered = exchange(latent.reshape(device_count, per_peer, model))
    in_vmem = pl.BlockSpec(memory_space=pltpu.VMEM)
    in_hbm = pl.BlockSpec(memory_space=pltpu.HBM)
    bf16, f32 = jnp.bfloat16, jnp.float32
    held = [pltpu.with_memory_space_constraint(a, pltpu.HBM) for a in (ln_gain, q_gain, k_gain, w_qkv, w_out)]
    gains, columns, member, spread, wq = pl.pallas_call(
        held_kernel,
        out_shape=(
            pltpu.VMEM((8, model), f32),
            pltpu.VMEM((HEAD_DIM, LANES), f32),
            pltpu.VMEM((model, LANES), bf16),
            pltpu.VMEM((2 * HEADS, model), bf16),
            pltpu.VMEM((model, model), bf16),
        ),
        in_specs=[in_hbm] * 4,
        out_specs=[in_vmem] * 5,
        scratch_shapes=[
            pltpu.VMEM((model,), f32),
            pltpu.VMEM((HEAD_DIM,), f32),
            pltpu.VMEM((HEAD_DIM,), f32),
            pltpu.SemaphoreType.DMA((4,)),
        ],
        compiler_params=pltpu.CompilerParams(vmem_limit_bytes=8 * 1024 * 1024),
        cost_estimate=pl.CostEstimate(flops=0, bytes_accessed=4 * model * model, transcendentals=0),
        name="held",
    )(*held[:4])
    result = pl.pallas_call(
        tokens_kernel,
        out_shape=jax.ShapeDtypeStruct(gathered.shape, bf16),
        in_specs=[in_vmem] * 6 + [in_hbm] * 2,
        out_specs=in_vmem,
        scratch_shapes=[
            pltpu.VMEM((model, 2 * model), bf16),
            pltpu.VMEM(w_out.shape, bf16),
            pltpu.VMEM((tokens, model), bf16),
            pltpu.VMEM((model, tokens), f32),
            pltpu.VMEM((tokens, model), f32),
            pltpu.VMEM((model, tokens), bf16),
            pltpu.VMEM((tokens, model), bf16),
            pltpu.VMEM((model, tokens), bf16),
            pltpu.VMEM((model, tokens), f32),
            pltpu.VMEM((tokens, model), bf16),
            pltpu.VMEM((tokens, model), f32),
            pltpu.VMEM((tokens, tokens), f32),
            pltpu.SemaphoreType.DMA((3,)),
        ],
        compiler_params=pltpu.CompilerParams(vmem_limit_bytes=40 * 1024 * 1024),
        name="tokens",
    )(gathered, gains, columns, member, spread, wq, *held[3:])
    return exchange(result).reshape(latent.shape)


def solution(mesh):
    placed = (P(("groups", "frame"), None, None), P(), P(), P(), P(), P())
    return jax.shard_map(
        body,
        mesh=mesh,
        in_specs=placed,
        out_specs=P(("groups", "frame"), None, None),
        check_vma=False,
    )
```

```python
import functools
import math

import jax
import jax.numpy as jnp
from jax import lax
from jax.experimental import pallas as pl
from jax.experimental.pallas import tpu as pltpu
from jax.sharding import PartitionSpec as P

HEADS = 16
HEAD_DIM = 72
LANES = 128
EPS = 1e-06
EXP2_SCALE = HEAD_DIM**-0.5 * math.log2(math.e)


def dot(a, b):
    return jnp.dot(a, b, preferred_element_type=jnp.float32)


def held_kernel(
    ln_ref, qg_ref, kg_ref, wqkv_ref, gains_out, columns_out, member_out, spread_out, wq_out, ln, qg, kg, sems
):
    width = wq_out.shape[1]
    pairs = [(ln_ref, ln), (qg_ref, qg), (kg_ref, kg), (wqkv_ref.at[:, pl.ds(0, width)], wq_out)]
    copies = [pltpu.make_async_copy(src, dst, sems.at[i]) for i, (src, dst) in enumerate(pairs)]
    for copy in copies:
        copy.start()

    def belongs(feature, lane):
        head = jnp.where(lane >= HEADS, lane - HEADS, lane)
        first = head * HEAD_DIM
        held = (feature >= first) & (feature < first + HEAD_DIM) & (lane < 2 * HEADS)
        return held.astype(jnp.float32).astype(jnp.bfloat16)

    for out, axis in ((member_out, 0), (spread_out, 1)):
        feature = lax.broadcasted_iota(jnp.int32, out.shape, axis)
        out[...] = belongs(feature, lax.broadcasted_iota(jnp.int32, out.shape, 1 - axis))
    for copy in copies[:3]:
        copy.wait()
    gains_out[0:1, :] = ln[...].reshape(1, width)
    row = jnp.concatenate([qg[...].reshape(1, HEAD_DIM), jnp.zeros((1, LANES - HEAD_DIM), jnp.float32)], axis=1)
    columns_out[...] = jnp.broadcast_to(row, (LANES, LANES)).T[:HEAD_DIM]
    gains_out[1:2, :] = jnp.concatenate([kg[...].reshape(1, HEAD_DIM)] * HEADS, axis=1)
    copies[3].wait()


def tokens_kernel(
    x_ref,
    gains_ref,
    columns_ref,
    member_ref,
    spread_ref,
    wq,
    wqkv_hbm,
    wout_hbm,
    o_ref,
    wkv,
    wout,
    normed,
    mixed_q,
    mixed_k,
    queries_t,
    keys,
    values_t,
    attended_t,
    attended,
    same,
    sems,
):
    frames, positions, width = x_ref.shape
    tokens = frames * positions
    bf16, f32 = jnp.bfloat16, jnp.float32

    pairs = [
        (wqkv_hbm.at[:, pl.ds(width, width)], wkv.at[:, pl.ds(0, width)]),
        (wqkv_hbm.at[:, pl.ds(2 * width, width)], wkv.at[:, pl.ds(width, width)]),
        (wout_hbm, wout),
    ]
    copies = [pltpu.make_async_copy(src, dst, sems.at[i]) for i, (src, dst) in enumerate(pairs)]
    copies[0].start()

    gain = gains_ref[0:1, :]
    step = max(1, 16 // positions)
    for frame in range(0, frames, step):
        x = x_ref[frame : frame + step].astype(f32).reshape(step * positions, width)
        center = x - jnp.mean(x, axis=-1, keepdims=True)
        spread = jnp.mean(center * center, axis=-1, keepdims=True)
        rows = slice(frame * positions, (frame + step) * positions)
        normed[rows, :] = (center * lax.rsqrt(spread + EPS) * gain).astype(bf16)

    def head_norm(mixed, row, out):
        squares = mixed[...] * mixed[...]
        high = squares.astype(bf16)
        low = (squares - high.astype(f32)).astype(bf16)
        total = dot(jnp.concatenate([high, low], axis=0), member_ref[...])
        total = total[:tokens] + total[tokens:]
        inverse = lax.rsqrt(total * (1.0 / HEAD_DIM) + EPS)
        high = inverse.astype(bf16)
        low = (inverse - high.astype(f32)).astype(bf16)
        lane = lax.broadcasted_iota(jnp.int32, inverse.shape, 1)
        parts = jnp.where(lane < HEADS, high, low)[:, : 2 * HEADS]
        out[...] = (mixed[...] * dot(parts, spread_ref[...]) * gains_ref[row : row + 1, :]).astype(bf16)

    copies[1].start()
    mixed_q[...] = dot(normed[...], wq[...]).T
    for pair in range(HEADS // 2):
        heads = []
        for first in (2 * pair * HEAD_DIM, (2 * pair + 1) * HEAD_DIM):
            head = mixed_q[first : first + HEAD_DIM, :]
            total = jnp.sum(head * head, axis=0, keepdims=True)
            heads.append(head * lax.rsqrt(total * (1.0 / HEAD_DIM) + EPS) * columns_ref[...])
        rows = slice(2 * pair * HEAD_DIM, (2 * pair + 2) * HEAD_DIM)
        queries_t[rows, :] = jnp.concatenate(heads, axis=0).astype(bf16)
    copies[0].wait()
    copies[2].start()
    mixed_k[...] = dot(normed[...], wkv[:, :width])
    head_norm(mixed_k, 1, keys)
    copies[1].wait()
    values_t[...] = dot(normed[...], wkv[:, width:]).astype(bf16).T

    place = lax.broadcasted_iota(jnp.int32, (tokens, tokens), 0) % positions
    other = lax.broadcasted_iota(jnp.int32, (tokens, tokens), 1) % positions
    same[...] = (place == other).astype(f32)

    row = lax.broadcasted_iota(jnp.int32, (2 * LANES, tokens), 0)
    for pair in range(HEADS // 2):
        window = slice(pair * LANES, (pair + 2) * LANES)
        begin = pair * (2 * HEAD_DIM - LANES)
        query = queries_t[window, :]
        both = [
            jnp.where((row >= begin + h * HEAD_DIM) & (row < begin + (h + 1) * HEAD_DIM), query, jnp.zeros((), bf16))
            for h in range(2)
        ]
        scores = dot(keys[:, window], jnp.concatenate(both, axis=1))
        weights = []
        for h in range(2):
            part = jnp.exp2(scores[:, h * tokens : (h + 1) * tokens] * EXP2_SCALE) * same[...]
            weights.append((part * (1.0 / jnp.sum(part, axis=0, keepdims=True))).astype(bf16))
        features = slice(pair * 2 * HEAD_DIM, (pair + 1) * 2 * HEAD_DIM)
        heads_out = dot(values_t[features, :], jnp.concatenate(weights, axis=1))
        for h in range(2):
            first = (2 * pair + h) * HEAD_DIM
            attended_t[first : first + HEAD_DIM, :] = heads_out[
                h * HEAD_DIM : (h + 1) * HEAD_DIM, h * tokens : (h + 1) * tokens
            ]
    attended[...] = attended_t[...].astype(bf16).T

    copies[2].wait()
    branch = dot(attended[...], wout[...])
    o_ref[...] = (x_ref[...].astype(f32) + branch.reshape(x_ref.shape)).astype(bf16)


def out_kernel(x_ref, o_ref, sem):
    copy = pltpu.make_async_copy(x_ref, o_ref, sem)
    copy.start()
    copy.wait()


def body(latent, ln_gain, q_gain, k_gain, w_qkv, w_out):
    device_count = lax.axis_size("frame")
    rows, columns, model = latent.shape
    tokens = rows * columns
    per_peer = tokens // device_count
    order = [4 * i + 2 * row + core for row in range(2) for i in range(device_count // 4) for core in range(2)]
    exchange = functools.partial(
        lax.all_to_all, axis_name="frame", split_axis=0, concat_axis=0, axis_index_groups=[order], tiled=True
    )
    gathered = exchange(latent.reshape(device_count, per_peer, model))
    in_vmem = pl.BlockSpec(memory_space=pltpu.VMEM)
    in_hbm = pl.BlockSpec(memory_space=pltpu.HBM)
    bf16, f32 = jnp.bfloat16, jnp.float32
    held = [pltpu.with_memory_space_constraint(a, pltpu.HBM) for a in (ln_gain, q_gain, k_gain, w_qkv, w_out)]
    gains, columns, member, spread, wq = pl.pallas_call(
        held_kernel,
        out_shape=(
            pltpu.VMEM((8, model), f32),
            pltpu.VMEM((HEAD_DIM, LANES), f32),
            pltpu.VMEM((model, LANES), bf16),
            pltpu.VMEM((2 * HEADS, model), bf16),
            pltpu.VMEM((model, model), bf16),
        ),
        in_specs=[in_hbm] * 4,
        out_specs=[in_vmem] * 5,
        scratch_shapes=[
            pltpu.VMEM((model,), f32),
            pltpu.VMEM((HEAD_DIM,), f32),
            pltpu.VMEM((HEAD_DIM,), f32),
            pltpu.SemaphoreType.DMA((4,)),
        ],
        compiler_params=pltpu.CompilerParams(vmem_limit_bytes=8 * 1024 * 1024),
        cost_estimate=pl.CostEstimate(flops=0, bytes_accessed=4 * model * model, transcendentals=0),
        name="held",
    )(*held[:4])
    result = pl.pallas_call(
        tokens_kernel,
        out_shape=jax.ShapeDtypeStruct(gathered.shape, bf16),
        in_specs=[in_vmem] * 6 + [in_hbm] * 2,
        out_specs=in_vmem,
        scratch_shapes=[
            pltpu.VMEM((model, 2 * model), bf16),
            pltpu.VMEM(w_out.shape, bf16),
            pltpu.VMEM((tokens, model), bf16),
            pltpu.VMEM((model, tokens), f32),
            pltpu.VMEM((tokens, model), f32),
            pltpu.VMEM((model, tokens), bf16),
            pltpu.VMEM((tokens, model), bf16),
            pltpu.VMEM((model, tokens), bf16),
            pltpu.VMEM((model, tokens), f32),
            pltpu.VMEM((tokens, model), bf16),
            pltpu.VMEM((tokens, tokens), f32),
            pltpu.SemaphoreType.DMA((3,)),
        ],
        compiler_params=pltpu.CompilerParams(vmem_limit_bytes=40 * 1024 * 1024),
        name="tokens",
    )(gathered, gains, columns, member, spread, wq, *held[3:])
    return pl.pallas_call(
        out_kernel,
        out_shape=pltpu.HBM(latent.shape, bf16),
        in_specs=[in_vmem],
        out_specs=in_hbm,
        scratch_shapes=[pltpu.SemaphoreType.DMA],
        name="out",
    )(exchange(result).reshape(latent.shape))


def solution(mesh):
    placed = (P(("groups", "frame"), None, None), P(), P(), P(), P(), P())
    return jax.shard_map(
        body,
        mesh=mesh,
        in_specs=placed,
        out_specs=P(("groups", "frame"), None, None),
        check_vma=False,
    )
```

```python
import functools
import math

import jax
import jax.numpy as jnp
from jax import lax
from jax.experimental import pallas as pl
from jax.experimental.pallas import tpu as pltpu
from jax.sharding import PartitionSpec as P

HEADS = 16
HEAD_DIM = 72
LANES = 128
EPS = 1e-06
EXP2_SCALE = HEAD_DIM**-0.5 * math.log2(math.e)


def dot(a, b):
    return jnp.dot(a, b, preferred_element_type=jnp.float32)


def held_kernel(
    ln_ref, qg_ref, kg_ref, wqkv_ref, gains_out, columns_out, member_out, spread_out, wq_out, ln, qg, kg, sems
):
    width = wq_out.shape[1]
    pairs = [(ln_ref, ln), (qg_ref, qg), (kg_ref, kg), (wqkv_ref.at[:, pl.ds(0, width)], wq_out)]
    copies = [pltpu.make_async_copy(src, dst, sems.at[i]) for i, (src, dst) in enumerate(pairs)]
    for copy in copies:
        copy.start()

    def belongs(feature, lane):
        head = jnp.where(lane >= HEADS, lane - HEADS, lane)
        first = head * HEAD_DIM
        held = (feature >= first) & (feature < first + HEAD_DIM) & (lane < 2 * HEADS)
        return held.astype(jnp.float32).astype(jnp.bfloat16)

    for out, axis in ((member_out, 0), (spread_out, 1)):
        feature = lax.broadcasted_iota(jnp.int32, out.shape, axis)
        out[...] = belongs(feature, lax.broadcasted_iota(jnp.int32, out.shape, 1 - axis))
    for copy in copies[:3]:
        copy.wait()
    gains_out[0:1, :] = ln[...].reshape(1, width)
    row = jnp.concatenate([qg[...].reshape(1, HEAD_DIM), jnp.zeros((1, LANES - HEAD_DIM), jnp.float32)], axis=1)
    columns_out[...] = jnp.broadcast_to(row, (LANES, LANES)).T[:HEAD_DIM]
    gains_out[1:2, :] = jnp.concatenate([kg[...].reshape(1, HEAD_DIM)] * HEADS, axis=1)
    copies[3].wait()


def tokens_kernel(
    x_ref,
    gains_ref,
    columns_ref,
    member_ref,
    spread_ref,
    wq,
    wqkv_hbm,
    wout_hbm,
    o_ref,
    wkv,
    wout,
    normed,
    mixed_q,
    mixed_k,
    queries_t,
    keys,
    values_t,
    attended_t,
    attended,
    same,
    sems,
):
    frames, positions, width = x_ref.shape
    tokens = frames * positions
    bf16, f32 = jnp.bfloat16, jnp.float32

    pairs = [
        (wqkv_hbm.at[:, pl.ds(width, width)], wkv.at[:, pl.ds(0, width)]),
        (wqkv_hbm.at[:, pl.ds(2 * width, width)], wkv.at[:, pl.ds(width, width)]),
        (wout_hbm, wout),
    ]
    copies = [pltpu.make_async_copy(src, dst, sems.at[i]) for i, (src, dst) in enumerate(pairs)]
    copies[0].start()

    gain = gains_ref[0:1, :]
    step = max(1, 16 // positions)
    for frame in range(0, frames, step):
        x = x_ref[frame : frame + step].astype(f32).reshape(step * positions, width)
        center = x - jnp.mean(x, axis=-1, keepdims=True)
        spread = jnp.mean(center * center, axis=-1, keepdims=True)
        rows = slice(frame * positions, (frame + step) * positions)
        normed[rows, :] = (center * lax.rsqrt(spread + EPS) * gain).astype(bf16)

    def head_norm(mixed, row, out):
        squares = mixed[...] * mixed[...]
        high = squares.astype(bf16)
        low = (squares - high.astype(f32)).astype(bf16)
        total = dot(jnp.concatenate([high, low], axis=0), member_ref[...])
        total = total[:tokens] + total[tokens:]
        inverse = lax.rsqrt(total * (1.0 / HEAD_DIM) + EPS)
        high = inverse.astype(bf16)
        low = (inverse - high.astype(f32)).astype(bf16)
        lane = lax.broadcasted_iota(jnp.int32, inverse.shape, 1)
        parts = jnp.where(lane < HEADS, high, low)[:, : 2 * HEADS]
        out[...] = (mixed[...] * dot(parts, spread_ref[...]) * gains_ref[row : row + 1, :]).astype(bf16)

    copies[1].start()
    mixed_q[...] = dot(normed[...], wq[...]).T
    for pair in range(HEADS // 2):
        heads = []
        for first in (2 * pair * HEAD_DIM, (2 * pair + 1) * HEAD_DIM):
            head = mixed_q[first : first + HEAD_DIM, :]
            total = jnp.sum(head * head, axis=0, keepdims=True)
            heads.append(head * lax.rsqrt(total * (1.0 / HEAD_DIM) + EPS) * columns_ref[...])
        rows = slice(2 * pair * HEAD_DIM, (2 * pair + 2) * HEAD_DIM)
        queries_t[rows, :] = jnp.concatenate(heads, axis=0).astype(bf16)
    copies[0].wait()
    copies[2].start()
    mixed_k[...] = dot(normed[...], wkv[:, :width])
    head_norm(mixed_k, 1, keys)
    copies[1].wait()
    values_t[...] = dot(normed[...], wkv[:, width:]).astype(bf16).T

    place = lax.broadcasted_iota(jnp.int32, (tokens, tokens), 0) % positions
    other = lax.broadcasted_iota(jnp.int32, (tokens, tokens), 1) % positions
    same[...] = (place == other).astype(f32)

    row = lax.broadcasted_iota(jnp.int32, (2 * LANES, tokens), 0)
    for pair in range(HEADS // 2):
        window = slice(pair * LANES, (pair + 2) * LANES)
        begin = pair * (2 * HEAD_DIM - LANES)
        query = queries_t[window, :]
        both = [
            jnp.where((row >= begin + h * HEAD_DIM) & (row < begin + (h + 1) * HEAD_DIM), query, jnp.zeros((), bf16))
            for h in range(2)
        ]
        scores = dot(keys[:, window], jnp.concatenate(both, axis=1))
        weights = []
        for h in range(2):
            part = jnp.exp2(scores[:, h * tokens : (h + 1) * tokens] * EXP2_SCALE) * same[...]
            weights.append((part * (1.0 / jnp.sum(part, axis=0, keepdims=True))).astype(bf16))
        features = slice(pair * 2 * HEAD_DIM, (pair + 1) * 2 * HEAD_DIM)
        heads_out = dot(values_t[features, :], jnp.concatenate(weights, axis=1))
        for h in range(2):
            first = (2 * pair + h) * HEAD_DIM
            attended_t[first : first + HEAD_DIM, :] = heads_out[
                h * HEAD_DIM : (h + 1) * HEAD_DIM, h * tokens : (h + 1) * tokens
            ]
    attended[...] = attended_t[...].astype(bf16).T

    copies[2].wait()
    branch = dot(attended[...], wout[...])
    o_ref[...] = (x_ref[...].astype(f32) + branch.reshape(x_ref.shape)).astype(bf16)


def out_kernel(x_ref, o_ref, sem):
    copy = pltpu.make_async_copy(x_ref, o_ref, sem)
    copy.start()
    copy.wait()


def body(latent, ln_gain, q_gain, k_gain, w_qkv, w_out):
    device_count = lax.axis_size("frame")
    rows, columns, model = latent.shape
    tokens = rows * columns
    per_peer = tokens // device_count
    order = [4 * i + 2 * row + core for row in range(2) for i in range(device_count // 4) for core in range(2)]
    exchange = functools.partial(
        lax.all_to_all, axis_name="frame", split_axis=0, concat_axis=0, axis_index_groups=[order], tiled=True
    )
    gathered = exchange(latent.reshape(device_count, per_peer, model))
    in_vmem = pl.BlockSpec(memory_space=pltpu.VMEM)
    in_hbm = pl.BlockSpec(memory_space=pltpu.HBM)
    bf16, f32 = jnp.bfloat16, jnp.float32
    held = [pltpu.with_memory_space_constraint(a, pltpu.HBM) for a in (ln_gain, q_gain, k_gain, w_qkv, w_out)]
    gains, columns, member, spread, wq = pl.pallas_call(
        held_kernel,
        out_shape=(
            pltpu.VMEM((8, model), f32),
            pltpu.VMEM((HEAD_DIM, LANES), f32),
            pltpu.VMEM((model, LANES), bf16),
            pltpu.VMEM((2 * HEADS, model), bf16),
            pltpu.VMEM((model, model), bf16),
        ),
        in_specs=[in_hbm] * 4,
        out_specs=[in_vmem] * 5,
        scratch_shapes=[
            pltpu.VMEM((model,), f32),
            pltpu.VMEM((HEAD_DIM,), f32),
            pltpu.VMEM((HEAD_DIM,), f32),
            pltpu.SemaphoreType.DMA((4,)),
        ],
        compiler_params=pltpu.CompilerParams(vmem_limit_bytes=8 * 1024 * 1024),
        cost_estimate=pl.CostEstimate(flops=0, bytes_accessed=4 * model * model, transcendentals=0),
        name="held",
    )(*held[:4])
    result = pl.pallas_call(
        tokens_kernel,
        out_shape=jax.ShapeDtypeStruct(gathered.shape, bf16),
        in_specs=[in_vmem] * 6 + [in_hbm] * 2,
        out_specs=in_vmem,
        scratch_shapes=[
            pltpu.VMEM((model, 2 * model), bf16),
            pltpu.VMEM(w_out.shape, bf16),
            pltpu.VMEM((tokens, model), bf16),
            pltpu.VMEM((model, tokens), f32),
            pltpu.VMEM((tokens, model), f32),
            pltpu.VMEM((model, tokens), bf16),
            pltpu.VMEM((tokens, model), bf16),
            pltpu.VMEM((model, tokens), bf16),
            pltpu.VMEM((model, tokens), f32),
            pltpu.VMEM((tokens, model), bf16),
            pltpu.VMEM((tokens, tokens), f32),
            pltpu.SemaphoreType.DMA((3,)),
        ],
        compiler_params=pltpu.CompilerParams(vmem_limit_bytes=40 * 1024 * 1024),
        name="tokens",
    )(gathered, gains, columns, member, spread, wq, *held[3:])
    return pl.pallas_call(
        out_kernel,
        out_shape=pltpu.HBM(latent.shape, bf16),
        in_specs=[in_vmem],
        out_specs=in_hbm,
        scratch_shapes=[pltpu.SemaphoreType.DMA],
        name="out",
    )(pltpu.with_memory_space_constraint(exchange(result).reshape(latent.shape), pltpu.VMEM))


def solution(mesh):
    placed = (P(("groups", "frame"), None, None), P(), P(), P(), P(), P())
    return jax.shard_map(
        body,
        mesh=mesh,
        in_specs=placed,
        out_specs=P(("groups", "frame"), None, None),
        check_vma=False,
    )
```

```python
import functools
import math

import jax
import jax.numpy as jnp
from jax import lax
from jax.experimental import pallas as pl
from jax.experimental.pallas import tpu as pltpu
from jax.sharding import PartitionSpec as P

HEADS = 16
HEAD_DIM = 72
LANES = 128
EPS = 1e-06
EXP2_SCALE = HEAD_DIM**-0.5 * math.log2(math.e)


def dot(a, b):
    return jnp.dot(a, b, preferred_element_type=jnp.float32)


def held_kernel(
    ln_ref, qg_ref, kg_ref, wqkv_ref, gains_out, columns_out, member_out, spread_out, wq_out, ln, qg, kg, wq, sems
):
    width = wq_out.shape[1]
    pairs = [(ln_ref, ln), (qg_ref, qg), (kg_ref, kg), (wqkv_ref.at[:, pl.ds(0, width)], wq)]
    copies = [pltpu.make_async_copy(src, dst, sems.at[i]) for i, (src, dst) in enumerate(pairs)]
    for copy in copies:
        copy.start()

    def belongs(feature, lane):
        head = jnp.where(lane >= HEADS, lane - HEADS, lane)
        first = head * HEAD_DIM
        held = (feature >= first) & (feature < first + HEAD_DIM) & (lane < 2 * HEADS)
        return held.astype(jnp.float32).astype(jnp.bfloat16)

    for out, axis in ((member_out, 0), (spread_out, 1)):
        feature = lax.broadcasted_iota(jnp.int32, out.shape, axis)
        out[...] = belongs(feature, lax.broadcasted_iota(jnp.int32, out.shape, 1 - axis))
    for copy in copies[:3]:
        copy.wait()
    gains_out[0:1, :] = ln[...].reshape(1, width)
    row = jnp.concatenate([qg[...].reshape(1, HEAD_DIM), jnp.zeros((1, LANES - HEAD_DIM), jnp.float32)], axis=1)
    columns_out[...] = jnp.broadcast_to(row, (LANES, LANES)).T[:HEAD_DIM]
    gains_out[1:2, :] = jnp.concatenate([kg[...].reshape(1, HEAD_DIM)] * HEADS, axis=1)
    copies[3].wait()
    for row in range(0, width, LANES):
        wq_out[:, row : row + LANES] = wq[row : row + LANES, :].T


def tokens_kernel(
    x_ref,
    gains_ref,
    columns_ref,
    member_ref,
    spread_ref,
    wq,
    wqkv_hbm,
    wout_hbm,
    o_ref,
    wkv,
    wout,
    normed,
    normed_t,
    mixed_k,
    queries_t,
    keys,
    values_t,
    attended_t,
    attended,
    same,
    sems,
):
    frames, positions, width = x_ref.shape
    tokens = frames * positions
    bf16, f32 = jnp.bfloat16, jnp.float32

    pairs = [
        (wqkv_hbm.at[:, pl.ds(width, width)], wkv.at[:, pl.ds(0, width)]),
        (wqkv_hbm.at[:, pl.ds(2 * width, width)], wkv.at[:, pl.ds(width, width)]),
        (wout_hbm, wout),
    ]
    copies = [pltpu.make_async_copy(src, dst, sems.at[i]) for i, (src, dst) in enumerate(pairs)]
    copies[0].start()

    gain = gains_ref[0:1, :]
    step = max(1, 16 // positions)
    for frame in range(0, frames, step):
        x = x_ref[frame : frame + step].astype(f32).reshape(step * positions, width)
        center = x - jnp.mean(x, axis=-1, keepdims=True)
        spread = jnp.mean(center * center, axis=-1, keepdims=True)
        rows = slice(frame * positions, (frame + step) * positions)
        normed[rows, :] = (center * lax.rsqrt(spread + EPS) * gain).astype(bf16)

    def head_norm(mixed, row, out):
        squares = mixed[...] * mixed[...]
        high = squares.astype(bf16)
        low = (squares - high.astype(f32)).astype(bf16)
        total = dot(jnp.concatenate([high, low], axis=0), member_ref[...])
        total = total[:tokens] + total[tokens:]
        inverse = lax.rsqrt(total * (1.0 / HEAD_DIM) + EPS)
        high = inverse.astype(bf16)
        low = (inverse - high.astype(f32)).astype(bf16)
        lane = lax.broadcasted_iota(jnp.int32, inverse.shape, 1)
        parts = jnp.where(lane < HEADS, high, low)[:, : 2 * HEADS]
        out[...] = (mixed[...] * dot(parts, spread_ref[...]) * gains_ref[row : row + 1, :]).astype(bf16)

    copies[1].start()
    normed_t[...] = normed[...].T
    span = 4 * HEAD_DIM
    for begin in range(0, width, span):
        mixed = dot(wq[begin : begin + span, :], normed_t[...])
        heads = []
        for first in range(0, span, HEAD_DIM):
            head = mixed[first : first + HEAD_DIM, :]
            total = jnp.sum(head * head, axis=0, keepdims=True)
            heads.append(head * lax.rsqrt(total * (1.0 / HEAD_DIM) + EPS) * columns_ref[...])
        queries_t[begin : begin + span, :] = jnp.concatenate(heads, axis=0).astype(bf16)
    copies[0].wait()
    copies[2].start()
    mixed_k[...] = dot(normed[...], wkv[:, :width])
    head_norm(mixed_k, 1, keys)
    copies[1].wait()
    values_t[...] = dot(normed[...], wkv[:, width:]).astype(bf16).T

    place = lax.broadcasted_iota(jnp.int32, (tokens, tokens), 0) % positions
    other = lax.broadcasted_iota(jnp.int32, (tokens, tokens), 1) % positions
    same[...] = (place == other).astype(f32)

    row = lax.broadcasted_iota(jnp.int32, (2 * LANES, tokens), 0)
    for pair in range(HEADS // 2):
        window = slice(pair * LANES, (pair + 2) * LANES)
        begin = pair * (2 * HEAD_DIM - LANES)
        query = queries_t[window, :]
        both = [
            jnp.where((row >= begin + h * HEAD_DIM) & (row < begin + (h + 1) * HEAD_DIM), query, jnp.zeros((), bf16))
            for h in range(2)
        ]
        scores = dot(keys[:, window], jnp.concatenate(both, axis=1))
        weights = []
        for h in range(2):
            part = jnp.exp2(scores[:, h * tokens : (h + 1) * tokens] * EXP2_SCALE) * same[...]
            weights.append((part * (1.0 / jnp.sum(part, axis=0, keepdims=True))).astype(bf16))
        features = slice(pair * 2 * HEAD_DIM, (pair + 1) * 2 * HEAD_DIM)
        heads_out = dot(values_t[features, :], jnp.concatenate(weights, axis=1))
        for h in range(2):
            first = (2 * pair + h) * HEAD_DIM
            attended_t[first : first + HEAD_DIM, :] = heads_out[
                h * HEAD_DIM : (h + 1) * HEAD_DIM, h * tokens : (h + 1) * tokens
            ]
    attended[...] = attended_t[...].astype(bf16).T

    copies[2].wait()
    branch = dot(attended[...], wout[...])
    o_ref[...] = (x_ref[...].astype(f32) + branch.reshape(x_ref.shape)).astype(bf16)


def body(latent, ln_gain, q_gain, k_gain, w_qkv, w_out):
    device_count = lax.axis_size("frame")
    rows, columns, model = latent.shape
    tokens = rows * columns
    per_peer = tokens // device_count
    order = [4 * i + 2 * row + core for row in range(2) for i in range(device_count // 4) for core in range(2)]
    exchange = functools.partial(
        lax.all_to_all, axis_name="frame", split_axis=0, concat_axis=0, axis_index_groups=[order], tiled=True
    )
    gathered = exchange(latent.reshape(device_count, per_peer, model))
    in_vmem = pl.BlockSpec(memory_space=pltpu.VMEM)
    in_hbm = pl.BlockSpec(memory_space=pltpu.HBM)
    bf16, f32 = jnp.bfloat16, jnp.float32
    held = [pltpu.with_memory_space_constraint(a, pltpu.HBM) for a in (ln_gain, q_gain, k_gain, w_qkv, w_out)]
    gains, columns, member, spread, wq = pl.pallas_call(
        held_kernel,
        out_shape=(
            pltpu.VMEM((8, model), f32),
            pltpu.VMEM((HEAD_DIM, LANES), f32),
            pltpu.VMEM((model, LANES), bf16),
            pltpu.VMEM((2 * HEADS, model), bf16),
            pltpu.VMEM((model, model), bf16),
        ),
        in_specs=[in_hbm] * 4,
        out_specs=[in_vmem] * 5,
        scratch_shapes=[
            pltpu.VMEM((model,), f32),
            pltpu.VMEM((HEAD_DIM,), f32),
            pltpu.VMEM((HEAD_DIM,), f32),
            pltpu.VMEM((model, model), bf16),
            pltpu.SemaphoreType.DMA((4,)),
        ],
        compiler_params=pltpu.CompilerParams(vmem_limit_bytes=8 * 1024 * 1024),
        cost_estimate=pl.CostEstimate(flops=0, bytes_accessed=4 * model * model, transcendentals=0),
        name="held",
    )(*held[:4])
    result = pl.pallas_call(
        tokens_kernel,
        out_shape=jax.ShapeDtypeStruct(gathered.shape, bf16),
        in_specs=[in_vmem] * 6 + [in_hbm] * 2,
        out_specs=in_vmem,
        scratch_shapes=[
            pltpu.VMEM((model, 2 * model), bf16),
            pltpu.VMEM(w_out.shape, bf16),
            pltpu.VMEM((tokens, model), bf16),
            pltpu.VMEM((model, tokens), bf16),
            pltpu.VMEM((tokens, model), f32),
            pltpu.VMEM((model, tokens), bf16),
            pltpu.VMEM((tokens, model), bf16),
            pltpu.VMEM((model, tokens), bf16),
            pltpu.VMEM((model, tokens), f32),
            pltpu.VMEM((tokens, model), bf16),
            pltpu.VMEM((tokens, tokens), f32),
            pltpu.SemaphoreType.DMA((3,)),
        ],
        compiler_params=pltpu.CompilerParams(vmem_limit_bytes=40 * 1024 * 1024),
        name="tokens",
    )(gathered, gains, columns, member, spread, wq, *held[3:])
    return exchange(result).reshape(latent.shape)


def solution(mesh):
    placed = (P(("groups", "frame"), None, None), P(), P(), P(), P(), P())
    return jax.shard_map(
        body,
        mesh=mesh,
        in_specs=placed,
        out_specs=P(("groups", "frame"), None, None),
        check_vma=False,
    )
```

```python
import functools
import math

import jax
import jax.numpy as jnp
from jax import lax
from jax.experimental import pallas as pl
from jax.experimental.pallas import tpu as pltpu
from jax.sharding import PartitionSpec as P

HEADS = 16
HEAD_DIM = 72
LANES = 128
EPS = 1e-06
EXP2_SCALE = HEAD_DIM**-0.5 * math.log2(math.e)


def dot(a, b):
    return jnp.dot(a, b, preferred_element_type=jnp.float32)


def held_kernel(
    ln_ref, qg_ref, kg_ref, wqkv_ref, gains_out, columns_out, member_out, spread_out, wq_out, ln, qg, kg, sems
):
    width = wq_out.shape[1]
    pairs = [(ln_ref, ln), (qg_ref, qg), (kg_ref, kg), (wqkv_ref.at[:, pl.ds(0, width)], wq_out)]
    copies = [pltpu.make_async_copy(src, dst, sems.at[i]) for i, (src, dst) in enumerate(pairs)]
    for copy in copies:
        copy.start()

    def belongs(feature, lane):
        head = jnp.where(lane >= HEADS, lane - HEADS, lane)
        first = head * HEAD_DIM
        held = (feature >= first) & (feature < first + HEAD_DIM) & (lane < 2 * HEADS)
        return held.astype(jnp.float32).astype(jnp.bfloat16)

    for out, axis in ((member_out, 0), (spread_out, 1)):
        feature = lax.broadcasted_iota(jnp.int32, out.shape, axis)
        out[...] = belongs(feature, lax.broadcasted_iota(jnp.int32, out.shape, 1 - axis))
    for copy in copies[:3]:
        copy.wait()
    gains_out[0:1, :] = ln[...].reshape(1, width)
    row = jnp.concatenate([qg[...].reshape(1, HEAD_DIM), jnp.zeros((1, LANES - HEAD_DIM), jnp.float32)], axis=1)
    columns_out[...] = jnp.broadcast_to(row, (LANES, LANES)).T[:HEAD_DIM]
    gains_out[1:2, :] = jnp.concatenate([kg[...].reshape(1, HEAD_DIM)] * HEADS, axis=1)
    copies[3].wait()


def tokens_kernel(
    x_ref,
    gains_ref,
    columns_ref,
    member_ref,
    spread_ref,
    wq,
    wqkv_hbm,
    wout_hbm,
    o_ref,
    wkv,
    wout,
    normed,
    mixed_q,
    mixed_k,
    queries_t,
    keys,
    values_t,
    attended_t,
    attended,
    same,
    sems,
):
    frames, positions, width = x_ref.shape
    tokens = frames * positions
    bf16, f32 = jnp.bfloat16, jnp.float32

    pairs = [
        (wqkv_hbm.at[:, pl.ds(width, width)], wkv.at[:, pl.ds(0, width)]),
        (wqkv_hbm.at[:, pl.ds(2 * width, width)], wkv.at[:, pl.ds(width, width)]),
        (wout_hbm, wout),
    ]
    copies = [pltpu.make_async_copy(src, dst, sems.at[i]) for i, (src, dst) in enumerate(pairs)]
    copies[0].start()

    gain = gains_ref[0:1, :]
    step = max(1, 16 // positions)
    for frame in range(0, frames, step):
        x = x_ref[frame : frame + step].astype(f32).reshape(step * positions, width)
        center = x - jnp.mean(x, axis=-1, keepdims=True)
        spread = jnp.mean(center * center, axis=-1, keepdims=True)
        rows = slice(frame * positions, (frame + step) * positions)
        normed[rows, :] = (center * lax.rsqrt(spread + EPS) * gain).astype(bf16)

    def head_norm(mixed, row, out):
        squares = mixed[...] * mixed[...]
        high = squares.astype(bf16)
        low = (squares - high.astype(f32)).astype(bf16)
        total = dot(jnp.concatenate([high, low], axis=0), member_ref[...])
        total = total[:tokens] + total[tokens:]
        inverse = lax.rsqrt(total * (1.0 / HEAD_DIM) + EPS)
        high = inverse.astype(bf16)
        low = (inverse - high.astype(f32)).astype(bf16)
        lane = lax.broadcasted_iota(jnp.int32, inverse.shape, 1)
        parts = jnp.where(lane < HEADS, high, low)[:, : 2 * HEADS]
        out[...] = (mixed[...] * dot(parts, spread_ref[...]) * gains_ref[row : row + 1, :]).astype(bf16)

    copies[1].start()
    mixed_q[...] = dot(normed[...], wq[...]).T
    for pair in range(HEADS // 2):
        heads = []
        for first in (2 * pair * HEAD_DIM, (2 * pair + 1) * HEAD_DIM):
            head = mixed_q[first : first + HEAD_DIM, :]
            total = jnp.sum(head * head, axis=0, keepdims=True)
            heads.append(head * lax.rsqrt(total * (1.0 / HEAD_DIM) + EPS) * columns_ref[...])
        rows = slice(2 * pair * HEAD_DIM, (2 * pair + 2) * HEAD_DIM)
        queries_t[rows, :] = jnp.concatenate(heads, axis=0).astype(bf16)
    copies[0].wait()
    copies[2].start()
    mixed_k[...] = dot(normed[...], wkv[:, :width])
    head_norm(mixed_k, 1, keys)
    copies[1].wait()
    values_t[...] = dot(normed[...], wkv[:, width:]).astype(bf16).T

    place = lax.broadcasted_iota(jnp.int32, (tokens, tokens), 0) % positions
    other = lax.broadcasted_iota(jnp.int32, (tokens, tokens), 1) % positions
    same[...] = (place == other).astype(f32)

    row = lax.broadcasted_iota(jnp.int32, (2 * LANES, tokens), 0)
    for pair in range(HEADS // 2):
        window = slice(pair * LANES, (pair + 2) * LANES)
        begin = pair * (2 * HEAD_DIM - LANES)
        query = queries_t[window, :]
        both = [
            jnp.where((row >= begin + h * HEAD_DIM) & (row < begin + (h + 1) * HEAD_DIM), query, jnp.zeros((), bf16))
            for h in range(2)
        ]
        scores = dot(keys[:, window], jnp.concatenate(both, axis=1))
        weights = []
        for h in range(2):
            part = jnp.exp2(scores[:, h * tokens : (h + 1) * tokens] * EXP2_SCALE) * same[...]
            weights.append((part * (1.0 / jnp.sum(part, axis=0, keepdims=True))).astype(bf16))
        features = slice(pair * 2 * HEAD_DIM, (pair + 1) * 2 * HEAD_DIM)
        heads_out = dot(values_t[features, :], jnp.concatenate(weights, axis=1))
        for h in range(2):
            first = (2 * pair + h) * HEAD_DIM
            attended_t[first : first + HEAD_DIM, :] = heads_out[
                h * HEAD_DIM : (h + 1) * HEAD_DIM, h * tokens : (h + 1) * tokens
            ]
    attended[...] = attended_t[...].astype(bf16).T

    copies[2].wait()
    branch = dot(attended[...], wout[...])
    o_ref[...] = (x_ref[...].astype(f32) + branch.reshape(x_ref.shape)).astype(bf16)


def body(latent, ln_gain, q_gain, k_gain, w_qkv, w_out):
    device_count = lax.axis_size("frame")
    rows, columns, model = latent.shape
    tokens = rows * columns
    per_peer = tokens // device_count
    order = [4 * i + 2 * row + core for core in range(2) for row in range(2) for i in range(device_count // 4)]
    exchange = functools.partial(
        lax.all_to_all, axis_name="frame", split_axis=0, concat_axis=0, axis_index_groups=[order], tiled=True
    )
    gathered = exchange(latent.reshape(device_count, per_peer, model))
    in_vmem = pl.BlockSpec(memory_space=pltpu.VMEM)
    in_hbm = pl.BlockSpec(memory_space=pltpu.HBM)
    bf16, f32 = jnp.bfloat16, jnp.float32
    held = [pltpu.with_memory_space_constraint(a, pltpu.HBM) for a in (ln_gain, q_gain, k_gain, w_qkv, w_out)]
    gains, columns, member, spread, wq = pl.pallas_call(
        held_kernel,
        out_shape=(
            pltpu.VMEM((8, model), f32),
            pltpu.VMEM((HEAD_DIM, LANES), f32),
            pltpu.VMEM((model, LANES), bf16),
            pltpu.VMEM((2 * HEADS, model), bf16),
            pltpu.VMEM((model, model), bf16),
        ),
        in_specs=[in_hbm] * 4,
        out_specs=[in_vmem] * 5,
        scratch_shapes=[
            pltpu.VMEM((model,), f32),
            pltpu.VMEM((HEAD_DIM,), f32),
            pltpu.VMEM((HEAD_DIM,), f32),
            pltpu.SemaphoreType.DMA((4,)),
        ],
        compiler_params=pltpu.CompilerParams(vmem_limit_bytes=8 * 1024 * 1024),
        cost_estimate=pl.CostEstimate(flops=0, bytes_accessed=4 * model * model, transcendentals=0),
        name="held",
    )(*held[:4])
    result = pl.pallas_call(
        tokens_kernel,
        out_shape=jax.ShapeDtypeStruct(gathered.shape, bf16),
        in_specs=[in_vmem] * 6 + [in_hbm] * 2,
        out_specs=in_vmem,
        scratch_shapes=[
            pltpu.VMEM((model, 2 * model), bf16),
            pltpu.VMEM(w_out.shape, bf16),
            pltpu.VMEM((tokens, model), bf16),
            pltpu.VMEM((model, tokens), f32),
            pltpu.VMEM((tokens, model), f32),
            pltpu.VMEM((model, tokens), bf16),
            pltpu.VMEM((tokens, model), bf16),
            pltpu.VMEM((model, tokens), bf16),
            pltpu.VMEM((model, tokens), f32),
            pltpu.VMEM((tokens, model), bf16),
            pltpu.VMEM((tokens, tokens), f32),
            pltpu.SemaphoreType.DMA((3,)),
        ],
        compiler_params=pltpu.CompilerParams(vmem_limit_bytes=40 * 1024 * 1024),
        name="tokens",
    )(gathered, gains, columns, member, spread, wq, *held[3:])
    return exchange(result).reshape(latent.shape)


def solution(mesh):
    placed = (P(("groups", "frame"), None, None), P(), P(), P(), P(), P())
    return jax.shard_map(
        body,
        mesh=mesh,
        in_specs=placed,
        out_specs=P(("groups", "frame"), None, None),
        check_vma=False,
    )
```

```python
import functools
import math

import jax
import jax.numpy as jnp
from jax import lax
from jax.experimental import pallas as pl
from jax.experimental.pallas import tpu as pltpu
from jax.sharding import PartitionSpec as P

HEADS = 16
HEAD_DIM = 72
LANES = 128
EPS = 1e-06
EXP2_SCALE = HEAD_DIM**-0.5 * math.log2(math.e)


def dot(a, b):
    return jnp.dot(a, b, preferred_element_type=jnp.float32)


def held_kernel(
    ln_ref, qg_ref, kg_ref, wqkv_ref, gains_out, columns_out, member_out, spread_out, wq_out, ln, qg, kg, sems
):
    width = wq_out.shape[1]
    pairs = [(ln_ref, ln), (qg_ref, qg), (kg_ref, kg), (wqkv_ref.at[:, pl.ds(0, width)], wq_out)]
    copies = [pltpu.make_async_copy(src, dst, sems.at[i]) for i, (src, dst) in enumerate(pairs)]
    for copy in copies:
        copy.start()

    def belongs(feature, lane):
        head = jnp.where(lane >= HEADS, lane - HEADS, lane)
        first = head * HEAD_DIM
        held = (feature >= first) & (feature < first + HEAD_DIM) & (lane < 2 * HEADS)
        return held.astype(jnp.float32).astype(jnp.bfloat16)

    for out, axis in ((member_out, 0), (spread_out, 1)):
        feature = lax.broadcasted_iota(jnp.int32, out.shape, axis)
        out[...] = belongs(feature, lax.broadcasted_iota(jnp.int32, out.shape, 1 - axis))
    for copy in copies[:3]:
        copy.wait()
    gains_out[0:1, :] = ln[...].reshape(1, width)
    row = jnp.concatenate([qg[...].reshape(1, HEAD_DIM), jnp.zeros((1, LANES - HEAD_DIM), jnp.float32)], axis=1)
    columns_out[...] = jnp.broadcast_to(row, (LANES, LANES)).T[:HEAD_DIM]
    gains_out[1:2, :] = jnp.concatenate([kg[...].reshape(1, HEAD_DIM)] * HEADS, axis=1)
    copies[3].wait()


def tokens_kernel(
    x_ref,
    gains_ref,
    columns_ref,
    member_ref,
    spread_ref,
    wq,
    wqkv_hbm,
    wout_hbm,
    o_ref,
    wkv,
    wout,
    normed,
    mixed_q,
    mixed_k,
    queries_t,
    keys,
    values_t,
    attended_t,
    attended,
    same,
    sems,
):
    frames, positions, width = x_ref.shape
    tokens = frames * positions
    bf16, f32 = jnp.bfloat16, jnp.float32

    pairs = [
        (wqkv_hbm.at[:, pl.ds(width, width)], wkv.at[:, pl.ds(0, width)]),
        (wqkv_hbm.at[:, pl.ds(2 * width, width)], wkv.at[:, pl.ds(width, width)]),
        (wout_hbm, wout),
    ]
    copies = [pltpu.make_async_copy(src, dst, sems.at[i]) for i, (src, dst) in enumerate(pairs)]
    copies[0].start()

    gain = gains_ref[0:1, :]
    step = max(1, 16 // positions)
    for frame in range(0, frames, step):
        x = x_ref[frame : frame + step].astype(f32).reshape(step * positions, width)
        center = x - jnp.mean(x, axis=-1, keepdims=True)
        spread = jnp.mean(center * center, axis=-1, keepdims=True)
        rows = slice(frame * positions, (frame + step) * positions)
        normed[rows, :] = (center * lax.rsqrt(spread + EPS) * gain).astype(bf16)

    def head_norm(mixed, row, out):
        squares = mixed[...] * mixed[...]
        high = squares.astype(bf16)
        low = (squares - high.astype(f32)).astype(bf16)
        total = dot(jnp.concatenate([high, low], axis=0), member_ref[...])
        total = total[:tokens] + total[tokens:]
        inverse = lax.rsqrt(total * (1.0 / HEAD_DIM) + EPS)
        high = inverse.astype(bf16)
        low = (inverse - high.astype(f32)).astype(bf16)
        lane = lax.broadcasted_iota(jnp.int32, inverse.shape, 1)
        parts = jnp.where(lane < HEADS, high, low)[:, : 2 * HEADS]
        out[...] = (mixed[...] * dot(parts, spread_ref[...]) * gains_ref[row : row + 1, :]).astype(bf16)

    copies[1].start()
    mixed_q[...] = dot(normed[...], wq[...]).T
    for pair in range(HEADS // 2):
        heads = []
        for first in (2 * pair * HEAD_DIM, (2 * pair + 1) * HEAD_DIM):
            head = mixed_q[first : first + HEAD_DIM, :]
            total = jnp.sum(head * head, axis=0, keepdims=True)
            heads.append(head * lax.rsqrt(total * (1.0 / HEAD_DIM) + EPS) * columns_ref[...])
        rows = slice(2 * pair * HEAD_DIM, (2 * pair + 2) * HEAD_DIM)
        queries_t[rows, :] = jnp.concatenate(heads, axis=0).astype(bf16)
    copies[0].wait()
    copies[2].start()
    mixed_k[...] = dot(normed[...], wkv[:, :width])
    head_norm(mixed_k, 1, keys)
    copies[1].wait()
    values_t[...] = dot(normed[...], wkv[:, width:]).astype(bf16).T

    place = lax.broadcasted_iota(jnp.int32, (tokens, tokens), 0) % positions
    other = lax.broadcasted_iota(jnp.int32, (tokens, tokens), 1) % positions
    same[...] = (place == other).astype(f32)

    row = lax.broadcasted_iota(jnp.int32, (2 * LANES, tokens), 0)
    for pair in range(HEADS // 2):
        window = slice(pair * LANES, (pair + 2) * LANES)
        begin = pair * (2 * HEAD_DIM - LANES)
        query = queries_t[window, :]
        both = [
            jnp.where((row >= begin + h * HEAD_DIM) & (row < begin + (h + 1) * HEAD_DIM), query, jnp.zeros((), bf16))
            for h in range(2)
        ]
        scores = dot(keys[:, window], jnp.concatenate(both, axis=1))
        weights = []
        for h in range(2):
            part = jnp.exp2(scores[:, h * tokens : (h + 1) * tokens] * EXP2_SCALE) * same[...]
            weights.append((part * (1.0 / jnp.sum(part, axis=0, keepdims=True))).astype(bf16))
        features = slice(pair * 2 * HEAD_DIM, (pair + 1) * 2 * HEAD_DIM)
        heads_out = dot(values_t[features, :], jnp.concatenate(weights, axis=1))
        for h in range(2):
            first = (2 * pair + h) * HEAD_DIM
            attended_t[first : first + HEAD_DIM, :] = heads_out[
                h * HEAD_DIM : (h + 1) * HEAD_DIM, h * tokens : (h + 1) * tokens
            ]
    attended[...] = attended_t[...].astype(bf16).T

    copies[2].wait()
    branch = dot(attended[...], wout[...])
    o_ref[...] = (x_ref[...].astype(f32) + branch.reshape(x_ref.shape)).astype(bf16)


def body(latent, ln_gain, q_gain, k_gain, w_qkv, w_out):
    device_count = lax.axis_size("frame")
    rows, columns, model = latent.shape
    tokens = rows * columns
    per_peer = tokens // device_count
    line = list(range(device_count // 4))
    order = [4 * i + 2 * row + core for row, walk in enumerate((line, line[::-1])) for i in walk for core in range(2)]
    exchange = functools.partial(
        lax.all_to_all, axis_name="frame", split_axis=0, concat_axis=0, axis_index_groups=[order], tiled=True
    )
    gathered = exchange(latent.reshape(device_count, per_peer, model))
    in_vmem = pl.BlockSpec(memory_space=pltpu.VMEM)
    in_hbm = pl.BlockSpec(memory_space=pltpu.HBM)
    bf16, f32 = jnp.bfloat16, jnp.float32
    held = [pltpu.with_memory_space_constraint(a, pltpu.HBM) for a in (ln_gain, q_gain, k_gain, w_qkv, w_out)]
    gains, columns, member, spread, wq = pl.pallas_call(
        held_kernel,
        out_shape=(
            pltpu.VMEM((8, model), f32),
            pltpu.VMEM((HEAD_DIM, LANES), f32),
            pltpu.VMEM((model, LANES), bf16),
            pltpu.VMEM((2 * HEADS, model), bf16),
            pltpu.VMEM((model, model), bf16),
        ),
        in_specs=[in_hbm] * 4,
        out_specs=[in_vmem] * 5,
        scratch_shapes=[
            pltpu.VMEM((model,), f32),
            pltpu.VMEM((HEAD_DIM,), f32),
            pltpu.VMEM((HEAD_DIM,), f32),
            pltpu.SemaphoreType.DMA((4,)),
        ],
        compiler_params=pltpu.CompilerParams(vmem_limit_bytes=8 * 1024 * 1024),
        cost_estimate=pl.CostEstimate(flops=0, bytes_accessed=4 * model * model, transcendentals=0),
        name="held",
    )(*held[:4])
    result = pl.pallas_call(
        tokens_kernel,
        out_shape=jax.ShapeDtypeStruct(gathered.shape, bf16),
        in_specs=[in_vmem] * 6 + [in_hbm] * 2,
        out_specs=in_vmem,
        scratch_shapes=[
            pltpu.VMEM((model, 2 * model), bf16),
            pltpu.VMEM(w_out.shape, bf16),
            pltpu.VMEM((tokens, model), bf16),
            pltpu.VMEM((model, tokens), f32),
            pltpu.VMEM((tokens, model), f32),
            pltpu.VMEM((model, tokens), bf16),
            pltpu.VMEM((tokens, model), bf16),
            pltpu.VMEM((model, tokens), bf16),
            pltpu.VMEM((model, tokens), f32),
            pltpu.VMEM((tokens, model), bf16),
            pltpu.VMEM((tokens, tokens), f32),
            pltpu.SemaphoreType.DMA((3,)),
        ],
        compiler_params=pltpu.CompilerParams(vmem_limit_bytes=40 * 1024 * 1024),
        name="tokens",
    )(gathered, gains, columns, member, spread, wq, *held[3:])
    return exchange(result).reshape(latent.shape)


def solution(mesh):
    placed = (P(("groups", "frame"), None, None), P(), P(), P(), P(), P())
    return jax.shard_map(
        body,
        mesh=mesh,
        in_specs=placed,
        out_specs=P(("groups", "frame"), None, None),
        check_vma=False,
    )
```

```python
import functools
import math

import jax
import jax.numpy as jnp
from jax import lax
from jax.experimental import pallas as pl
from jax.experimental.pallas import tpu as pltpu
from jax.sharding import PartitionSpec as P

HEADS = 16
HEAD_DIM = 72
LANES = 128
EPS = 1e-06
EXP2_SCALE = HEAD_DIM**-0.5 * math.log2(math.e)


def dot(a, b):
    return jnp.dot(a, b, preferred_element_type=jnp.float32)


def held_kernel(
    ln_ref, qg_ref, kg_ref, wqkv_ref, gains_out, columns_out, member_out, spread_out, wq_out, ln, qg, kg, sems
):
    width = wq_out.shape[1]
    pairs = [(ln_ref, ln), (qg_ref, qg), (kg_ref, kg), (wqkv_ref.at[:, pl.ds(0, width)], wq_out)]
    copies = [pltpu.make_async_copy(src, dst, sems.at[i]) for i, (src, dst) in enumerate(pairs)]
    for copy in copies:
        copy.start()

    def belongs(feature, lane):
        head = jnp.where(lane >= HEADS, lane - HEADS, lane)
        first = head * HEAD_DIM
        held = (feature >= first) & (feature < first + HEAD_DIM) & (lane < 2 * HEADS)
        return held.astype(jnp.float32).astype(jnp.bfloat16)

    for out, axis in ((member_out, 0), (spread_out, 1)):
        feature = lax.broadcasted_iota(jnp.int32, out.shape, axis)
        out[...] = belongs(feature, lax.broadcasted_iota(jnp.int32, out.shape, 1 - axis))
    for copy in copies[:3]:
        copy.wait()
    gains_out[0:1, :] = ln[...].reshape(1, width)
    row = jnp.concatenate([qg[...].reshape(1, HEAD_DIM), jnp.zeros((1, LANES - HEAD_DIM), jnp.float32)], axis=1)
    columns_out[...] = jnp.broadcast_to(row, (LANES, LANES)).T[:HEAD_DIM]
    gains_out[1:2, :] = jnp.concatenate([kg[...].reshape(1, HEAD_DIM)] * HEADS, axis=1)
    copies[3].wait()


def tokens_kernel(
    x_ref,
    gains_ref,
    columns_ref,
    member_ref,
    spread_ref,
    wq,
    wqkv_hbm,
    wout_hbm,
    o_ref,
    wkv,
    wout,
    normed,
    mixed_q,
    mixed_k,
    queries_t,
    keys,
    values_t,
    attended_t,
    attended,
    same,
    sems,
):
    frames, positions, width = x_ref.shape
    tokens = frames * positions
    bf16, f32 = jnp.bfloat16, jnp.float32

    pairs = [
        (wqkv_hbm.at[:, pl.ds(width, width)], wkv.at[:, pl.ds(0, width)]),
        (wqkv_hbm.at[:, pl.ds(2 * width, width)], wkv.at[:, pl.ds(width, width)]),
        (wout_hbm, wout),
    ]
    copies = [pltpu.make_async_copy(src, dst, sems.at[i]) for i, (src, dst) in enumerate(pairs)]
    copies[0].start()

    gain = gains_ref[0:1, :]
    step = max(1, 16 // positions)
    for frame in range(0, frames, step):
        x = x_ref[frame : frame + step].astype(f32).reshape(step * positions, width)
        center = x - jnp.mean(x, axis=-1, keepdims=True)
        spread = jnp.mean(center * center, axis=-1, keepdims=True)
        rows = slice(frame * positions, (frame + step) * positions)
        normed[rows, :] = (center * lax.rsqrt(spread + EPS) * gain).astype(bf16)

    def head_norm(mixed, row, out):
        squares = mixed[...] * mixed[...]
        high = squares.astype(bf16)
        low = (squares - high.astype(f32)).astype(bf16)
        total = dot(jnp.concatenate([high, low], axis=0), member_ref[...])
        total = total[:tokens] + total[tokens:]
        inverse = lax.rsqrt(total * (1.0 / HEAD_DIM) + EPS)
        high = inverse.astype(bf16)
        low = (inverse - high.astype(f32)).astype(bf16)
        lane = lax.broadcasted_iota(jnp.int32, inverse.shape, 1)
        parts = jnp.where(lane < HEADS, high, low)[:, : 2 * HEADS]
        out[...] = (mixed[...] * dot(parts, spread_ref[...]) * gains_ref[row : row + 1, :]).astype(bf16)

    copies[1].start()
    mixed_q[...] = dot(normed[...], wq[...]).T
    for pair in range(HEADS // 2):
        heads = []
        for first in (2 * pair * HEAD_DIM, (2 * pair + 1) * HEAD_DIM):
            head = mixed_q[first : first + HEAD_DIM, :]
            total = jnp.sum(head * head, axis=0, keepdims=True)
            heads.append(head * lax.rsqrt(total * (1.0 / HEAD_DIM) + EPS) * columns_ref[...])
        rows = slice(2 * pair * HEAD_DIM, (2 * pair + 2) * HEAD_DIM)
        queries_t[rows, :] = jnp.concatenate(heads, axis=0).astype(bf16)
    copies[0].wait()
    copies[2].start()
    mixed_k[...] = dot(normed[...], wkv[:, :width])
    head_norm(mixed_k, 1, keys)
    copies[1].wait()
    values_t[...] = dot(normed[...], wkv[:, width:]).astype(bf16).T

    place = lax.broadcasted_iota(jnp.int32, (tokens, tokens), 0) % positions
    other = lax.broadcasted_iota(jnp.int32, (tokens, tokens), 1) % positions
    same[...] = (place == other).astype(f32)

    row = lax.broadcasted_iota(jnp.int32, (2 * LANES, tokens), 0)
    for pair in range(HEADS // 2):
        window = slice(pair * LANES, (pair + 2) * LANES)
        begin = pair * (2 * HEAD_DIM - LANES)
        query = queries_t[window, :]
        both = [
            jnp.where((row >= begin + h * HEAD_DIM) & (row < begin + (h + 1) * HEAD_DIM), query, jnp.zeros((), bf16))
            for h in range(2)
        ]
        scores = dot(keys[:, window], jnp.concatenate(both, axis=1))
        weights = []
        for h in range(2):
            part = jnp.exp2(scores[:, h * tokens : (h + 1) * tokens] * EXP2_SCALE) * same[...]
            weights.append((part * (1.0 / jnp.sum(part, axis=0, keepdims=True))).astype(bf16))
        features = slice(pair * 2 * HEAD_DIM, (pair + 1) * 2 * HEAD_DIM)
        heads_out = dot(values_t[features, :], jnp.concatenate(weights, axis=1))
        for h in range(2):
            first = (2 * pair + h) * HEAD_DIM
            attended_t[first : first + HEAD_DIM, :] = heads_out[
                h * HEAD_DIM : (h + 1) * HEAD_DIM, h * tokens : (h + 1) * tokens
            ]
    attended[...] = attended_t[...].astype(bf16).T

    copies[2].wait()
    branch = dot(attended[...], wout[...])
    o_ref[...] = (x_ref[...].astype(f32) + branch.reshape(x_ref.shape)).astype(bf16)


def body(latent, ln_gain, q_gain, k_gain, w_qkv, w_out):
    device_count = lax.axis_size("frame")
    rows, columns, model = latent.shape
    tokens = rows * columns
    per_peer = tokens // device_count
    line = list(range(device_count // 4))
    chips = [2 * i + row for row, walk in enumerate((line, line[::-1])) for i in walk]
    order = [2 * chip + (core + place) % 2 for place, chip in enumerate(chips) for core in range(2)]
    exchange = functools.partial(
        lax.all_to_all, axis_name="frame", split_axis=0, concat_axis=0, axis_index_groups=[order], tiled=True
    )
    gathered = exchange(latent.reshape(device_count, per_peer, model))
    in_vmem = pl.BlockSpec(memory_space=pltpu.VMEM)
    in_hbm = pl.BlockSpec(memory_space=pltpu.HBM)
    bf16, f32 = jnp.bfloat16, jnp.float32
    held = [pltpu.with_memory_space_constraint(a, pltpu.HBM) for a in (ln_gain, q_gain, k_gain, w_qkv, w_out)]
    gains, columns, member, spread, wq = pl.pallas_call(
        held_kernel,
        out_shape=(
            pltpu.VMEM((8, model), f32),
            pltpu.VMEM((HEAD_DIM, LANES), f32),
            pltpu.VMEM((model, LANES), bf16),
            pltpu.VMEM((2 * HEADS, model), bf16),
            pltpu.VMEM((model, model), bf16),
        ),
        in_specs=[in_hbm] * 4,
        out_specs=[in_vmem] * 5,
        scratch_shapes=[
            pltpu.VMEM((model,), f32),
            pltpu.VMEM((HEAD_DIM,), f32),
            pltpu.VMEM((HEAD_DIM,), f32),
            pltpu.SemaphoreType.DMA((4,)),
        ],
        compiler_params=pltpu.CompilerParams(vmem_limit_bytes=8 * 1024 * 1024),
        cost_estimate=pl.CostEstimate(flops=0, bytes_accessed=4 * model * model, transcendentals=0),
        name="held",
    )(*held[:4])
    result = pl.pallas_call(
        tokens_kernel,
        out_shape=jax.ShapeDtypeStruct(gathered.shape, bf16),
        in_specs=[in_vmem] * 6 + [in_hbm] * 2,
        out_specs=in_vmem,
        scratch_shapes=[
            pltpu.VMEM((model, 2 * model), bf16),
            pltpu.VMEM(w_out.shape, bf16),
            pltpu.VMEM((tokens, model), bf16),
            pltpu.VMEM((model, tokens), f32),
            pltpu.VMEM((tokens, model), f32),
            pltpu.VMEM((model, tokens), bf16),
            pltpu.VMEM((tokens, model), bf16),
            pltpu.VMEM((model, tokens), bf16),
            pltpu.VMEM((model, tokens), f32),
            pltpu.VMEM((tokens, model), bf16),
            pltpu.VMEM((tokens, tokens), f32),
            pltpu.SemaphoreType.DMA((3,)),
        ],
        compiler_params=pltpu.CompilerParams(vmem_limit_bytes=40 * 1024 * 1024),
        name="tokens",
    )(gathered, gains, columns, member, spread, wq, *held[3:])
    return exchange(result).reshape(latent.shape)


def solution(mesh):
    placed = (P(("groups", "frame"), None, None), P(), P(), P(), P(), P())
    return jax.shard_map(
        body,
        mesh=mesh,
        in_specs=placed,
        out_specs=P(("groups", "frame"), None, None),
        check_vma=False,
    )
```

```python
import functools
import math

import jax
import jax.numpy as jnp
from jax import lax
from jax.experimental import pallas as pl
from jax.experimental.pallas import tpu as pltpu
from jax.sharding import PartitionSpec as P

HEADS = 16
HEAD_DIM = 72
LANES = 128
EPS = 1e-06
EXP2_SCALE = HEAD_DIM**-0.5 * math.log2(math.e)


def dot(a, b):
    return jnp.dot(a, b, preferred_element_type=jnp.float32)


def held_kernel(
    ln_ref, qg_ref, kg_ref, wqkv_ref, gains_out, columns_out, member_out, spread_out, wq_out, ln, qg, kg, sems
):
    width = wq_out.shape[1]
    pairs = [(ln_ref, ln), (qg_ref, qg), (kg_ref, kg), (wqkv_ref.at[:, pl.ds(0, width)], wq_out)]
    copies = [pltpu.make_async_copy(src, dst, sems.at[i]) for i, (src, dst) in enumerate(pairs)]
    for copy in copies:
        copy.start()

    def belongs(feature, lane):
        head = jnp.where(lane >= HEADS, lane - HEADS, lane)
        first = head * HEAD_DIM
        held = (feature >= first) & (feature < first + HEAD_DIM) & (lane < 2 * HEADS)
        return held.astype(jnp.float32).astype(jnp.bfloat16)

    for out, axis in ((member_out, 0), (spread_out, 1)):
        feature = lax.broadcasted_iota(jnp.int32, out.shape, axis)
        out[...] = belongs(feature, lax.broadcasted_iota(jnp.int32, out.shape, 1 - axis))
    for copy in copies[:3]:
        copy.wait()
    gains_out[0:1, :] = ln[...].reshape(1, width)
    row = jnp.concatenate([qg[...].reshape(1, HEAD_DIM), jnp.zeros((1, LANES - HEAD_DIM), jnp.float32)], axis=1)
    columns_out[...] = jnp.broadcast_to(row, (LANES, LANES)).T[:HEAD_DIM]
    gains_out[1:2, :] = jnp.concatenate([kg[...].reshape(1, HEAD_DIM)] * HEADS, axis=1)
    copies[3].wait()


def tokens_kernel(
    x_ref,
    gains_ref,
    columns_ref,
    member_ref,
    spread_ref,
    wq,
    wqkv_hbm,
    wout_hbm,
    o_ref,
    wkv,
    wout,
    normed,
    mixed_q,
    mixed_k,
    queries_t,
    keys,
    values_t,
    attended_t,
    attended,
    same,
    sems,
):
    frames, positions, width = x_ref.shape
    tokens = frames * positions
    bf16, f32 = jnp.bfloat16, jnp.float32

    pairs = [
        (wqkv_hbm.at[:, pl.ds(width, width)], wkv.at[:, pl.ds(0, width)]),
        (wqkv_hbm.at[:, pl.ds(2 * width, width)], wkv.at[:, pl.ds(width, width)]),
        (wout_hbm, wout),
    ]
    copies = [pltpu.make_async_copy(src, dst, sems.at[i]) for i, (src, dst) in enumerate(pairs)]
    copies[0].start()

    gain = gains_ref[0:1, :]
    step = max(1, 16 // positions)
    for frame in range(0, frames, step):
        x = x_ref[frame : frame + step].astype(f32).reshape(step * positions, width)
        center = x - jnp.mean(x, axis=-1, keepdims=True)
        spread = jnp.mean(center * center, axis=-1, keepdims=True)
        rows = slice(frame * positions, (frame + step) * positions)
        normed[rows, :] = (center * lax.rsqrt(spread + EPS) * gain).astype(bf16)

    def head_norm(mixed, row, out):
        squares = mixed[...] * mixed[...]
        high = squares.astype(bf16)
        low = (squares - high.astype(f32)).astype(bf16)
        total = dot(jnp.concatenate([high, low], axis=0), member_ref[...])
        total = total[:tokens] + total[tokens:]
        inverse = lax.rsqrt(total * (1.0 / HEAD_DIM) + EPS)
        high = inverse.astype(bf16)
        low = (inverse - high.astype(f32)).astype(bf16)
        lane = lax.broadcasted_iota(jnp.int32, inverse.shape, 1)
        parts = jnp.where(lane < HEADS, high, low)[:, : 2 * HEADS]
        out[...] = (mixed[...] * dot(parts, spread_ref[...]) * gains_ref[row : row + 1, :]).astype(bf16)

    copies[1].start()
    mixed_q[...] = dot(normed[...], wq[...]).T
    for pair in range(HEADS // 2):
        heads = []
        for first in (2 * pair * HEAD_DIM, (2 * pair + 1) * HEAD_DIM):
            head = mixed_q[first : first + HEAD_DIM, :]
            total = jnp.sum(head * head, axis=0, keepdims=True)
            heads.append(head * lax.rsqrt(total * (1.0 / HEAD_DIM) + EPS) * columns_ref[...])
        rows = slice(2 * pair * HEAD_DIM, (2 * pair + 2) * HEAD_DIM)
        queries_t[rows, :] = jnp.concatenate(heads, axis=0).astype(bf16)
    copies[0].wait()
    copies[2].start()
    mixed_k[...] = dot(normed[...], wkv[:, :width])
    head_norm(mixed_k, 1, keys)
    copies[1].wait()
    values_t[...] = dot(normed[...], wkv[:, width:]).astype(bf16).T

    place = lax.broadcasted_iota(jnp.int32, (tokens, tokens), 0) % positions
    other = lax.broadcasted_iota(jnp.int32, (tokens, tokens), 1) % positions
    same[...] = (place == other).astype(f32)

    row = lax.broadcasted_iota(jnp.int32, (2 * LANES, tokens), 0)
    for pair in range(HEADS // 2):
        window = slice(pair * LANES, (pair + 2) * LANES)
        begin = pair * (2 * HEAD_DIM - LANES)
        query = queries_t[window, :]
        both = [
            jnp.where((row >= begin + h * HEAD_DIM) & (row < begin + (h + 1) * HEAD_DIM), query, jnp.zeros((), bf16))
            for h in range(2)
        ]
        scores = dot(keys[:, window], jnp.concatenate(both, axis=1))
        weights = []
        for h in range(2):
            part = jnp.exp2(scores[:, h * tokens : (h + 1) * tokens] * EXP2_SCALE) * same[...]
            weights.append((part * (1.0 / jnp.sum(part, axis=0, keepdims=True))).astype(bf16))
        features = slice(pair * 2 * HEAD_DIM, (pair + 1) * 2 * HEAD_DIM)
        heads_out = dot(values_t[features, :], jnp.concatenate(weights, axis=1))
        for h in range(2):
            first = (2 * pair + h) * HEAD_DIM
            attended_t[first : first + HEAD_DIM, :] = heads_out[
                h * HEAD_DIM : (h + 1) * HEAD_DIM, h * tokens : (h + 1) * tokens
            ]
    attended[...] = attended_t[...].astype(bf16).T

    copies[2].wait()
    branch = dot(attended[...], wout[...])
    o_ref[...] = (x_ref[...].astype(f32) + branch.reshape(x_ref.shape)).astype(bf16)


def body(latent, ln_gain, q_gain, k_gain, w_qkv, w_out):
    device_count = lax.axis_size("frame")
    rows, columns, model = latent.shape
    tokens = rows * columns
    per_peer = tokens // device_count
    line = list(range(device_count // 4))
    order = [4 * i + member for i in line[::2] + line[1::2][::-1] for member in range(4)]
    exchange = functools.partial(
        lax.all_to_all, axis_name="frame", split_axis=0, concat_axis=0, axis_index_groups=[order], tiled=True
    )
    gathered = exchange(latent.reshape(device_count, per_peer, model))
    in_vmem = pl.BlockSpec(memory_space=pltpu.VMEM)
    in_hbm = pl.BlockSpec(memory_space=pltpu.HBM)
    bf16, f32 = jnp.bfloat16, jnp.float32
    held = [pltpu.with_memory_space_constraint(a, pltpu.HBM) for a in (ln_gain, q_gain, k_gain, w_qkv, w_out)]
    gains, columns, member, spread, wq = pl.pallas_call(
        held_kernel,
        out_shape=(
            pltpu.VMEM((8, model), f32),
            pltpu.VMEM((HEAD_DIM, LANES), f32),
            pltpu.VMEM((model, LANES), bf16),
            pltpu.VMEM((2 * HEADS, model), bf16),
            pltpu.VMEM((model, model), bf16),
        ),
        in_specs=[in_hbm] * 4,
        out_specs=[in_vmem] * 5,
        scratch_shapes=[
            pltpu.VMEM((model,), f32),
            pltpu.VMEM((HEAD_DIM,), f32),
            pltpu.VMEM((HEAD_DIM,), f32),
            pltpu.SemaphoreType.DMA((4,)),
        ],
        compiler_params=pltpu.CompilerParams(vmem_limit_bytes=8 * 1024 * 1024),
        cost_estimate=pl.CostEstimate(flops=0, bytes_accessed=4 * model * model, transcendentals=0),
        name="held",
    )(*held[:4])
    result = pl.pallas_call(
        tokens_kernel,
        out_shape=jax.ShapeDtypeStruct(gathered.shape, bf16),
        in_specs=[in_vmem] * 6 + [in_hbm] * 2,
        out_specs=in_vmem,
        scratch_shapes=[
            pltpu.VMEM((model, 2 * model), bf16),
            pltpu.VMEM(w_out.shape, bf16),
            pltpu.VMEM((tokens, model), bf16),
            pltpu.VMEM((model, tokens), f32),
            pltpu.VMEM((tokens, model), f32),
            pltpu.VMEM((model, tokens), bf16),
            pltpu.VMEM((tokens, model), bf16),
            pltpu.VMEM((model, tokens), bf16),
            pltpu.VMEM((model, tokens), f32),
            pltpu.VMEM((tokens, model), bf16),
            pltpu.VMEM((tokens, tokens), f32),
            pltpu.SemaphoreType.DMA((3,)),
        ],
        compiler_params=pltpu.CompilerParams(vmem_limit_bytes=40 * 1024 * 1024),
        name="tokens",
    )(gathered, gains, columns, member, spread, wq, *held[3:])
    return exchange(result).reshape(latent.shape)


def solution(mesh):
    placed = (P(("groups", "frame"), None, None), P(), P(), P(), P(), P())
    return jax.shard_map(
        body,
        mesh=mesh,
        in_specs=placed,
        out_specs=P(("groups", "frame"), None, None),
        check_vma=False,
    )
```

```python
import functools
import math

import jax
import jax.numpy as jnp
from jax import lax
from jax.experimental import pallas as pl
from jax.experimental.pallas import tpu as pltpu
from jax.sharding import PartitionSpec as P

HEADS = 16
HEAD_DIM = 72
LANES = 128
EPS = 1e-06
EXP2_SCALE = HEAD_DIM**-0.5 * math.log2(math.e)


def dot(a, b):
    return jnp.dot(a, b, preferred_element_type=jnp.float32)


def held_kernel(
    ln_ref, qg_ref, kg_ref, wqkv_ref, gains_out, columns_out, member_out, spread_out, wq_out, ln, qg, kg, sems
):
    width = wq_out.shape[1]
    pairs = [(ln_ref, ln), (qg_ref, qg), (kg_ref, kg), (wqkv_ref.at[:, pl.ds(0, width)], wq_out)]
    copies = [pltpu.make_async_copy(src, dst, sems.at[i]) for i, (src, dst) in enumerate(pairs)]
    for copy in copies:
        copy.start()

    def belongs(feature, lane):
        head = jnp.where(lane >= HEADS, lane - HEADS, lane)
        first = head * HEAD_DIM
        held = (feature >= first) & (feature < first + HEAD_DIM) & (lane < 2 * HEADS)
        return held.astype(jnp.float32).astype(jnp.bfloat16)

    for out, axis in ((member_out, 0), (spread_out, 1)):
        feature = lax.broadcasted_iota(jnp.int32, out.shape, axis)
        out[...] = belongs(feature, lax.broadcasted_iota(jnp.int32, out.shape, 1 - axis))
    for copy in copies[:3]:
        copy.wait()
    gains_out[0:1, :] = ln[...].reshape(1, width)
    row = jnp.concatenate([qg[...].reshape(1, HEAD_DIM), jnp.zeros((1, LANES - HEAD_DIM), jnp.float32)], axis=1)
    columns_out[...] = jnp.broadcast_to(row, (LANES, LANES)).T[:HEAD_DIM]
    gains_out[1:2, :] = jnp.concatenate([kg[...].reshape(1, HEAD_DIM)] * HEADS, axis=1)
    copies[3].wait()


def tokens_kernel(
    x_ref,
    gains_ref,
    columns_ref,
    member_ref,
    spread_ref,
    wq,
    wqkv_hbm,
    wout_hbm,
    o_ref,
    wkv,
    wout,
    normed,
    mixed_q,
    mixed_k,
    queries_t,
    keys,
    values_t,
    attended_t,
    attended,
    same,
    sems,
):
    frames, positions, width = x_ref.shape
    tokens = frames * positions
    bf16, f32 = jnp.bfloat16, jnp.float32

    pairs = [
        (wqkv_hbm.at[:, pl.ds(width, width)], wkv.at[:, pl.ds(0, width)]),
        (wqkv_hbm.at[:, pl.ds(2 * width, width)], wkv.at[:, pl.ds(width, width)]),
        (wout_hbm, wout),
    ]
    copies = [pltpu.make_async_copy(src, dst, sems.at[i]) for i, (src, dst) in enumerate(pairs)]
    copies[0].start()

    gain = gains_ref[0:1, :]
    step = max(1, 16 // positions)
    for frame in range(0, frames, step):
        x = x_ref[frame : frame + step].astype(f32).reshape(step * positions, width)
        center = x - jnp.mean(x, axis=-1, keepdims=True)
        spread = jnp.mean(center * center, axis=-1, keepdims=True)
        rows = slice(frame * positions, (frame + step) * positions)
        normed[rows, :] = (center * lax.rsqrt(spread + EPS) * gain).astype(bf16)

    def head_norm(mixed, row, out):
        squares = mixed[...] * mixed[...]
        high = squares.astype(bf16)
        low = (squares - high.astype(f32)).astype(bf16)
        total = dot(jnp.concatenate([high, low], axis=0), member_ref[...])
        total = total[:tokens] + total[tokens:]
        inverse = lax.rsqrt(total * (1.0 / HEAD_DIM) + EPS)
        high = inverse.astype(bf16)
        low = (inverse - high.astype(f32)).astype(bf16)
        lane = lax.broadcasted_iota(jnp.int32, inverse.shape, 1)
        parts = jnp.where(lane < HEADS, high, low)[:, : 2 * HEADS]
        out[...] = (mixed[...] * dot(parts, spread_ref[...]) * gains_ref[row : row + 1, :]).astype(bf16)

    copies[1].start()
    mixed_q[...] = dot(normed[...], wq[...]).T
    for pair in range(HEADS // 2):
        heads = []
        for first in (2 * pair * HEAD_DIM, (2 * pair + 1) * HEAD_DIM):
            head = mixed_q[first : first + HEAD_DIM, :]
            total = jnp.sum(head * head, axis=0, keepdims=True)
            heads.append(head * lax.rsqrt(total * (1.0 / HEAD_DIM) + EPS) * columns_ref[...])
        rows = slice(2 * pair * HEAD_DIM, (2 * pair + 2) * HEAD_DIM)
        queries_t[rows, :] = jnp.concatenate(heads, axis=0).astype(bf16)
    copies[0].wait()
    copies[2].start()
    mixed_k[...] = dot(normed[...], wkv[:, :width])
    head_norm(mixed_k, 1, keys)
    copies[1].wait()
    values_t[...] = dot(normed[...], wkv[:, width:]).astype(bf16).T

    place = lax.broadcasted_iota(jnp.int32, (tokens, tokens), 0) % positions
    other = lax.broadcasted_iota(jnp.int32, (tokens, tokens), 1) % positions
    same[...] = (place == other).astype(f32)

    row = lax.broadcasted_iota(jnp.int32, (2 * LANES, tokens), 0)
    for pair in range(HEADS // 2):
        window = slice(pair * LANES, (pair + 2) * LANES)
        begin = pair * (2 * HEAD_DIM - LANES)
        query = queries_t[window, :]
        both = [
            jnp.where((row >= begin + h * HEAD_DIM) & (row < begin + (h + 1) * HEAD_DIM), query, jnp.zeros((), bf16))
            for h in range(2)
        ]
        scores = dot(keys[:, window], jnp.concatenate(both, axis=1))
        weights = []
        for h in range(2):
            part = jnp.exp2(scores[:, h * tokens : (h + 1) * tokens] * EXP2_SCALE) * same[...]
            weights.append((part * (1.0 / jnp.sum(part, axis=0, keepdims=True))).astype(bf16))
        features = slice(pair * 2 * HEAD_DIM, (pair + 1) * 2 * HEAD_DIM)
        heads_out = dot(values_t[features, :], jnp.concatenate(weights, axis=1))
        for h in range(2):
            first = (2 * pair + h) * HEAD_DIM
            attended_t[first : first + HEAD_DIM, :] = heads_out[
                h * HEAD_DIM : (h + 1) * HEAD_DIM, h * tokens : (h + 1) * tokens
            ]
    attended[...] = attended_t[...].astype(bf16).T

    copies[2].wait()
    branch = dot(attended[...], wout[...])
    o_ref[...] = (x_ref[...].astype(f32) + branch.reshape(x_ref.shape)).astype(bf16)


def body(latent, ln_gain, q_gain, k_gain, w_qkv, w_out):
    device_count = lax.axis_size("frame")
    rows, columns, model = latent.shape
    tokens = rows * columns
    per_peer = tokens // device_count
    line = list(range(device_count // 4))
    chips = [2 * i + row for row, walk in enumerate((line, line[::-1])) for i in walk]
    order = [2 * chips[3 * place % len(chips)] + core for place in range(len(chips)) for core in range(2)]
    exchange = functools.partial(
        lax.all_to_all, axis_name="frame", split_axis=0, concat_axis=0, axis_index_groups=[order], tiled=True
    )
    gathered = exchange(latent.reshape(device_count, per_peer, model))
    in_vmem = pl.BlockSpec(memory_space=pltpu.VMEM)
    in_hbm = pl.BlockSpec(memory_space=pltpu.HBM)
    bf16, f32 = jnp.bfloat16, jnp.float32
    held = [pltpu.with_memory_space_constraint(a, pltpu.HBM) for a in (ln_gain, q_gain, k_gain, w_qkv, w_out)]
    gains, columns, member, spread, wq = pl.pallas_call(
        held_kernel,
        out_shape=(
            pltpu.VMEM((8, model), f32),
            pltpu.VMEM((HEAD_DIM, LANES), f32),
            pltpu.VMEM((model, LANES), bf16),
            pltpu.VMEM((2 * HEADS, model), bf16),
            pltpu.VMEM((model, model), bf16),
        ),
        in_specs=[in_hbm] * 4,
        out_specs=[in_vmem] * 5,
        scratch_shapes=[
            pltpu.VMEM((model,), f32),
            pltpu.VMEM((HEAD_DIM,), f32),
            pltpu.VMEM((HEAD_DIM,), f32),
            pltpu.SemaphoreType.DMA((4,)),
        ],
        compiler_params=pltpu.CompilerParams(vmem_limit_bytes=8 * 1024 * 1024),
        cost_estimate=pl.CostEstimate(flops=0, bytes_accessed=4 * model * model, transcendentals=0),
        name="held",
    )(*held[:4])
    result = pl.pallas_call(
        tokens_kernel,
        out_shape=jax.ShapeDtypeStruct(gathered.shape, bf16),
        in_specs=[in_vmem] * 6 + [in_hbm] * 2,
        out_specs=in_vmem,
        scratch_shapes=[
            pltpu.VMEM((model, 2 * model), bf16),
            pltpu.VMEM(w_out.shape, bf16),
            pltpu.VMEM((tokens, model), bf16),
            pltpu.VMEM((model, tokens), f32),
            pltpu.VMEM((tokens, model), f32),
            pltpu.VMEM((model, tokens), bf16),
            pltpu.VMEM((tokens, model), bf16),
            pltpu.VMEM((model, tokens), bf16),
            pltpu.VMEM((model, tokens), f32),
            pltpu.VMEM((tokens, model), bf16),
            pltpu.VMEM((tokens, tokens), f32),
            pltpu.SemaphoreType.DMA((3,)),
        ],
        compiler_params=pltpu.CompilerParams(vmem_limit_bytes=40 * 1024 * 1024),
        name="tokens",
    )(gathered, gains, columns, member, spread, wq, *held[3:])
    return exchange(result).reshape(latent.shape)


def solution(mesh):
    placed = (P(("groups", "frame"), None, None), P(), P(), P(), P(), P())
    return jax.shard_map(
        body,
        mesh=mesh,
        in_specs=placed,
        out_specs=P(("groups", "frame"), None, None),
        check_vma=False,
    )
```

```python
import functools
import math

import jax
import jax.numpy as jnp
from jax import lax
from jax.experimental import pallas as pl
from jax.experimental.pallas import tpu as pltpu
from jax.sharding import PartitionSpec as P

HEADS = 16
HEAD_DIM = 72
LANES = 128
EPS = 1e-06
EXP2_SCALE = HEAD_DIM**-0.5 * math.log2(math.e)


def dot(a, b):
    return jnp.dot(a, b, preferred_element_type=jnp.float32)


def held_kernel(
    ln_ref, qg_ref, kg_ref, wqkv_ref, gains_out, columns_out, member_out, spread_out, wq_out, ln, qg, kg, sems
):
    width = wq_out.shape[1]
    pairs = [(ln_ref, ln), (qg_ref, qg), (kg_ref, kg), (wqkv_ref.at[:, pl.ds(0, width)], wq_out)]
    copies = [pltpu.make_async_copy(src, dst, sems.at[i]) for i, (src, dst) in enumerate(pairs)]
    for copy in copies:
        copy.start()

    def belongs(feature, lane):
        head = jnp.where(lane >= HEADS, lane - HEADS, lane)
        first = head * HEAD_DIM
        held = (feature >= first) & (feature < first + HEAD_DIM) & (lane < 2 * HEADS)
        return held.astype(jnp.float32).astype(jnp.bfloat16)

    for out, axis in ((member_out, 0), (spread_out, 1)):
        feature = lax.broadcasted_iota(jnp.int32, out.shape, axis)
        out[...] = belongs(feature, lax.broadcasted_iota(jnp.int32, out.shape, 1 - axis))
    for copy in copies[:3]:
        copy.wait()
    gains_out[0:1, :] = ln[...].reshape(1, width)
    row = jnp.concatenate([qg[...].reshape(1, HEAD_DIM), jnp.zeros((1, LANES - HEAD_DIM), jnp.float32)], axis=1)
    columns_out[...] = jnp.broadcast_to(row, (LANES, LANES)).T[:HEAD_DIM]
    gains_out[1:2, :] = jnp.concatenate([kg[...].reshape(1, HEAD_DIM)] * HEADS, axis=1)
    copies[3].wait()


def tokens_kernel(
    x_ref,
    gains_ref,
    columns_ref,
    member_ref,
    spread_ref,
    wq,
    wqkv_hbm,
    wout_hbm,
    o_ref,
    wkv,
    wout,
    normed,
    mixed_q,
    mixed_k,
    queries_t,
    keys,
    values_t,
    attended_t,
    attended,
    same,
    sems,
):
    frames, positions, width = x_ref.shape
    tokens = frames * positions
    bf16, f32 = jnp.bfloat16, jnp.float32

    pairs = [
        (wqkv_hbm.at[:, pl.ds(width, width)], wkv.at[:, pl.ds(0, width)]),
        (wqkv_hbm.at[:, pl.ds(2 * width, width)], wkv.at[:, pl.ds(width, width)]),
        (wout_hbm, wout),
    ]
    copies = [pltpu.make_async_copy(src, dst, sems.at[i]) for i, (src, dst) in enumerate(pairs)]
    copies[0].start()

    gain = gains_ref[0:1, :]
    step = max(1, 16 // positions)
    for frame in range(0, frames, step):
        x = x_ref[frame : frame + step].astype(f32).reshape(step * positions, width)
        center = x - jnp.mean(x, axis=-1, keepdims=True)
        spread = jnp.mean(center * center, axis=-1, keepdims=True)
        rows = slice(frame * positions, (frame + step) * positions)
        normed[rows, :] = (center * lax.rsqrt(spread + EPS) * gain).astype(bf16)

    def head_norm(mixed, row, out):
        squares = mixed[...] * mixed[...]
        high = squares.astype(bf16)
        low = (squares - high.astype(f32)).astype(bf16)
        total = dot(jnp.concatenate([high, low], axis=0), member_ref[...])
        total = total[:tokens] + total[tokens:]
        inverse = lax.rsqrt(total * (1.0 / HEAD_DIM) + EPS)
        high = inverse.astype(bf16)
        low = (inverse - high.astype(f32)).astype(bf16)
        lane = lax.broadcasted_iota(jnp.int32, inverse.shape, 1)
        parts = jnp.where(lane < HEADS, high, low)[:, : 2 * HEADS]
        out[...] = (mixed[...] * dot(parts, spread_ref[...]) * gains_ref[row : row + 1, :]).astype(bf16)

    copies[1].start()
    mixed_q[...] = dot(normed[...], wq[...]).T
    for pair in range(HEADS // 2):
        heads = []
        for first in (2 * pair * HEAD_DIM, (2 * pair + 1) * HEAD_DIM):
            head = mixed_q[first : first + HEAD_DIM, :]
            total = jnp.sum(head * head, axis=0, keepdims=True)
            heads.append(head * lax.rsqrt(total * (1.0 / HEAD_DIM) + EPS) * columns_ref[...])
        rows = slice(2 * pair * HEAD_DIM, (2 * pair + 2) * HEAD_DIM)
        queries_t[rows, :] = jnp.concatenate(heads, axis=0).astype(bf16)
    copies[0].wait()
    copies[2].start()
    mixed_k[...] = dot(normed[...], wkv[:, :width])
    head_norm(mixed_k, 1, keys)
    copies[1].wait()
    values_t[...] = dot(normed[...], wkv[:, width:]).astype(bf16).T

    place = lax.broadcasted_iota(jnp.int32, (tokens, tokens), 0) % positions
    other = lax.broadcasted_iota(jnp.int32, (tokens, tokens), 1) % positions
    same[...] = (place == other).astype(f32)

    row = lax.broadcasted_iota(jnp.int32, (2 * LANES, tokens), 0)
    for pair in range(HEADS // 2):
        window = slice(pair * LANES, (pair + 2) * LANES)
        begin = pair * (2 * HEAD_DIM - LANES)
        query = queries_t[window, :]
        both = [
            jnp.where((row >= begin + h * HEAD_DIM) & (row < begin + (h + 1) * HEAD_DIM), query, jnp.zeros((), bf16))
            for h in range(2)
        ]
        scores = dot(keys[:, window], jnp.concatenate(both, axis=1))
        weights = []
        for h in range(2):
            part = jnp.exp2(scores[:, h * tokens : (h + 1) * tokens] * EXP2_SCALE) * same[...]
            weights.append((part * (1.0 / jnp.sum(part, axis=0, keepdims=True))).astype(bf16))
        features = slice(pair * 2 * HEAD_DIM, (pair + 1) * 2 * HEAD_DIM)
        heads_out = dot(values_t[features, :], jnp.concatenate(weights, axis=1))
        for h in range(2):
            first = (2 * pair + h) * HEAD_DIM
            attended_t[first : first + HEAD_DIM, :] = heads_out[
                h * HEAD_DIM : (h + 1) * HEAD_DIM, h * tokens : (h + 1) * tokens
            ]
    attended[...] = attended_t[...].astype(bf16).T

    copies[2].wait()
    branch = dot(attended[...], wout[...])
    o_ref[...] = (x_ref[...].astype(f32) + branch.reshape(x_ref.shape)).astype(bf16)


def body(latent, ln_gain, q_gain, k_gain, w_qkv, w_out):
    device_count = lax.axis_size("frame")
    rows, columns, model = latent.shape
    tokens = rows * columns
    per_peer = tokens // device_count
    line = list(range(device_count // 4))
    order = [4 * i + 2 * row + core for row, walk in enumerate((line[::-1], line)) for i in walk for core in range(2)]
    exchange = functools.partial(
        lax.all_to_all, axis_name="frame", split_axis=0, concat_axis=0, axis_index_groups=[order], tiled=True
    )
    gathered = exchange(latent.reshape(device_count, per_peer, model))
    in_vmem = pl.BlockSpec(memory_space=pltpu.VMEM)
    in_hbm = pl.BlockSpec(memory_space=pltpu.HBM)
    bf16, f32 = jnp.bfloat16, jnp.float32
    held = [pltpu.with_memory_space_constraint(a, pltpu.HBM) for a in (ln_gain, q_gain, k_gain, w_qkv, w_out)]
    gains, columns, member, spread, wq = pl.pallas_call(
        held_kernel,
        out_shape=(
            pltpu.VMEM((8, model), f32),
            pltpu.VMEM((HEAD_DIM, LANES), f32),
            pltpu.VMEM((model, LANES), bf16),
            pltpu.VMEM((2 * HEADS, model), bf16),
            pltpu.VMEM((model, model), bf16),
        ),
        in_specs=[in_hbm] * 4,
        out_specs=[in_vmem] * 5,
        scratch_shapes=[
            pltpu.VMEM((model,), f32),
            pltpu.VMEM((HEAD_DIM,), f32),
            pltpu.VMEM((HEAD_DIM,), f32),
            pltpu.SemaphoreType.DMA((4,)),
        ],
        compiler_params=pltpu.CompilerParams(vmem_limit_bytes=8 * 1024 * 1024),
        cost_estimate=pl.CostEstimate(flops=0, bytes_accessed=4 * model * model, transcendentals=0),
        name="held",
    )(*held[:4])
    result = pl.pallas_call(
        tokens_kernel,
        out_shape=jax.ShapeDtypeStruct(gathered.shape, bf16),
        in_specs=[in_vmem] * 6 + [in_hbm] * 2,
        out_specs=in_vmem,
        scratch_shapes=[
            pltpu.VMEM((model, 2 * model), bf16),
            pltpu.VMEM(w_out.shape, bf16),
            pltpu.VMEM((tokens, model), bf16),
            pltpu.VMEM((model, tokens), f32),
            pltpu.VMEM((tokens, model), f32),
            pltpu.VMEM((model, tokens), bf16),
            pltpu.VMEM((tokens, model), bf16),
            pltpu.VMEM((model, tokens), bf16),
            pltpu.VMEM((model, tokens), f32),
            pltpu.VMEM((tokens, model), bf16),
            pltpu.VMEM((tokens, tokens), f32),
            pltpu.SemaphoreType.DMA((3,)),
        ],
        compiler_params=pltpu.CompilerParams(vmem_limit_bytes=40 * 1024 * 1024),
        name="tokens",
    )(gathered, gains, columns, member, spread, wq, *held[3:])
    return exchange(result).reshape(latent.shape)


def solution(mesh):
    placed = (P(("groups", "frame"), None, None), P(), P(), P(), P(), P())
    return jax.shard_map(
        body,
        mesh=mesh,
        in_specs=placed,
        out_specs=P(("groups", "frame"), None, None),
        check_vma=False,
    )
```
